512 devices in a mesh: tile: 128 (over y_lo, x, z, core), chan: 4 (over y_hi).
Axes of the slice: x: 4, y: 8 (y_hi: 4, y_lo: 2; y = y_hi * 2 + y_lo), z: 8, core: 2. Of those that a mesh axis runs over, the one named last changes fastest.
Arguments:
- fields: bfloat16 [384, 256, 144], P('tile', 'chan'), may hold values from -6 to 6
- seam_table: int32 [384, 4, 3], replicated, may hold values from 0 to 383, as said below
- w_first: bfloat16 [9, 256, 256], P(None, 'chan'), may hold values from -0.125 to 0.125
- w_down: bfloat16 [9, 256, 256], P(None, 'chan'), may hold values from -0.125 to 0.125
- cotangent: bfloat16 [384, 256, 36], P('tile', 'chan'), may hold values from -6 to 6
Outputs:
- coarse: bfloat16 [384, 256, 36], P('tile', 'chan')
- grad_first: float32 [9, 256, 256], P(None, 'chan')
- grad_down: float32 [9, 256, 256], P(None, 'chan')
- grad_pre: bfloat16 [384, 256, 144], P('tile', 'chan')
The draws below stay inside these ranges and needn't reach their ends.
Inputs may be any that keep to these rules, and one draw needn't show every extreme that they name: seam_table[t, e] = (n, f, r): the tiles tile the six faces of a cube, each face an equal square grid of tiles, and tile t is held by the device at position t // 3 along tile; tile n lies across edge e of tile t, f is its edge on the shared seam, r is 1 where the two edges run in opposite directions and 0 else; the matching is symmetric, seam_table[n, f] = (t, e, r). Columns 1 and 2 hold 0 to 3 and 0 to 1.
All inputs are finite; a program needn't handle non-finite values.
Results may differ from the reference program's by a relative error of at most 0.023.
Values may be sent and summed in bfloat16 or wider, within the bound.
No kernel may reach another device: no remote copies, remote signals or barrier semaphores. Data moves between devices by JAX's collectives and lax.ppermute only.
A program may use at most 64 MiB of HBM per device.

```python
import math
import jax
import jax.numpy as jnp
import numpy as np
from jax import lax

C = 256
S = 12
TILES = 384
HALF = 6
CELLS = 144
COARSE = 36
N_CHAN = 4


def cube_matching(tile_count):
    tile_side = math.isqrt(tile_count // 6)
    normals = [(1, 0, 0), (-1, 0, 0), (0, 1, 0), (0, -1, 0), (0, 0, 1), (0, 0, -1)]
    across = [(0, 1, 0), (0, 0, 1), (0, 0, 1), (1, 0, 0), (1, 0, 0), (0, 1, 0)]
    upward = [(0, 0, 1), (0, 1, 0), (1, 0, 0), (0, 0, 1), (0, 1, 0), (1, 0, 0)]

    def corner(face_at, column_at, row_at):
        return tuple((tile_side * normals[face_at][coord] + (2 * column_at - tile_side) * across[face_at][coord] + (2 * row_at - tile_side) * upward[face_at][coord] for coord in range(3)))
    owners = {}
    endings = {}
    for face_at in range(6):
        for row_at in range(tile_side):
            for column_at in range(tile_side):
                tile_id = face_at * tile_side * tile_side + row_at * tile_side + column_at
                pairs = [(corner(face_at, column_at, row_at), corner(face_at, column_at + 1, row_at)), (corner(face_at, column_at, row_at + 1), corner(face_at, column_at + 1, row_at + 1)), (corner(face_at, column_at, row_at), corner(face_at, column_at, row_at + 1)), (corner(face_at, column_at + 1, row_at), corner(face_at, column_at + 1, row_at + 1))]
                for edge_at in range(4):
                    endings[tile_id, edge_at] = pairs[edge_at]
                    edge_key = frozenset(pairs[edge_at])
                    if edge_key not in owners:
                        owners[edge_key] = []
                    owners[edge_key] = owners[edge_key] + [(tile_id, edge_at)]
    neighbour = np.zeros((tile_count, 4), np.int32)
    facing = np.zeros((tile_count, 4), np.int32)
    flipped = np.zeros((tile_count, 4), np.int32)
    for tile_id, edge_at in endings:
        first_end, second_end = endings[tile_id, edge_at]
        partner = [entry for entry in owners[frozenset((first_end, second_end))] if entry != (tile_id, edge_at)][0]
        neighbour[tile_id, edge_at] = partner[0]
        facing[tile_id, edge_at] = partner[1]
        flipped[tile_id, edge_at] = 1 if endings[partner][0] == second_end else 0
    return (neighbour, facing, flipped)


def draw_seam_table(key, part):
    key = jax.random.fold_in(key, 7)
    neighbour, facing, flipped = cube_matching(TILES)
    relabel = jax.random.permutation(key, TILES).astype(jnp.int32)
    rows_new = jnp.stack([relabel[jnp.asarray(neighbour)], jnp.asarray(facing), jnp.asarray(flipped)], axis=-1)
    return jnp.zeros((TILES, 4, 3), jnp.int32).at[relabel].set(rows_new)


def block_scale(own_key, extent, split, low, top_value):
    gain, own = 1.0, jax.random.fold_in(own_key, 6)
    for dim, shards_of in split:
        steps = jnp.exp(jax.random.uniform(jax.random.fold_in(own, dim), (shards_of,), jnp.float32, low / len(split), top_value / len(split)))
        gain = gain * jnp.repeat(steps, extent[dim] // shards_of).reshape([-1 if axis == dim else 1 for axis in range(len(extent))])
    return gain


def normal_values(own_key, extent, scale, reach, pieces=(), held_as=jnp.bfloat16):
    result = jax.random.normal(own_key, extent, jnp.float32) * scale
    if len(pieces) > 0:
        result = block_scale(own_key, extent, pieces, -0.22, 0.18) * result
    return jnp.clip(result, min=-reach, max=reach).astype(held_as)


def setup_inputs(seed: int = 0) -> dict:
    splits = jax.random.split(jax.random.key(seed), 6)
    fields = normal_values(splits[0], (TILES, C, CELLS), 1.0, 6.0, ((0, 128), (1, 4)))
    seam_table = draw_seam_table(jax.random.fold_in(splits[5], 71), 0)
    w_first = normal_values(splits[2], (9, C, C), (9 * C) ** -0.5, 0.125, ((1, 4),))
    w_down = normal_values(splits[3], (9, C, C), (9 * C) ** -0.5, 0.125, ((1, 4),))
    cotangent = normal_values(splits[4], (TILES, C, COARSE), 1.0, 6.0, ((0, 128), (1, 4)))
    return dict(fields=fields, seam_table=seam_table, w_first=w_first, w_down=w_down, cotangent=cotangent)


def edge_strips(values):
    return jnp.stack([values[:, :, 0, :], values[:, :, -1, :], values[:, :, :, 0], values[:, :, :, -1]], axis=1)

def flip_where(picked, flipped):
    return jnp.where(flipped[:, :, None, None] == 1, picked[..., ::-1], picked)

def frame_tile(values, picked):
    left_col = picked[:, 2][..., None]
    right_col = picked[:, 3][..., None]
    middle = jnp.concatenate([left_col, values, right_col], axis=3)
    zero_cell = jnp.zeros(values.shape[:2] + (1,), values.dtype)
    top_line = jnp.concatenate([zero_cell, picked[:, 0], zero_cell], axis=2)[:, :, None, :]
    low_line = jnp.concatenate([zero_cell, picked[:, 1], zero_cell], axis=2)[:, :, None, :]
    return jnp.concatenate([top_line, middle, low_line], axis=2)

def seam_pad(values, seam_table):
    picked = edge_strips(values)[seam_table[:, :, 0], seam_table[:, :, 1]]
    return frame_tile(values, flip_where(picked, seam_table[:, :, 2]))

def conv_part(padded, weight, stride):
    kernel = weight.astype(jnp.float32).reshape(3, 3, weight.shape[1], weight.shape[2])
    return lax.conv_general_dilated(padded.astype(jnp.float32), kernel, (stride, stride), 'VALID', dimension_numbers=('NCHW', 'HWIO', 'NCHW'), precision=lax.Precision.HIGHEST)

def split_conv(padded, weight, stride):
    block = C // N_CHAN
    summed = None
    for index in range(N_CHAN):
        partial_value = conv_part(padded[:, index * block:(index + 1) * block], weight[:, index * block:(index + 1) * block], stride)
        rounded = lax.optimization_barrier(partial_value.astype(jnp.bfloat16)).astype(jnp.float32)
        summed = rounded if summed is None else summed + rounded
    return summed

def reference(fields, seam_table, w_first, w_down, cotangent):
    inputs = fields.reshape(TILES, C, S, S)
    padded_in = seam_pad(inputs, seam_table)
    preact = split_conv(padded_in, w_first, 1)
    hidden = jax.nn.gelu(preact, approximate=True).astype(jnp.bfloat16)
    padded_hid = seam_pad(hidden, seam_table)
    coarse = split_conv(padded_hid, w_down, 2).astype(jnp.bfloat16).reshape(TILES, C, COARSE)
    upstream = cotangent.reshape(TILES, C, HALF, HALF).astype(jnp.float32)
    down_terms = []
    spread = jnp.zeros((TILES, C, S + 2, S + 2), jnp.float32)
    for tap in range(9):
        row_at, col_at = (tap // 3, tap % 3)
        window = padded_hid[:, :, row_at:row_at + S:2, col_at:col_at + S:2].astype(jnp.float32)
        down_terms.append(jnp.einsum('tihw,tohw->io', window, upstream, precision=lax.Precision.HIGHEST))
        spread = spread.at[:, :, row_at:row_at + S:2, col_at:col_at + S:2].add(jnp.einsum('io,tohw->tihw', w_down[tap].astype(jnp.float32), upstream, precision=lax.Precision.HIGHEST))
    grad_down = jnp.stack(down_terms, 0) * float(TILES * COARSE) ** (-0.5)
    rims = jnp.stack([spread[:, :, 0, 1:-1], spread[:, :, -1, 1:-1], spread[:, :, 1:-1, 0], spread[:, :, 1:-1, -1]], axis=1)
    rims = lax.optimization_barrier(rims.astype(jnp.bfloat16)).astype(jnp.float32)
    picked = flip_where(rims[seam_table[:, :, 0], seam_table[:, :, 1]], seam_table[:, :, 2])
    grad_hidden = spread[:, :, 1:-1, 1:-1]
    grad_hidden = grad_hidden.at[:, :, 0, :].add(picked[:, 0])
    grad_hidden = grad_hidden.at[:, :, -1, :].add(picked[:, 1])
    grad_hidden = grad_hidden.at[:, :, :, 0].add(picked[:, 2])
    grad_hidden = grad_hidden.at[:, :, :, -1].add(picked[:, 3])
    unused, gelu_back = jax.vjp(lambda value: jax.nn.gelu(value, approximate=True), preact)
    grad_pre_low = gelu_back(grad_hidden)[0].astype(jnp.bfloat16)
    grad_pre = lax.optimization_barrier(grad_pre_low).astype(jnp.float32)
    first_terms = []
    for tap in range(9):
        row_at, col_at = (tap // 3, tap % 3)
        window = padded_in[:, :, row_at:row_at + S, col_at:col_at + S].astype(jnp.float32)
        first_terms.append(jnp.einsum('tihw,tohw->io', window, grad_pre, precision=lax.Precision.HIGHEST))
    grad_first = jnp.stack(first_terms, 0) * float(TILES * CELLS) ** (-0.5)
    return (coarse, grad_first, grad_down, grad_pre_low.reshape(TILES, C, CELLS))
```

```python
import numpy as np
import jax
import jax.numpy as jnp
from jax import lax
from jax.experimental import pallas as pl
from jax.experimental.pallas import tpu as pltpu
from jax.sharding import Mesh, PartitionSpec as P

S = 12
HALF = 6
CELLS = 144
COARSE = 36
TILES_HERE = 3
CH = 64
C = 256
YLO, NX, NZ, CORE, CHAN = 2, 4, 8, 2, 4
PLANE = NX * NZ
QUAD = YLO * CORE
TILE_AXES = ("ylo", "x", "z", "core")
BF = jnp.bfloat16
F32 = jnp.float32

EDGE_ROWS = (0, 28, 14, 34)
FIELD_ROWS = 40
BLOCK_ROWS = 52
SEND_ROWS = 160
OWN_ROWS = 72
X_HALF = OWN_ROWS + FIELD_ROWS
C_OWN = 18
C_HALF = 32
PAY_ROWS = X_HALF + C_HALF
PACK_ROWS = 96
UNIT = 16
PRE_ROWS = 176
DOWN_ROWS = 48
SPREAD_ROWS = 192


def strip_cells(edge, depth):
    if edge == 0:
        return [depth * S + i for i in range(S)]
    if edge == 1:
        return [(S - 1 - depth) * S + i for i in range(S)]
    if edge == 2:
        return [i * S + depth for i in range(S)]
    return [i * S + S - 1 - depth for i in range(S)]


def pack_selectors():
    rows = PACK_ROWS + 4 * UNIT
    fields = np.zeros((2, rows, CELLS), np.float32)
    coarse = np.zeros((2, rows, COARSE), np.float32)
    for half in range(2):
        for row in range(OWN_ROWS):
            fields[half, row, 2 * row + half] = 1
        for row in range(C_OWN):
            coarse[half, OWN_ROWS + row, 2 * row + half] = 1
        for edge in range(4):
            base = PACK_ROWS + edge * UNIT
            near, far = strip_cells(edge, 0), strip_cells(edge, 1)
            for row in range(6):
                fields[half, base + row, near[2 * row + half]] = 1
                fields[half, base + 9 + row, far[2 * row + half]] = 1
            for row in range(3):
                at = 2 * row + half
                if edge == 0:
                    coarse[half, base + 6 + row, at] = 1
                if edge == 2:
                    coarse[half, base + 6 + row, at * HALF] = 1
            fields[half, base + 15, near[11 - half]] = 1
    return fields, coarse


def own_at(cell):
    return cell // 2 + X_HALF * (cell % 2)


def near_at(edge, along, depth):
    row = OWN_ROWS + EDGE_ROWS[edge] + 6 * depth
    if along < 0:
        return OWN_ROWS + EDGE_ROWS[edge] + 12 + X_HALF * depth
    if along >= S:
        return OWN_ROWS + EDGE_ROWS[edge] + 13 + X_HALF * depth
    return row + along // 2 + X_HALF * (along % 2)


def window_index():
    fixed = np.zeros((9, PRE_ROWS), np.float32)
    varied = np.zeros((4, 4, 2, 9, PRE_ROWS), np.float32)
    for k in range(9):
        a, b = k // 3, k % 3
        for cell in range(CELLS):
            row, col = cell // S + a, cell % S + b
            inner_row, inner_col = 1 <= row <= S, 1 <= col <= S
            if inner_row and inner_col:
                fixed[k, cell] = 1 + own_at((row - 1) * S + col - 1)
            elif inner_row or inner_col:
                edge = (2 if col == 0 else 3) if inner_row else (0 if row == 0 else 1)
                at = row - 1 if inner_row else col - 1
                for flip in range(2):
                    varied[edge, :, flip, k, cell] = 1 + near_at(edge, 11 - at if flip else at, 0)
        for slot, edge in enumerate((0, 2)):
            own = strip_cells(edge, 0)
            for facing in range(4):
                depth = (a - 1, 1 - a, b - 1, 1 - b)[facing]
                shift = (b - 1, b - 1, a - 1, a - 1)[facing]
                for flip in range(2):
                    for j in range(S):
                        along = (11 - j if flip else j) + shift
                        if depth >= 0:
                            at = near_at(edge, along, depth)
                        elif 0 <= along < S:
                            at = own_at(own[11 - along if flip else along])
                        else:
                            continue
                        varied[edge, facing, flip, k, CELLS + 16 * slot + j] = 1 + at
    return fixed.reshape(-1), varied.reshape(32, -1)


def spread_index():
    fixed = np.zeros((9, SPREAD_ROWS), np.float32)
    varied = np.zeros((4, 4, 2, 9, SPREAD_ROWS), np.float32)
    for k in range(9):
        a, b = k // 3, k % 3
        for cell in range(CELLS):
            row, col = cell // S + 1 - a, cell % S + 1 - b
            if row % 2 == 0 and col % 2 == 0 and 0 <= row < S and 0 <= col < S:
                at = (row // 2) * HALF + col // 2
                fixed[k, cell] = 1 + at // 2 + C_HALF * (at % 2)
        for edge in range(4):
            for flip in range(2):
                for j in range(S):
                    for facing, live, tap in ((0, a == 0, b), (2, b == 0, a)):
                        at = (11 - j if flip else j) + 1 - tap
                        if live and at % 2 == 0 and 0 <= at < S:
                            at //= 2
                            varied[edge, facing, flip, k, CELLS + edge * S + j] = (
                                1 + C_OWN + 3 * edge + at // 2 + C_HALF * (at % 2)
                            )
    return fixed.reshape(-1), varied.reshape(32, -1)


def down_selector():
    chosen = np.zeros((9, DOWN_ROWS, PRE_ROWS), np.float32)
    for k in range(9):
        for cell in range(COARSE):
            row, col = 2 * (cell // HALF) + k // 3, 2 * (cell % HALF) + k % 3
            if row == 0 and col == 0:
                continue
            if row == 0:
                at = CELLS + col - 1
            elif col == 0:
                at = CELLS + 16 + row - 1
            else:
                at = (row - 1) * S + col - 1
            chosen[k, cell, at] = 1
    return chosen.reshape(9 * DOWN_ROWS, PRE_ROWS)


def rim_selector():
    chosen = np.zeros((CELLS, 4 * S), np.float32)
    for edge in range(4):
        for j, cell in enumerate(strip_cells(edge, 0)):
            chosen[cell, edge * S + j] = 1
    return chosen


def order_selector():
    chosen = np.zeros((DOWN_ROWS, 2 * C_HALF), np.float32)
    for cell in range(COARSE):
        chosen[cell, cell // 2 + C_HALF * (cell % 2)] = 1
    return chosen


def dot_nn(left, right):
    return lax.dot_general(left, right, (((1,), (0,)), ((), ())), preferred_element_type=F32)


def dot_nt(left, right):
    return lax.dot_general(left, right, (((1,), (1,)), ((), ())), preferred_element_type=F32)


def pack_kernel(fields_ref, cot_ref, self_ref, selc_ref, own_ref, unit_ref):
    for t in range(TILES_HERE):
        halves = [
            (dot_nt(self_ref[h], fields_ref[t]) + dot_nt(selc_ref[h], cot_ref[t])).astype(BF)
            for h in range(2)
        ]
        for h in range(2):
            own_ref[t, :, h * CH : (h + 1) * CH] = halves[h][:PACK_ROWS]
            unit_ref[t * 4 * UNIT : (t + 1) * 4 * UNIT, h * CH : (h + 1) * CH] = halves[h][PACK_ROWS:]


def edge_row(edge):
    return jnp.where(edge < 2, edge * 28, 14 + (edge - 2) * 20)


def place_kernel(table_ref, me_ref, unit_ref, out_ref, source, sent):
    ylo, x, z, core = me_ref[0], me_ref[1], me_ref[2], me_ref[3]
    for s in range(QUAD):
        source[s * 192 : (s + 1) * 192, :] = unit_ref[s].astype(F32)
    sent[...] = jnp.zeros_like(sent)

    def target(tile, wanted):
        device = tile // TILES_HERE
        slot = tile - device * TILES_HERE
        mine = jnp.logical_and(device % CORE == core, device // (CORE * PLANE) == ylo)
        place = jnp.where(jnp.logical_and(mine, wanted), (device // CORE) % PLANE, PLANE)
        return place, slot * BLOCK_ROWS

    def body(i, carry):
        s = i // 12
        device = (((s // CORE) * NX + x) * NZ + z) * CORE + s % CORE
        at = (device * TILES_HERE * 4 + i % 12) * 3
        n, p, r = table_ref[at], table_ref[at + 1], table_ref[at + 2]
        base = pl.multiple_of(i * UNIT, UNIT)
        place, rows = target(n, True)
        sent[place, pl.ds(rows + edge_row(p), 6), :] = source[pl.ds(base, 6), :]
        sent[place, pl.ds(rows + FIELD_ROWS + 3 * p, 3), :] = source[pl.ds(base + 6, 3), :]
        deep = jnp.where(p % 2 == 0, place, PLANE)
        sent[deep, pl.ds(rows + edge_row(p) + 6, 6), :] = source[pl.ds(base + 9, 6), :]
        for last in range(2):
            f = jnp.where(p >= 2, 0, 2) + last
            beyond = (n * 4 + f) * 3
            t2, e2 = table_ref[beyond], table_ref[beyond + 1]
            place2, rows2 = target(t2, e2 % 2 == 0)
            end = base + jnp.where(r == last, 0, 15)
            sent[place2, pl.ds(rows2 + edge_row(e2) + 12 + p % 2, 1), :] = source[pl.ds(end, 1), :]
        return carry

    lax.fori_loop(0, QUAD * 12, body, 0)
    out_ref[...] = sent[:PLANE].astype(BF)


def join_kernel(got_ref, own_ref, out_ref, rows):
    total = got_ref[0].astype(F32)
    for q in range(1, PLANE):
        total = total + got_ref[q].astype(F32)
    for t in range(TILES_HERE):
        base, block = t * PAY_ROWS, t * BLOCK_ROWS
        own = own_ref[t].astype(F32)
        rows[base : base + OWN_ROWS, :] = own[:OWN_ROWS]
        rows[base + OWN_ROWS : base + X_HALF, :] = total[block : block + FIELD_ROWS]
        rows[base + X_HALF : base + X_HALF + C_OWN, :] = own[OWN_ROWS : OWN_ROWS + C_OWN]
        rows[base + X_HALF + C_OWN : base + PAY_ROWS - 2, :] = total[block + FIELD_ROWS : block + BLOCK_ROWS]
        rows[base + PAY_ROWS - 2 : base + PAY_ROWS, :] = jnp.zeros((2, 128), F32)
    whole = rows[...].astype(BF)
    for c in range(CHAN):
        out_ref[c] = whole


def main_kernel(
    me_ref, pay_ref, window_ref, lift_ref, down_ref, rim_ref, order_ref, wf_ref, wd_ref,
    coarse_ref, gp_ref, grads_ref, xs, cs, wf, wd, wins, lifts,
):
    chan = me_ref[4]
    pick = jnp.where(
        lax.broadcasted_iota(jnp.int32, (CH, C), 1) == lax.broadcasted_iota(jnp.int32, (CH, C), 0) + chan * CH, 1.0, 0.0
    ).astype(BF)
    for c in range(CHAN):
        for k in range(9):
            wf[k, c * CH : (c + 1) * CH, :] = wf_ref[c, k]
            wd[k, c * CH : (c + 1) * CH, :] = wd_ref[c, k]
        for t in range(TILES_HERE):
            base = t * PAY_ROWS
            for h in range(2):
                lanes = slice(h * CH, (h + 1) * CH)
                xs[t, h * X_HALF : (h + 1) * X_HALF, c * CH : (c + 1) * CH] = pay_ref[c, base : base + X_HALF, lanes]
                cs[t, h * C_HALF : (h + 1) * C_HALF, c * CH : (c + 1) * CH] = pay_ref[
                    c, base + X_HALF : base + PAY_ROWS, lanes
                ]
    for t in range(TILES_HERE):
        xs[t, 2 * X_HALF :, :] = jnp.zeros((C - 2 * X_HALF, C), BF)
    for k in range(9):
        for t in range(TILES_HERE):
            wins[k, t * PRE_ROWS : (t + 1) * PRE_ROWS, :] = dot_nn(
                window_ref[t, k * PRE_ROWS : (k + 1) * PRE_ROWS, :], xs[t]
            ).astype(BF)
            lifts[k, t * SPREAD_ROWS : (t + 1) * SPREAD_ROWS, :] = dot_nn(
                lift_ref[t, k * SPREAD_ROWS : (k + 1) * SPREAD_ROWS, :], cs[t]
            ).astype(BF)
    pre = dot_nn(wins[0], wf[0])
    back = dot_nt(lifts[0], wd[0])
    for k in range(1, 9):
        pre = pre + dot_nn(wins[k], wf[k])
        back = back + dot_nt(lifts[k], wd[k])
    scale = np.float32(np.sqrt(2 / np.pi))
    squared = pre * pre
    bent = jnp.tanh(scale * (pre + np.float32(0.044715) * squared * pre))
    gate = 0.5 * (1.0 + bent)
    hidden = (pre * gate).astype(BF)
    slope = gate + 0.5 * pre * (1.0 - bent * bent) * scale * (1.0 + np.float32(3 * 0.044715) * squared)

    down = [None] * TILES_HERE
    first_sum = None
    down_sum = None
    for t in range(TILES_HERE):
        own_hidden = hidden[t * PRE_ROWS : (t + 1) * PRE_ROWS]
        coarse = None
        windows = dot_nn(down_ref[...], own_hidden).astype(BF)
        for k in range(9):
            part = dot_nn(windows[k * DOWN_ROWS : (k + 1) * DOWN_ROWS], wd[k])
            coarse = part if coarse is None else coarse + part
        coarse_ref[t] = dot_nt(pick, coarse.astype(BF))[:, :COARSE].astype(BF)

        rows = back[t * SPREAD_ROWS : (t + 1) * SPREAD_ROWS]
        rims = rows[CELLS:].astype(BF)
        grad_hidden = rows[:CELLS] + dot_nn(rim_ref[...], rims)
        grad_pre = (grad_hidden * slope[t * PRE_ROWS : t * PRE_ROWS + CELLS]).astype(BF)
        gp_ref[t] = dot_nt(pick, grad_pre).astype(BF)

        x_own = dot_nt(pick, xs[t]).astype(BF)
        h_own = dot_nt(pick, own_hidden).astype(BF)
        up = dot_nn(order_ref[...], cs[t]).astype(BF)
        first_parts, down_parts = [], []
        for k in range(9):
            first_parts.append(
                dot_nt(x_own, window_ref[t, k * PRE_ROWS : k * PRE_ROWS + CELLS, :]).astype(BF)
            )
            down_parts.append(
                dot_nt(h_own, down_ref[k * DOWN_ROWS : (k + 1) * DOWN_ROWS, :]).astype(BF)
            )
        first = dot_nn(jnp.concatenate(first_parts, axis=0), grad_pre)
        first_sum = first if first_sum is None else first_sum + first
        part = dot_nn(jnp.concatenate(down_parts, axis=0), up)
        down_sum = part if down_sum is None else down_sum + part
    grads_ref[: 9 * CH, :] = first_sum.astype(BF)
    grads_ref[9 * CH :, :] = down_sum.astype(BF)


def vmem(count):
    return [pl.BlockSpec(memory_space=pltpu.VMEM)] * count


def smem(count):
    return [pl.BlockSpec(memory_space=pltpu.SMEM)] * count


LIMIT = pltpu.CompilerParams(vmem_limit_bytes=48 * 1024 * 1024)


def shards(fields, seam_table, w_first, w_down, cotangent):
    coords = [lax.axis_index(axis) for axis in ("ylo", "x", "z", "core", "chan")]
    me = jnp.stack(coords).astype(jnp.int32)
    all_first = lax.all_gather(w_first, "chan", axis=0, tiled=False)
    all_down = lax.all_gather(w_down, "chan", axis=0, tiled=False)

    sel_fields, sel_coarse = pack_selectors()
    own, units = pl.pallas_call(
        pack_kernel,
        out_shape=(
            jax.ShapeDtypeStruct((TILES_HERE, PACK_ROWS, 128), BF),
            jax.ShapeDtypeStruct((TILES_HERE * 4 * UNIT, 128), BF),
        ),
        in_specs=vmem(4),
        out_specs=tuple(vmem(2)),
        compiler_params=LIMIT,
        name="pack",
    )(fields, cotangent, jnp.asarray(sel_fields, BF), jnp.asarray(sel_coarse, BF))
    quad = lax.all_gather(units, ("ylo", "core"), axis=0, tiled=False)
    table = seam_table.reshape(-1)
    sends = pl.pallas_call(
        place_kernel,
        out_shape=jax.ShapeDtypeStruct((PLANE, SEND_ROWS, 128), BF),
        in_specs=smem(2) + vmem(1),
        out_specs=vmem(1)[0],
        scratch_shapes=[pltpu.VMEM((QUAD * 192, 128), F32), pltpu.VMEM((PLANE + 1, SEND_ROWS, 128), F32)],
        compiler_params=LIMIT,
        name="place",
    )(table, me, quad)
    got = lax.all_to_all(sends, ("x", "z"), 0, 0)
    joined = pl.pallas_call(
        join_kernel,
        out_shape=jax.ShapeDtypeStruct((CHAN, TILES_HERE * PAY_ROWS, 128), BF),
        in_specs=vmem(2),
        out_specs=vmem(1)[0],
        scratch_shapes=[pltpu.VMEM((TILES_HERE * PAY_ROWS, 128), F32)],
        compiler_params=LIMIT,
        name="join",
    )(got, own)
    payload = lax.all_to_all(joined, "chan", 0, 0)

    tile_at = ((coords[0] * NX + coords[1]) * NZ + coords[2]) * CORE + coords[3]
    own_table = lax.dynamic_slice_in_dim(seam_table, tile_at * TILES_HERE, TILES_HERE, 0)
    code = own_table[:, :, 1] * 2 + own_table[:, :, 2]
    chosen = (code[:, :, None] == jnp.arange(8, dtype=jnp.int32)).astype(BF).reshape(TILES_HERE, 32)
    one_hots = []
    for (fixed, varied), depth in ((window_index(), C), (spread_index(), 2 * C_HALF)):
        at = jnp.dot(chosen, jnp.asarray(varied, BF), preferred_element_type=F32) + jnp.asarray(fixed, F32)
        one_hots.append((at[:, :, None] == jnp.arange(1, depth + 1, dtype=jnp.int32).astype(F32)).astype(BF))

    coarse, grad_pre, grads = pl.pallas_call(
        main_kernel,
        out_shape=(
            jax.ShapeDtypeStruct((TILES_HERE, CH, COARSE), BF),
            jax.ShapeDtypeStruct((TILES_HERE, CH, CELLS), BF),
            jax.ShapeDtypeStruct((18 * CH, C), BF),
        ),
        in_specs=smem(1) + vmem(8),
        out_specs=tuple(vmem(3)),
        scratch_shapes=[
            pltpu.VMEM((TILES_HERE, C, C), BF),
            pltpu.VMEM((TILES_HERE, 2 * C_HALF, C), BF),
            pltpu.VMEM((9, C, C), BF),
            pltpu.VMEM((9, C, C), BF),
            pltpu.VMEM((9, TILES_HERE * PRE_ROWS, C), BF),
            pltpu.VMEM((9, TILES_HERE * SPREAD_ROWS, C), BF),
        ],
        compiler_params=LIMIT,
        name="tiles",
    )(
        me, payload, one_hots[0], one_hots[1], jnp.asarray(down_selector(), BF), jnp.asarray(rim_selector(), BF),
        jnp.asarray(order_selector(), BF), all_first, all_down,
    )

    part = lax.all_to_all(grads.reshape(QUAD, 18 * CH // QUAD, C), ("ylo", "core"), 0, 0)
    part = part.astype(F32).sum(0).astype(BF).reshape(PLANE, 18, 128)
    part = lax.all_to_all(part, ("x", "z"), 0, 0)
    part = part.astype(F32).sum(0).astype(BF)
    part = lax.all_to_all(jnp.broadcast_to(part[None], (PLANE, 18, 128)), ("x", "z"), 0, 0)
    whole = lax.all_gather(part.reshape(18 * CH // QUAD, C), ("ylo", "core"), axis=0, tiled=True)
    whole = whole.astype(F32).reshape(2, 9, CH, C)
    tiles = TILES_HERE * PLANE * QUAD
    return (
        coarse,
        whole[0] * float(tiles * CELLS) ** (-0.5),
        whole[1] * float(tiles * COARSE) ** (-0.5),
        grad_pre,
    )


def solution(mesh):
    fine = Mesh(mesh.devices.reshape(YLO, NX, NZ, CORE, CHAN), ("ylo", "x", "z", "core", "chan"))
    return jax.shard_map(
        shards,
        mesh=fine,
        in_specs=(
            P(TILE_AXES, "chan", None),
            P(),
            P(None, "chan", None),
            P(None, "chan", None),
            P(TILE_AXES, "chan", None),
        ),
        out_specs=(
            P(TILE_AXES, "chan", None),
            P(None, "chan", None),
            P(None, "chan", None),
            P(TILE_AXES, "chan", None),
        ),
        check_vma=False,
    )
```

```python
import numpy as np
import jax
import jax.numpy as jnp
from jax import lax
from jax.experimental import pallas as pl
from jax.experimental.pallas import tpu as pltpu
from jax.sharding import Mesh, PartitionSpec as P

S = 12
HALF = 6
CELLS = 144
COARSE = 36
TILES_HERE = 3
CH = 64
C = 256
YLO, NX, NZ, CORE, CHAN = 2, 4, 8, 2, 4
YX = YLO * NX
NEAR = YX * CORE
PLANE = YX * NZ
TILE_AXES = ("ylo", "x", "z", "core")
BF = jnp.bfloat16
F32 = jnp.float32

EDGE_ROWS = (0, 28, 14, 34)
FIELD_ROWS = 40
BLOCK_ROWS = 52
SEND_ROWS = 160
OWN_ROWS = 72
X_HALF = OWN_ROWS + FIELD_ROWS
C_OWN = 18
C_HALF = 32
PAY_ROWS = X_HALF + C_HALF
PACK_ROWS = 96
UNIT = 16
PRE_ROWS = 176
DOWN_ROWS = 48
SPREAD_ROWS = 192


def strip_cells(edge, depth):
    if edge == 0:
        return [depth * S + i for i in range(S)]
    if edge == 1:
        return [(S - 1 - depth) * S + i for i in range(S)]
    if edge == 2:
        return [i * S + depth for i in range(S)]
    return [i * S + S - 1 - depth for i in range(S)]


def pack_selectors():
    rows = PACK_ROWS + 4 * UNIT
    fields = np.zeros((2, rows, CELLS), np.float32)
    coarse = np.zeros((2, rows, COARSE), np.float32)
    for half in range(2):
        for row in range(OWN_ROWS):
            fields[half, row, 2 * row + half] = 1
        for row in range(C_OWN):
            coarse[half, OWN_ROWS + row, 2 * row + half] = 1
        for edge in range(4):
            base = PACK_ROWS + edge * UNIT
            near, far = strip_cells(edge, 0), strip_cells(edge, 1)
            for row in range(6):
                fields[half, base + row, near[2 * row + half]] = 1
                fields[half, base + 9 + row, far[2 * row + half]] = 1
            for row in range(3):
                at = 2 * row + half
                if edge == 0:
                    coarse[half, base + 6 + row, at] = 1
                if edge == 2:
                    coarse[half, base + 6 + row, at * HALF] = 1
            fields[half, base + 15, near[11 - half]] = 1
    return fields, coarse


def own_at(cell):
    return cell // 2 + X_HALF * (cell % 2)


def near_at(edge, along, depth):
    row = OWN_ROWS + EDGE_ROWS[edge] + 6 * depth
    if along < 0:
        return OWN_ROWS + EDGE_ROWS[edge] + 12 + X_HALF * depth
    if along >= S:
        return OWN_ROWS + EDGE_ROWS[edge] + 13 + X_HALF * depth
    return row + along // 2 + X_HALF * (along % 2)


def window_index():
    fixed = np.zeros((9, PRE_ROWS), np.float32)
    varied = np.zeros((4, 4, 2, 9, PRE_ROWS), np.float32)
    for k in range(9):
        a, b = k // 3, k % 3
        for cell in range(CELLS):
            row, col = cell // S + a, cell % S + b
            inner_row, inner_col = 1 <= row <= S, 1 <= col <= S
            if inner_row and inner_col:
                fixed[k, cell] = 1 + own_at((row - 1) * S + col - 1)
            elif inner_row or inner_col:
                edge = (2 if col == 0 else 3) if inner_row else (0 if row == 0 else 1)
                at = row - 1 if inner_row else col - 1
                for flip in range(2):
                    varied[edge, :, flip, k, cell] = 1 + near_at(edge, 11 - at if flip else at, 0)
        for slot, edge in enumerate((0, 2)):
            own = strip_cells(edge, 0)
            for facing in range(4):
                depth = (a - 1, 1 - a, b - 1, 1 - b)[facing]
                shift = (b - 1, b - 1, a - 1, a - 1)[facing]
                for flip in range(2):
                    for j in range(S):
                        along = (11 - j if flip else j) + shift
                        if depth >= 0:
                            at = near_at(edge, along, depth)
                        elif 0 <= along < S:
                            at = own_at(own[11 - along if flip else along])
                        else:
                            continue
                        varied[edge, facing, flip, k, CELLS + 16 * slot + j] = 1 + at
    return fixed.reshape(-1), varied.reshape(32, -1)


def spread_index():
    fixed = np.zeros((9, SPREAD_ROWS), np.float32)
    varied = np.zeros((4, 4, 2, 9, SPREAD_ROWS), np.float32)
    for k in range(9):
        a, b = k // 3, k % 3
        for cell in range(CELLS):
            row, col = cell // S + 1 - a, cell % S + 1 - b
            if row % 2 == 0 and col % 2 == 0 and 0 <= row < S and 0 <= col < S:
                at = (row // 2) * HALF + col // 2
                fixed[k, cell] = 1 + at // 2 + C_HALF * (at % 2)
        for edge in range(4):
            for flip in range(2):
                for j in range(S):
                    for facing, live, tap in ((0, a == 0, b), (2, b == 0, a)):
                        at = (11 - j if flip else j) + 1 - tap
                        if live and at % 2 == 0 and 0 <= at < S:
                            at //= 2
                            varied[edge, facing, flip, k, CELLS + edge * S + j] = (
                                1 + C_OWN + 3 * edge + at // 2 + C_HALF * (at % 2)
                            )
    return fixed.reshape(-1), varied.reshape(32, -1)


def down_selector():
    chosen = np.zeros((9, DOWN_ROWS, PRE_ROWS), np.float32)
    for k in range(9):
        for cell in range(COARSE):
            row, col = 2 * (cell // HALF) + k // 3, 2 * (cell % HALF) + k % 3
            if row == 0 and col == 0:
                continue
            if row == 0:
                at = CELLS + col - 1
            elif col == 0:
                at = CELLS + 16 + row - 1
            else:
                at = (row - 1) * S + col - 1
            chosen[k, cell, at] = 1
    return chosen.reshape(9 * DOWN_ROWS, PRE_ROWS)


def rim_selector():
    chosen = np.zeros((CELLS, 4 * S), np.float32)
    for edge in range(4):
        for j, cell in enumerate(strip_cells(edge, 0)):
            chosen[cell, edge * S + j] = 1
    return chosen


def order_selector():
    chosen = np.zeros((DOWN_ROWS, 2 * C_HALF), np.float32)
    for cell in range(COARSE):
        chosen[cell, cell // 2 + C_HALF * (cell % 2)] = 1
    return chosen


def dot_nn(left, right):
    return lax.dot_general(left, right, (((1,), (0,)), ((), ())), preferred_element_type=F32)


def dot_nt(left, right):
    return lax.dot_general(left, right, (((1,), (1,)), ((), ())), preferred_element_type=F32)


def pack_kernel(fields_ref, cot_ref, self_ref, selc_ref, own_ref, unit_ref):
    for t in range(TILES_HERE):
        halves = [
            (dot_nt(self_ref[h], fields_ref[t]) + dot_nt(selc_ref[h], cot_ref[t])).astype(BF)
            for h in range(2)
        ]
        for h in range(2):
            own_ref[t, :, h * CH : (h + 1) * CH] = halves[h][:PACK_ROWS]
            for copy in range(YX):
                unit_ref[copy, t * 4 * UNIT : (t + 1) * 4 * UNIT, h * CH : (h + 1) * CH] = halves[h][PACK_ROWS:]


def edge_words(seam_table):
    n, f, r = seam_table[:, :, 0], seam_table[:, :, 1], seam_table[:, :, 2]
    device = n // TILES_HERE
    group = (device % CORE) * YX + device // (NZ * CORE)
    unit = (group * TILES_HERE + n % TILES_HERE) * 4 + f
    z = (device // CORE) % NZ
    word = unit + r * 256 + z * 512
    beyond = (n * 4 + jnp.where(f < 2, 2, 0)) * 2 + f % 2
    return word.reshape(-1), beyond.reshape(-1)


def place_kernel(word_ref, beyond_ref, me_ref, unit_ref, out_ref, sent):
    ylo, x, z, core = me_ref[0], me_ref[1], me_ref[2], me_ref[3]

    def unit_at(word):
        keep = jnp.where(word // 512 == z, 1.0, 0.0).astype(F32)
        at = pl.multiple_of((word % 256) * UNIT, UNIT)
        return unit_ref[pl.ds(at, UNIT), :].astype(F32) * keep

    def body(z_to, carry):
        device = ((ylo * NX + x) * NZ + z_to) * CORE + core
        for t in range(TILES_HERE):
            for edge in range(4):
                at = (device * TILES_HERE + t) * 4 + edge
                unit = unit_at(word_ref[at])
                row = t * BLOCK_ROWS + EDGE_ROWS[edge]
                cot = t * BLOCK_ROWS + FIELD_ROWS + 3 * edge
                sent[z_to, row : row + 6, :] = unit[0:6]
                sent[z_to, cot : cot + 3, :] = unit[6:9]
                if edge % 2 == 0:
                    sent[z_to, row + 6 : row + 12, :] = unit[9:15]
                    beyond = beyond_ref[at]
                    for last in range(2):
                        word = word_ref[beyond // 2 + last]
                        end = unit_at(word)
                        low = (beyond + word // 256) % 2 == 0
                        sent[z_to, row + 12 + last : row + 13 + last, :] = jnp.where(low, end[0:1], end[15:16])
        sent[z_to, TILES_HERE * BLOCK_ROWS :, :] = jnp.zeros((SEND_ROWS - TILES_HERE * BLOCK_ROWS, 128), F32)
        return carry

    lax.fori_loop(0, NZ, body, 0)
    out_ref[...] = sent[...].astype(BF)


def join_kernel(got_ref, own_ref, out_ref, rows):
    total = got_ref[0].astype(F32)
    for q in range(1, NZ):
        total = total + got_ref[q].astype(F32)
    for t in range(TILES_HERE):
        base, block = t * PAY_ROWS, t * BLOCK_ROWS
        own = own_ref[t].astype(F32)
        rows[base : base + OWN_ROWS, :] = own[:OWN_ROWS]
        rows[base + OWN_ROWS : base + X_HALF, :] = total[block : block + FIELD_ROWS]
        rows[base + X_HALF : base + X_HALF + C_OWN, :] = own[OWN_ROWS : OWN_ROWS + C_OWN]
        rows[base + X_HALF + C_OWN : base + PAY_ROWS - 2, :] = total[block + FIELD_ROWS : block + BLOCK_ROWS]
        rows[base + PAY_ROWS - 2 : base + PAY_ROWS, :] = jnp.zeros((2, 128), F32)
    whole = rows[...].astype(BF)
    for c in range(CHAN):
        out_ref[c] = whole


def main_kernel(
    me_ref, pay_ref, window_ref, lift_ref, down_ref, rim_ref, order_ref, weights_ref,
    coarse_ref, gp_ref, grads_ref, xs, cs, wf, wd, wins, lifts,
):
    chan = me_ref[4]
    pick = jnp.where(
        lax.broadcasted_iota(jnp.int32, (CH, C), 1) == lax.broadcasted_iota(jnp.int32, (CH, C), 0) + chan * CH, 1.0, 0.0
    ).astype(BF)
    for c in range(CHAN):
        for k in range(9):
            wf[k, c * CH : (c + 1) * CH, :] = weights_ref[2 * c, k]
            wd[k, c * CH : (c + 1) * CH, :] = weights_ref[2 * c + 1, k]
        for t in range(TILES_HERE):
            base = t * PAY_ROWS
            for h in range(2):
                lanes = slice(h * CH, (h + 1) * CH)
                xs[t, h * X_HALF : (h + 1) * X_HALF, c * CH : (c + 1) * CH] = pay_ref[c, base : base + X_HALF, lanes]
                cs[t, h * C_HALF : (h + 1) * C_HALF, c * CH : (c + 1) * CH] = pay_ref[
                    c, base + X_HALF : base + PAY_ROWS, lanes
                ]
    for t in range(TILES_HERE):
        xs[t, 2 * X_HALF :, :] = jnp.zeros((C - 2 * X_HALF, C), BF)
    for k in range(9):
        for t in range(TILES_HERE):
            wins[k, t * PRE_ROWS : (t + 1) * PRE_ROWS, :] = dot_nn(
                window_ref[t, k * PRE_ROWS : (k + 1) * PRE_ROWS, :], xs[t]
            ).astype(BF)
            lifts[k, t * SPREAD_ROWS : (t + 1) * SPREAD_ROWS, :] = dot_nn(
                lift_ref[t, k * SPREAD_ROWS : (k + 1) * SPREAD_ROWS, :], cs[t]
            ).astype(BF)
    pre = dot_nn(wins[0], wf[0])
    back = dot_nt(lifts[0], wd[0])
    for k in range(1, 9):
        pre = pre + dot_nn(wins[k], wf[k])
        back = back + dot_nt(lifts[k], wd[k])
    scale = np.float32(np.sqrt(2 / np.pi))
    squared = pre * pre
    bent = jnp.tanh(scale * (pre + np.float32(0.044715) * squared * pre))
    gate = 0.5 * (1.0 + bent)
    hidden = (pre * gate).astype(BF)
    slope = gate + 0.5 * pre * (1.0 - bent * bent) * scale * (1.0 + np.float32(3 * 0.044715) * squared)

    down = [None] * TILES_HERE
    first_sum = None
    down_sum = None
    for t in range(TILES_HERE):
        own_hidden = hidden[t * PRE_ROWS : (t + 1) * PRE_ROWS]
        coarse = None
        windows = dot_nn(down_ref[...], own_hidden).astype(BF)
        for k in range(9):
            part = dot_nn(windows[k * DOWN_ROWS : (k + 1) * DOWN_ROWS], wd[k])
            coarse = part if coarse is None else coarse + part
        coarse_ref[t] = dot_nt(pick, coarse.astype(BF))[:, :COARSE].astype(BF)

        rows = back[t * SPREAD_ROWS : (t + 1) * SPREAD_ROWS]
        rims = rows[CELLS:].astype(BF)
        grad_hidden = rows[:CELLS] + dot_nn(rim_ref[...], rims)
        grad_pre = (grad_hidden * slope[t * PRE_ROWS : t * PRE_ROWS + CELLS]).astype(BF)
        gp_ref[t] = dot_nt(pick, grad_pre).astype(BF)

        x_own = dot_nt(pick, xs[t]).astype(BF)
        h_own = dot_nt(pick, own_hidden).astype(BF)
        up = dot_nn(order_ref[...], cs[t]).astype(BF)
        first_parts, down_parts = [], []
        for k in range(9):
            first_parts.append(
                dot_nt(x_own, window_ref[t, k * PRE_ROWS : k * PRE_ROWS + CELLS, :]).astype(BF)
            )
            down_parts.append(
                dot_nt(h_own, down_ref[k * DOWN_ROWS : (k + 1) * DOWN_ROWS, :]).astype(BF)
            )
        first = dot_nn(jnp.concatenate(first_parts, axis=0), grad_pre)
        first_sum = first if first_sum is None else first_sum + first
        part = dot_nn(jnp.concatenate(down_parts, axis=0), up)
        down_sum = part if down_sum is None else down_sum + part
    for h in range(CORE):
        grads_ref[h, : 9 * CH, :] = first_sum[:, h * 128 : (h + 1) * 128].astype(BF)
        grads_ref[h, 9 * CH :, :] = down_sum[:, h * 128 : (h + 1) * 128].astype(BF)


def vmem(count):
    return [pl.BlockSpec(memory_space=pltpu.VMEM)] * count


def smem(count):
    return [pl.BlockSpec(memory_space=pltpu.SMEM)] * count


LIMIT = pltpu.CompilerParams(vmem_limit_bytes=48 * 1024 * 1024)


def shards(fields, seam_table, w_first, w_down, cotangent):
    coords = [lax.axis_index(axis) for axis in ("ylo", "x", "z", "core", "chan")]
    me = jnp.stack(coords).astype(jnp.int32)
    half = jnp.where(coords[3] == 0, w_first, w_down)
    weights = lax.all_gather(half, ("chan", "core"), axis=0, tiled=False)

    sel_fields, sel_coarse = pack_selectors()
    own, units = pl.pallas_call(
        pack_kernel,
        out_shape=(
            jax.ShapeDtypeStruct((TILES_HERE, PACK_ROWS, 128), BF),
            jax.ShapeDtypeStruct((YX, TILES_HERE * 4 * UNIT, 128), BF),
        ),
        in_specs=vmem(4),
        out_specs=tuple(vmem(2)),
        compiler_params=LIMIT,
        name="pack",
    )(fields, cotangent, jnp.asarray(sel_fields, BF), jnp.asarray(sel_coarse, BF))
    units = lax.all_to_all(units, ("ylo", "x"), 0, 0).reshape(-1, 128)
    units = lax.all_gather(units, "core", axis=0, tiled=True)
    words, beyond = edge_words(seam_table)
    sends = pl.pallas_call(
        place_kernel,
        out_shape=jax.ShapeDtypeStruct((NZ, SEND_ROWS, 128), BF),
        in_specs=smem(3) + vmem(1),
        out_specs=vmem(1)[0],
        scratch_shapes=[pltpu.VMEM((NZ, SEND_ROWS, 128), F32)],
        compiler_params=LIMIT,
        name="place",
    )(words, beyond, me, units)
    got = lax.all_to_all(sends, "z", 0, 0)
    joined = pl.pallas_call(
        join_kernel,
        out_shape=jax.ShapeDtypeStruct((CHAN, TILES_HERE * PAY_ROWS, 128), BF),
        in_specs=vmem(2),
        out_specs=vmem(1)[0],
        scratch_shapes=[pltpu.VMEM((TILES_HERE * PAY_ROWS, 128), F32)],
        compiler_params=LIMIT,
        name="join",
    )(got, own)
    payload = lax.all_to_all(joined, "chan", 0, 0)

    tile_at = ((coords[0] * NX + coords[1]) * NZ + coords[2]) * CORE + coords[3]
    own_table = lax.dynamic_slice_in_dim(seam_table, tile_at * TILES_HERE, TILES_HERE, 0)
    code = own_table[:, :, 1] * 2 + own_table[:, :, 2]
    chosen = (code[:, :, None] == jnp.arange(8, dtype=jnp.int32)).astype(BF).reshape(TILES_HERE, 32)
    one_hots = []
    for (fixed, varied), depth in ((window_index(), C), (spread_index(), 2 * C_HALF)):
        at = jnp.dot(chosen, jnp.asarray(varied, BF), preferred_element_type=F32) + jnp.asarray(fixed, F32)
        one_hots.append((at[:, :, None] == jnp.arange(1, depth + 1, dtype=jnp.int32).astype(F32)).astype(BF))

    coarse, grad_pre, grads = pl.pallas_call(
        main_kernel,
        out_shape=(
            jax.ShapeDtypeStruct((TILES_HERE, CH, COARSE), BF),
            jax.ShapeDtypeStruct((TILES_HERE, CH, CELLS), BF),
            jax.ShapeDtypeStruct((CORE, 18 * CH, 128), BF),
        ),
        in_specs=smem(1) + vmem(7),
        out_specs=tuple(vmem(3)),
        scratch_shapes=[
            pltpu.VMEM((TILES_HERE, C, C), BF),
            pltpu.VMEM((TILES_HERE, 2 * C_HALF, C), BF),
            pltpu.VMEM((9, C, C), BF),
            pltpu.VMEM((9, C, C), BF),
            pltpu.VMEM((9, TILES_HERE * PRE_ROWS, C), BF),
            pltpu.VMEM((9, TILES_HERE * SPREAD_ROWS, C), BF),
        ],
        compiler_params=LIMIT,
        name="tiles",
    )(
        me, payload, one_hots[0], one_hots[1], jnp.asarray(down_selector(), BF), jnp.asarray(rim_selector(), BF),
        jnp.asarray(order_selector(), BF), weights,
    )

    part = lax.all_to_all(grads, "core", 0, 0)
    part = (part[0].astype(F32) + part[1].astype(F32)).astype(BF).reshape(PLANE, 18, 128)
    part = lax.all_to_all(part, ("ylo", "x", "z"), 0, 0)
    part = part.astype(F32).sum(0).astype(BF)
    part = lax.all_to_all(jnp.broadcast_to(part[None], (PLANE, 18, 128)), ("ylo", "x", "z"), 0, 0)
    whole = lax.all_gather(part.reshape(18 * CH, 128), "core", axis=0, tiled=False)
    whole = jnp.concatenate([whole[0], whole[1]], axis=1).astype(F32).reshape(2, 9, CH, C)
    tiles = TILES_HERE * PLANE * CORE
    return (
        coarse,
        whole[0] * float(tiles * CELLS) ** (-0.5),
        whole[1] * float(tiles * COARSE) ** (-0.5),
        grad_pre,
    )


def solution(mesh):
    fine = Mesh(mesh.devices.reshape(YLO, NX, NZ, CORE, CHAN), ("ylo", "x", "z", "core", "chan"))
    return jax.shard_map(
        shards,
        mesh=fine,
        in_specs=(
            P(TILE_AXES, "chan", None),
            P(),
            P(None, "chan", None),
            P(None, "chan", None),
            P(TILE_AXES, "chan", None),
        ),
        out_specs=(
            P(TILE_AXES, "chan", None),
            P(None, "chan", None),
            P(None, "chan", None),
            P(TILE_AXES, "chan", None),
        ),
        check_vma=False,
    )
```

```python
import numpy as np
import jax
import jax.numpy as jnp
from jax import lax
from jax.experimental import pallas as pl
from jax.experimental.pallas import tpu as pltpu
from jax.sharding import Mesh, PartitionSpec as P

S = 12
HALF = 6
CELLS = 144
COARSE = 36
TILES_HERE = 3
CH = 64
C = 256
YLO, NX, NZ, CORE, CHAN = 2, 4, 8, 2, 4
YX = YLO * NX
NEAR = YX * CORE
PLANE = YX * NZ
TILE_AXES = ("ylo", "x", "z", "core")
BF = jnp.bfloat16
F32 = jnp.float32

EDGE_ROWS = (0, 28, 14, 34)
FIELD_ROWS = 40
BLOCK_ROWS = 52
SEND_ROWS = 160
OWN_ROWS = 72
X_HALF = OWN_ROWS + FIELD_ROWS
C_OWN = 18
C_HALF = 32
PAY_ROWS = X_HALF + C_HALF
PACK_ROWS = 96
UNIT = 16
PRE_ROWS = 176
DOWN_ROWS = 48
SPREAD_ROWS = 192


def strip_cells(edge, depth):
    if edge == 0:
        return [depth * S + i for i in range(S)]
    if edge == 1:
        return [(S - 1 - depth) * S + i for i in range(S)]
    if edge == 2:
        return [i * S + depth for i in range(S)]
    return [i * S + S - 1 - depth for i in range(S)]


def pack_selectors():
    rows = PACK_ROWS + 4 * UNIT
    fields = np.zeros((2, rows, CELLS), np.float32)
    coarse = np.zeros((2, rows, COARSE), np.float32)
    for half in range(2):
        for row in range(OWN_ROWS):
            fields[half, row, 2 * row + half] = 1
        for row in range(C_OWN):
            coarse[half, OWN_ROWS + row, 2 * row + half] = 1
        for edge in range(4):
            base = PACK_ROWS + edge * UNIT
            near, far = strip_cells(edge, 0), strip_cells(edge, 1)
            for row in range(6):
                fields[half, base + row, near[2 * row + half]] = 1
                fields[half, base + 9 + row, far[2 * row + half]] = 1
            for row in range(3):
                at = 2 * row + half
                if edge == 0:
                    coarse[half, base + 6 + row, at] = 1
                if edge == 2:
                    coarse[half, base + 6 + row, at * HALF] = 1
            fields[half, base + 15, near[11 - half]] = 1
    return fields, coarse


def own_at(cell):
    return cell // 2 + X_HALF * (cell % 2)


def near_at(edge, along, depth):
    row = OWN_ROWS + EDGE_ROWS[edge] + 6 * depth
    if along < 0:
        return OWN_ROWS + EDGE_ROWS[edge] + 12 + X_HALF * depth
    if along >= S:
        return OWN_ROWS + EDGE_ROWS[edge] + 13 + X_HALF * depth
    return row + along // 2 + X_HALF * (along % 2)


def window_index():
    fixed = np.zeros((9, PRE_ROWS), np.float32)
    varied = np.zeros((4, 4, 2, 9, PRE_ROWS), np.float32)
    for k in range(9):
        a, b = k // 3, k % 3
        for cell in range(CELLS):
            row, col = cell // S + a, cell % S + b
            inner_row, inner_col = 1 <= row <= S, 1 <= col <= S
            if inner_row and inner_col:
                fixed[k, cell] = 1 + own_at((row - 1) * S + col - 1)
            elif inner_row or inner_col:
                edge = (2 if col == 0 else 3) if inner_row else (0 if row == 0 else 1)
                at = row - 1 if inner_row else col - 1
                for flip in range(2):
                    varied[edge, :, flip, k, cell] = 1 + near_at(edge, 11 - at if flip else at, 0)
        for slot, edge in enumerate((0, 2)):
            own = strip_cells(edge, 0)
            for facing in range(4):
                depth = (a - 1, 1 - a, b - 1, 1 - b)[facing]
                shift = (b - 1, b - 1, a - 1, a - 1)[facing]
                for flip in range(2):
                    for j in range(S):
                        along = (11 - j if flip else j) + shift
                        if depth >= 0:
                            at = near_at(edge, along, depth)
                        elif 0 <= along < S:
                            at = own_at(own[11 - along if flip else along])
                        else:
                            continue
                        varied[edge, facing, flip, k, CELLS + 16 * slot + j] = 1 + at
    return fixed.reshape(-1), varied.reshape(32, -1)


def spread_index():
    fixed = np.zeros((9, SPREAD_ROWS), np.float32)
    varied = np.zeros((4, 4, 2, 9, SPREAD_ROWS), np.float32)
    for k in range(9):
        a, b = k // 3, k % 3
        for cell in range(CELLS):
            row, col = cell // S + 1 - a, cell % S + 1 - b
            if row % 2 == 0 and col % 2 == 0 and 0 <= row < S and 0 <= col < S:
                at = (row // 2) * HALF + col // 2
                fixed[k, cell] = 1 + at // 2 + C_HALF * (at % 2)
        for edge in range(4):
            for flip in range(2):
                for j in range(S):
                    for facing, live, tap in ((0, a == 0, b), (2, b == 0, a)):
                        at = (11 - j if flip else j) + 1 - tap
                        if live and at % 2 == 0 and 0 <= at < S:
                            at //= 2
                            varied[edge, facing, flip, k, CELLS + edge * S + j] = (
                                1 + C_OWN + 3 * edge + at // 2 + C_HALF * (at % 2)
                            )
    return fixed.reshape(-1), varied.reshape(32, -1)


def down_selector():
    chosen = np.zeros((9, DOWN_ROWS, PRE_ROWS), np.float32)
    for k in range(9):
        for cell in range(COARSE):
            row, col = 2 * (cell // HALF) + k // 3, 2 * (cell % HALF) + k % 3
            if row == 0 and col == 0:
                continue
            if row == 0:
                at = CELLS + col - 1
            elif col == 0:
                at = CELLS + 16 + row - 1
            else:
                at = (row - 1) * S + col - 1
            chosen[k, cell, at] = 1
    return chosen.reshape(9 * DOWN_ROWS, PRE_ROWS)


def rim_selector():
    chosen = np.zeros((CELLS, 4 * S), np.float32)
    for edge in range(4):
        for j, cell in enumerate(strip_cells(edge, 0)):
            chosen[cell, edge * S + j] = 1
    return chosen


def order_selector():
    chosen = np.zeros((DOWN_ROWS, 2 * C_HALF), np.float32)
    for cell in range(COARSE):
        chosen[cell, cell // 2 + C_HALF * (cell % 2)] = 1
    return chosen


def dot_nn(left, right):
    return lax.dot_general(left, right, (((1,), (0,)), ((), ())), preferred_element_type=F32)


def dot_nt(left, right):
    return lax.dot_general(left, right, (((1,), (1,)), ((), ())), preferred_element_type=F32)


def pack_kernel(me_ref, fields_ref, cot_ref, self_ref, selc_ref, first_ref, down_ref, own_ref, unit_ref, half_ref, sem):
    @pl.when(me_ref[3] == 0)
    def _():
        pltpu.make_async_copy(first_ref, half_ref, sem).start()

    @pl.when(me_ref[3] == 1)
    def _():
        pltpu.make_async_copy(down_ref, half_ref, sem).start()

    for t in range(TILES_HERE):
        halves = [
            (dot_nt(self_ref[h], fields_ref[t]) + dot_nn(selc_ref[h], cot_ref[t])).astype(BF)
            for h in range(2)
        ]
        for h in range(2):
            own_ref[t, :, h * CH : (h + 1) * CH] = halves[h][:PACK_ROWS]
            for copy in range(YX):
                unit_ref[copy, t * 4 * UNIT : (t + 1) * 4 * UNIT, h * CH : (h + 1) * CH] = halves[h][PACK_ROWS:]
    pltpu.make_async_copy(first_ref, half_ref, sem).wait()


def edge_words(seam_table):
    n, f, r = seam_table[:, :, 0], seam_table[:, :, 1], seam_table[:, :, 2]
    device = n // TILES_HERE
    group = (device % CORE) * YX + device // (NZ * CORE)
    unit = (group * TILES_HERE + n % TILES_HERE) * 4 + f
    z = (device // CORE) % NZ
    word = unit + r * 256 + z * 512
    beyond = (n * 4 + jnp.where(f < 2, 2, 0)) * 2 + f % 2
    return word.reshape(-1), beyond.reshape(-1)


def place_kernel(word_ref, beyond_ref, me_ref, unit_ref, out_ref, sent):
    ylo, x, z, core = me_ref[0], me_ref[1], me_ref[2], me_ref[3]

    def unit_at(word):
        keep = jnp.where((word >> 9) == z, 1.0, 0.0).astype(F32)
        at = pl.multiple_of((word & 255) * UNIT, UNIT)
        return unit_ref[pl.ds(at, UNIT), :].astype(F32) * keep

    def body(z_to, carry):
        device = ((ylo * NX + x) * NZ + z_to) * CORE + core
        for t in range(TILES_HERE):
            for edge in range(4):
                at = (device * TILES_HERE + t) * 4 + edge
                unit = unit_at(word_ref[at])
                row = t * BLOCK_ROWS + EDGE_ROWS[edge]
                cot = t * BLOCK_ROWS + FIELD_ROWS + 3 * edge
                sent[z_to, row : row + 6, :] = unit[0:6]
                sent[z_to, cot : cot + 3, :] = unit[6:9]
                if edge % 2 == 0:
                    sent[z_to, row + 6 : row + 12, :] = unit[9:15]
                    beyond = beyond_ref[at]
                    for last in range(2):
                        word = word_ref[(beyond >> 1) + last]
                        end = unit_at(word)
                        low = ((beyond + (word >> 8)) & 1) == 0
                        sent[z_to, row + 12 + last : row + 13 + last, :] = jnp.where(low, end[0:1], end[15:16])
        sent[z_to, TILES_HERE * BLOCK_ROWS :, :] = jnp.zeros((SEND_ROWS - TILES_HERE * BLOCK_ROWS, 128), F32)
        return carry

    lax.fori_loop(0, NZ, body, 0)
    out_ref[...] = sent[...].astype(BF)


def join_kernel(got_ref, own_ref, out_ref, rows):
    total = got_ref[0].astype(F32)
    for q in range(1, NZ):
        total = total + got_ref[q].astype(F32)
    for t in range(TILES_HERE):
        base, block = t * PAY_ROWS, t * BLOCK_ROWS
        own = own_ref[t].astype(F32)
        rows[base : base + OWN_ROWS, :] = own[:OWN_ROWS]
        rows[base + OWN_ROWS : base + X_HALF, :] = total[block : block + FIELD_ROWS]
        rows[base + X_HALF : base + X_HALF + C_OWN, :] = own[OWN_ROWS : OWN_ROWS + C_OWN]
        rows[base + X_HALF + C_OWN : base + PAY_ROWS - 2, :] = total[block + FIELD_ROWS : block + BLOCK_ROWS]
        rows[base + PAY_ROWS - 2 : base + PAY_ROWS, :] = jnp.zeros((2, 128), F32)
    whole = rows[...].astype(BF)
    for c in range(CHAN):
        out_ref[c] = whole


def main_kernel(
    me_ref, pay_ref, window_ref, lift_ref, down_ref, rim_ref, order_ref, weights_ref,
    coarse_ref, gp_ref, grads_ref, xs, cs, wf, wd, wins, lifts, sems,
):
    copies = []
    for c in range(CHAN):
        for which, held in enumerate((wf, wd)):
            copies.append(
                pltpu.make_async_copy(
                    weights_ref.at[2 * c + which], held.at[:, pl.ds(c * CH, CH), :], sems.at[2 * c + which]
                )
            )
    for copy in copies:
        copy.start()
    chan = me_ref[4]
    pick = jnp.where(
        lax.broadcasted_iota(jnp.int32, (CH, C), 1) == lax.broadcasted_iota(jnp.int32, (CH, C), 0) + chan * CH, 1.0, 0.0
    ).astype(BF)
    for c in range(CHAN):
        for t in range(TILES_HERE):
            base = t * PAY_ROWS
            for h in range(2):
                lanes = slice(h * CH, (h + 1) * CH)
                xs[t, h * X_HALF : (h + 1) * X_HALF, c * CH : (c + 1) * CH] = pay_ref[c, base : base + X_HALF, lanes]
                cs[t, h * C_HALF : (h + 1) * C_HALF, c * CH : (c + 1) * CH] = pay_ref[
                    c, base + X_HALF : base + PAY_ROWS, lanes
                ]
    for t in range(TILES_HERE):
        xs[t, 2 * X_HALF :, :] = jnp.zeros((C - 2 * X_HALF, C), BF)
    for k in range(9):
        for t in range(TILES_HERE):
            wins[k, t * PRE_ROWS : (t + 1) * PRE_ROWS, :] = dot_nn(
                window_ref[t, k * PRE_ROWS : (k + 1) * PRE_ROWS, :], xs[t]
            ).astype(BF)
            lifts[k, t * SPREAD_ROWS : (t + 1) * SPREAD_ROWS, :] = dot_nn(
                lift_ref[t, k * SPREAD_ROWS : (k + 1) * SPREAD_ROWS, :], cs[t]
            ).astype(BF)
    for copy in copies:
        copy.wait()
    pre = dot_nn(wins[0], wf[0])
    back = dot_nt(lifts[0], wd[0])
    for k in range(1, 9):
        pre = pre + dot_nn(wins[k], wf[k])
        back = back + dot_nt(lifts[k], wd[k])
    scale = np.float32(np.sqrt(2 / np.pi))
    squared = pre * pre
    bent = jnp.tanh(scale * (pre + np.float32(0.044715) * squared * pre))
    gate = 0.5 * (1.0 + bent)
    hidden = (pre * gate).astype(BF)
    slope = gate + 0.5 * pre * (1.0 - bent * bent) * scale * (1.0 + np.float32(3 * 0.044715) * squared)

    down = [None] * TILES_HERE
    first_sum = None
    down_sum = None
    for t in range(TILES_HERE):
        own_hidden = hidden[t * PRE_ROWS : (t + 1) * PRE_ROWS]
        coarse = None
        windows = dot_nn(down_ref[...], own_hidden).astype(BF)
        for k in range(9):
            part = dot_nn(windows[k * DOWN_ROWS : (k + 1) * DOWN_ROWS], wd[k])
            coarse = part if coarse is None else coarse + part
        coarse_ref[t] = dot_nt(coarse.astype(BF), pick)[:COARSE].astype(BF)

        rows = back[t * SPREAD_ROWS : (t + 1) * SPREAD_ROWS]
        rims = rows[CELLS:].astype(BF)
        grad_hidden = rows[:CELLS] + dot_nn(rim_ref[...], rims)
        grad_pre = (grad_hidden * slope[t * PRE_ROWS : t * PRE_ROWS + CELLS]).astype(BF)
        gp_ref[t] = dot_nt(pick, grad_pre).astype(BF)

        x_own = dot_nt(pick, xs[t]).astype(BF)
        h_own = dot_nt(pick, own_hidden).astype(BF)
        up = dot_nn(order_ref[...], cs[t]).astype(BF)
        first_parts, down_parts = [], []
        for k in range(9):
            first_parts.append(
                dot_nt(x_own, window_ref[t, k * PRE_ROWS : k * PRE_ROWS + CELLS, :]).astype(BF)
            )
            down_parts.append(
                dot_nt(h_own, down_ref[k * DOWN_ROWS : (k + 1) * DOWN_ROWS, :]).astype(BF)
            )
        first = dot_nn(jnp.concatenate(first_parts, axis=0), grad_pre)
        first_sum = first if first_sum is None else first_sum + first
        part = dot_nn(jnp.concatenate(down_parts, axis=0), up)
        down_sum = part if down_sum is None else down_sum + part
    for h in range(CORE):
        grads_ref[h, : 9 * CH, :] = first_sum[:, h * 128 : (h + 1) * 128].astype(BF)
        grads_ref[h, 9 * CH :, :] = down_sum[:, h * 128 : (h + 1) * 128].astype(BF)


def vmem(count):
    return [pl.BlockSpec(memory_space=pltpu.VMEM)] * count


def anywhere(count):
    return [pl.BlockSpec(memory_space=pl.ANY)] * count


def smem(count):
    return [pl.BlockSpec(memory_space=pltpu.SMEM)] * count


LIMIT = pltpu.CompilerParams(vmem_limit_bytes=48 * 1024 * 1024)


def shards(fields, seam_table, w_first, w_down, cotangent):
    coords = [lax.axis_index(axis) for axis in ("ylo", "x", "z", "core", "chan")]
    me = jnp.stack(coords).astype(jnp.int32)
    sel_fields, sel_coarse = pack_selectors()
    own, units, half = pl.pallas_call(
        pack_kernel,
        out_shape=(
            jax.ShapeDtypeStruct((TILES_HERE, PACK_ROWS, 128), BF),
            jax.ShapeDtypeStruct((YX, TILES_HERE * 4 * UNIT, 128), BF),
            jax.ShapeDtypeStruct(w_first.shape, BF),
        ),
        in_specs=smem(1) + vmem(4) + anywhere(2),
        out_specs=tuple(vmem(2) + anywhere(1)),
        scratch_shapes=[pltpu.SemaphoreType.DMA],
        compiler_params=LIMIT,
        name="pack",
    )(
        me, fields, jnp.swapaxes(cotangent, 1, 2), jnp.asarray(sel_fields, BF), jnp.asarray(sel_coarse, BF),
        w_first, w_down,
    )
    weights = lax.all_gather(half, ("chan", "core"), axis=0, tiled=False)
    units = lax.all_to_all(units, ("ylo", "x"), 0, 0).reshape(-1, 128)
    units = lax.all_gather(units, "core", axis=0, tiled=True)
    words, beyond = edge_words(seam_table)
    sends = pl.pallas_call(
        place_kernel,
        out_shape=jax.ShapeDtypeStruct((NZ, SEND_ROWS, 128), BF),
        in_specs=smem(3) + vmem(1),
        out_specs=vmem(1)[0],
        scratch_shapes=[pltpu.VMEM((NZ, SEND_ROWS, 128), F32)],
        compiler_params=LIMIT,
        name="place",
    )(words, beyond, me, units)
    got = lax.all_to_all(sends, "z", 0, 0)
    joined = pl.pallas_call(
        join_kernel,
        out_shape=jax.ShapeDtypeStruct((CHAN, TILES_HERE * PAY_ROWS, 128), BF),
        in_specs=vmem(2),
        out_specs=vmem(1)[0],
        scratch_shapes=[pltpu.VMEM((TILES_HERE * PAY_ROWS, 128), F32)],
        compiler_params=LIMIT,
        name="join",
    )(got, own)
    payload = lax.all_to_all(joined, "chan", 0, 0)

    tile_at = ((coords[0] * NX + coords[1]) * NZ + coords[2]) * CORE + coords[3]
    own_table = lax.dynamic_slice_in_dim(seam_table, tile_at * TILES_HERE, TILES_HERE, 0)
    code = own_table[:, :, 1] * 2 + own_table[:, :, 2]
    chosen = (code[:, :, None] == jnp.arange(8, dtype=jnp.int32)).astype(BF).reshape(TILES_HERE, 32)
    one_hots = []
    for (fixed, varied), depth in ((window_index(), C), (spread_index(), 2 * C_HALF)):
        at = jnp.dot(chosen, jnp.asarray(varied, BF), preferred_element_type=F32) + jnp.asarray(fixed, F32)
        one_hots.append((at[:, :, None] == jnp.arange(1, depth + 1, dtype=jnp.int32).astype(F32)).astype(BF))

    coarse, grad_pre, grads = pl.pallas_call(
        main_kernel,
        out_shape=(
            jax.ShapeDtypeStruct((TILES_HERE, COARSE, CH), BF),
            jax.ShapeDtypeStruct((TILES_HERE, CH, CELLS), BF),
            jax.ShapeDtypeStruct((CORE, 18 * CH, 128), BF),
        ),
        in_specs=smem(1) + vmem(6) + anywhere(1),
        out_specs=tuple(vmem(3)),
        scratch_shapes=[
            pltpu.VMEM((TILES_HERE, C, C), BF),
            pltpu.VMEM((TILES_HERE, 2 * C_HALF, C), BF),
            pltpu.VMEM((9, C, C), BF),
            pltpu.VMEM((9, C, C), BF),
            pltpu.VMEM((9, TILES_HERE * PRE_ROWS, C), BF),
            pltpu.VMEM((9, TILES_HERE * SPREAD_ROWS, C), BF),
            pltpu.SemaphoreType.DMA((2 * CHAN,)),
        ],
        compiler_params=LIMIT,
        name="tiles",
    )(
        me, payload, one_hots[0], one_hots[1], jnp.asarray(down_selector(), BF), jnp.asarray(rim_selector(), BF),
        jnp.asarray(order_selector(), BF), weights,
    )

    part = lax.all_to_all(grads, "core", 0, 0)
    part = (part[0].astype(F32) + part[1].astype(F32)).astype(BF).reshape(NX * NZ, 36, 128)
    part = lax.all_to_all(part, ("x", "z"), 0, 0)
    part = part.astype(F32).sum(0).astype(BF)
    part = lax.all_gather(part, "ylo", axis=0, tiled=False)
    part = (part[0].astype(F32) + part[1].astype(F32)).astype(BF)
    part = lax.all_to_all(jnp.broadcast_to(part[None], (NX * NZ, 36, 128)), ("x", "z"), 0, 0)
    whole = lax.all_gather(part.reshape(18 * CH, 128), "core", axis=0, tiled=False)
    whole = jnp.concatenate([whole[0], whole[1]], axis=1).astype(F32).reshape(2, 9, CH, C)
    tiles = TILES_HERE * PLANE * CORE
    return (
        jnp.swapaxes(coarse, 1, 2),
        whole[0] * float(tiles * CELLS) ** (-0.5),
        whole[1] * float(tiles * COARSE) ** (-0.5),
        grad_pre,
    )


def solution(mesh):
    fine = Mesh(mesh.devices.reshape(YLO, NX, NZ, CORE, CHAN), ("ylo", "x", "z", "core", "chan"))
    return jax.shard_map(
        shards,
        mesh=fine,
        in_specs=(
            P(TILE_AXES, "chan", None),
            P(),
            P(None, "chan", None),
            P(None, "chan", None),
            P(TILE_AXES, "chan", None),
        ),
        out_specs=(
            P(TILE_AXES, "chan", None),
            P(None, "chan", None),
            P(None, "chan", None),
            P(TILE_AXES, "chan", None),
        ),
        check_vma=False,
    )
```

```python
import numpy as np
import jax
import jax.numpy as jnp
from jax import lax
from jax.experimental import pallas as pl
from jax.experimental.pallas import tpu as pltpu
from jax.sharding import Mesh, PartitionSpec as P

S = 12
HALF = 6
CELLS = 144
COARSE = 36
TILES_HERE = 3
CH = 64
C = 256
YLO, NX, NZ, CORE, CHAN = 2, 4, 8, 2, 4
YX = YLO * NX
NEAR = YX * CORE
PLANE = YX * NZ
TILE_AXES = ("ylo", "x", "z", "core")
BF = jnp.bfloat16
F32 = jnp.float32

EDGE_ROWS = (0, 28, 14, 34)
FIELD_ROWS = 40
BLOCK_ROWS = 52
SEND_ROWS = 160
OWN_ROWS = 72
X_HALF = OWN_ROWS + FIELD_ROWS
C_OWN = 18
C_HALF = 32
PAY_ROWS = X_HALF + C_HALF
PACK_ROWS = 96
UNIT = 16
PART = 40
INNER = 4 * PART
PRE_ROWS = INNER + 32
DOWN_ROWS = 48
RIM_ROWS = 48
RIM_TAPS = (0, 1, 2, 3, 6)


def strip_cells(edge, depth):
    if edge == 0:
        return [depth * S + i for i in range(S)]
    if edge == 1:
        return [(S - 1 - depth) * S + i for i in range(S)]
    if edge == 2:
        return [i * S + depth for i in range(S)]
    return [i * S + S - 1 - depth for i in range(S)]


def cell_row(row, col):
    return (row % 2 * 2 + col % 2) * PART + row // 2 * HALF + col // 2


def own_at(cell):
    return cell // 2 + X_HALF * (cell % 2)


def near_at(edge, along, depth):
    row = OWN_ROWS + EDGE_ROWS[edge] + 6 * depth
    if along < 0:
        return OWN_ROWS + EDGE_ROWS[edge] + 12 + X_HALF * depth
    if along >= S:
        return OWN_ROWS + EDGE_ROWS[edge] + 13 + X_HALF * depth
    return row + along // 2 + X_HALF * (along % 2)


def window_index():
    fixed = np.zeros((9, PRE_ROWS), np.float32)
    varied = np.zeros((4, 4, 2, 9, PRE_ROWS), np.float32)
    for k in range(9):
        a, b = k // 3, k % 3
        for cell in range(CELLS):
            row, col = cell // S + a, cell % S + b
            inner_row, inner_col = 1 <= row <= S, 1 <= col <= S
            if inner_row and inner_col:
                fixed[k, cell_row(cell // S, cell % S)] = 1 + own_at((row - 1) * S + col - 1)
            elif inner_row or inner_col:
                edge = (2 if col == 0 else 3) if inner_row else (0 if row == 0 else 1)
                at = row - 1 if inner_row else col - 1
                for flip in range(2):
                    varied[edge, :, flip, k, cell_row(cell // S, cell % S)] = 1 + near_at(
                        edge, 11 - at if flip else at, 0
                    )
        for slot, edge in enumerate((0, 2)):
            own = strip_cells(edge, 0)
            for facing in range(4):
                depth = (a - 1, 1 - a, b - 1, 1 - b)[facing]
                shift = (b - 1, b - 1, a - 1, a - 1)[facing]
                for flip in range(2):
                    for j in range(S):
                        along = (11 - j if flip else j) + shift
                        if depth >= 0:
                            at = near_at(edge, along, depth)
                        elif 0 <= along < S:
                            at = own_at(own[11 - along if flip else along])
                        else:
                            continue
                        varied[edge, facing, flip, k, INNER + 16 * slot + j] = 1 + at
    return fixed.reshape(-1), varied.reshape(32, -1)


def rim_index():
    varied = np.zeros((4, 4, 2, len(RIM_TAPS), RIM_ROWS), np.float32)
    for slot, k in enumerate(RIM_TAPS):
        a, b = k // 3, k % 3
        for edge in range(4):
            for flip in range(2):
                for j in range(S):
                    for facing, live, tap in ((0, a == 0, b), (2, b == 0, a)):
                        at = (11 - j if flip else j) + 1 - tap
                        if live and at % 2 == 0 and 0 <= at < S:
                            at //= 2
                            varied[edge, facing, flip, slot, edge * S + j] = (
                                1 + C_OWN + 3 * edge + at // 2 + C_HALF * (at % 2)
                            )
    return np.zeros(len(RIM_TAPS) * RIM_ROWS, np.float32), varied.reshape(32, -1)


def shift_selector():
    chosen = np.zeros((2, 2, PART, 2 * C_HALF), np.float32)
    for down in range(2):
        for right in range(2):
            for row in range(HALF - down):
                for col in range(HALF - right):
                    at = (row + down) * HALF + col + right
                    chosen[down, right, row * HALF + col, at // 2 + C_HALF * (at % 2)] = 1
    return chosen.reshape(INNER, 2 * C_HALF)


def down_selector():
    chosen = np.zeros((9, DOWN_ROWS, PRE_ROWS), np.float32)
    for k in range(9):
        for cell in range(COARSE):
            row, col = 2 * (cell // HALF) + k // 3, 2 * (cell % HALF) + k % 3
            if row == 0 and col == 0:
                continue
            if row == 0:
                at = INNER + col - 1
            elif col == 0:
                at = INNER + 16 + row - 1
            else:
                at = cell_row(row - 1, col - 1)
            chosen[k, cell, at] = 1
    return chosen.reshape(9 * DOWN_ROWS, PRE_ROWS)


def rim_selector():
    chosen = np.zeros((INNER, RIM_ROWS), np.float32)
    for edge in range(4):
        for j, cell in enumerate(strip_cells(edge, 0)):
            chosen[cell_row(cell // S, cell % S), edge * S + j] = 1
    return chosen


def cell_selector():
    chosen = np.zeros((INNER, CELLS), np.float32)
    for cell in range(CELLS):
        chosen[cell_row(cell // S, cell % S), cell] = 1
    return chosen


def order_selector():
    chosen = np.zeros((DOWN_ROWS, 2 * C_HALF), np.float32)
    for cell in range(COARSE):
        chosen[cell, cell // 2 + C_HALF * (cell % 2)] = 1
    return chosen


def dot_nn(left, right):
    return lax.dot_general(left, right, (((1,), (0,)), ((), ())), preferred_element_type=F32)


def dot_nt(left, right):
    return lax.dot_general(left, right, (((1,), (1,)), ((), ())), preferred_element_type=F32)


def pack_selectors(half):
    rows = PACK_ROWS + 4 * UNIT
    row = lax.broadcasted_iota(jnp.int32, (rows, CELLS), 0)
    at = lax.broadcasted_iota(jnp.int32, (rows, CELLS), 1)
    edge, j = (row - PACK_ROWS) >> 4, (row - PACK_ROWS) & 15
    deep = jnp.where(jnp.logical_and(j >= 9, j < 15), 1, 0)
    along = jnp.where(j < 6, 2 * j + half, jnp.where(j < 15, 2 * (j - 9) + half, 11 - half))
    start = jnp.where(edge == 0, S * deep, jnp.where(edge == 1, S * (S - 1 - deep), jnp.where(edge == 2, deep, S - 1 - deep)))
    cell = start + along * jnp.where(edge < 2, 1, S)
    cell = jnp.where(jnp.logical_or(j < 6, j >= 9), cell, -1)
    cell = jnp.where(row < OWN_ROWS, 2 * row + half, jnp.where(row < PACK_ROWS, -1, cell))
    fields = jnp.where(at == cell, 1.0, 0.0).astype(BF)
    row, at, edge, j = row[:, :COARSE], at[:, :COARSE], edge[:, :COARSE], j[:, :COARSE]
    cell = (2 * (j - 6) + half) * jnp.where(edge == 0, 1, HALF)
    live = jnp.logical_and(jnp.logical_and(j >= 6, j < 9), jnp.logical_or(edge == 0, edge == 2))
    cell = jnp.where(live, cell, -1)
    own = jnp.where(row < OWN_ROWS + C_OWN, 2 * (row - OWN_ROWS) + half, -1)
    cell = jnp.where(row < PACK_ROWS, own, cell)
    return fields, jnp.where(at == cell, 1.0, 0.0).astype(BF)


def pack_kernel(me_ref, fields_hbm, cot_hbm, first_ref, down_ref, own_ref, unit_ref, half_ref, fields_ref, cot_ref, sems):
    loads = [
        pltpu.make_async_copy(fields_hbm, fields_ref, sems.at[0]),
        pltpu.make_async_copy(cot_hbm, cot_ref, sems.at[1]),
    ]
    for load in loads:
        load.start()

    @pl.when(me_ref[3] == 0)
    def _():
        pltpu.make_async_copy(first_ref, half_ref, sems.at[2]).start()

    @pl.when(me_ref[3] == 1)
    def _():
        pltpu.make_async_copy(down_ref, half_ref, sems.at[2]).start()

    chosen = [pack_selectors(h) for h in range(2)]
    for load in loads:
        load.wait()
    for t in range(TILES_HERE):
        halves = [(dot_nt(f, fields_ref[t]) + dot_nn(c, cot_ref[t])).astype(BF) for f, c in chosen]
        for h in range(2):
            own_ref[t, :, h * CH : (h + 1) * CH] = halves[h][:PACK_ROWS]
            for copy in range(YX):
                unit_ref[copy, t * 4 * UNIT : (t + 1) * 4 * UNIT, h * CH : (h + 1) * CH] = halves[h][PACK_ROWS:]
    pltpu.make_async_copy(first_ref, half_ref, sems.at[2]).wait()


def edge_words(seam_table):
    n, f, r = seam_table[:, :, 0], seam_table[:, :, 1], seam_table[:, :, 2]
    device = n // TILES_HERE
    group = (device % CORE) * YX + device // (NZ * CORE)
    unit = (group * TILES_HERE + n % TILES_HERE) * 4 + f
    z = (device // CORE) % NZ
    word = unit + r * 256 + z * 512
    beyond = (n * 4 + jnp.where(f < 2, 2, 0)) * 2 + f % 2
    return word.reshape(-1), beyond.reshape(-1)


def place_kernel(word_ref, beyond_ref, me_ref, unit_ref, out_ref, sent):
    ylo, x, z, core = me_ref[0], me_ref[1], me_ref[2], me_ref[3]

    def unit_at(word):
        keep = jnp.where((word >> 9) == z, 1.0, 0.0).astype(F32)
        at = pl.multiple_of((word & 255) * UNIT, UNIT)
        return unit_ref[pl.ds(at, UNIT), :].astype(F32) * keep

    def body(z_to, carry):
        device = ((ylo * NX + x) * NZ + z_to) * CORE + core
        for t in range(TILES_HERE):
            for edge in range(4):
                at = (device * TILES_HERE + t) * 4 + edge
                unit = unit_at(word_ref[at])
                row = t * BLOCK_ROWS + EDGE_ROWS[edge]
                cot = t * BLOCK_ROWS + FIELD_ROWS + 3 * edge
                sent[z_to, row : row + 6, :] = unit[0:6]
                sent[z_to, cot : cot + 3, :] = unit[6:9]
                if edge % 2 == 0:
                    sent[z_to, row + 6 : row + 12, :] = unit[9:15]
                    beyond = beyond_ref[at]
                    for last in range(2):
                        word = word_ref[(beyond >> 1) + last]
                        end = unit_at(word)
                        low = ((beyond + (word >> 8)) & 1) == 0
                        sent[z_to, row + 12 + last : row + 13 + last, :] = jnp.where(low, end[0:1], end[15:16])
        sent[z_to, TILES_HERE * BLOCK_ROWS :, :] = jnp.zeros((SEND_ROWS - TILES_HERE * BLOCK_ROWS, 128), F32)
        return carry

    lax.fori_loop(0, NZ, body, 0)
    out_ref[...] = sent[...].astype(BF)


def join_kernel(got_ref, own_ref, out_ref, rows):
    total = got_ref[0].astype(F32)
    for q in range(1, NZ):
        total = total + got_ref[q].astype(F32)
    for t in range(TILES_HERE):
        base, block = t * PAY_ROWS, t * BLOCK_ROWS
        own = own_ref[t].astype(F32)
        rows[base : base + OWN_ROWS, :] = own[:OWN_ROWS]
        rows[base + OWN_ROWS : base + X_HALF, :] = total[block : block + FIELD_ROWS]
        rows[base + X_HALF : base + X_HALF + C_OWN, :] = own[OWN_ROWS : OWN_ROWS + C_OWN]
        rows[base + X_HALF + C_OWN : base + PAY_ROWS - 2, :] = total[block + FIELD_ROWS : block + BLOCK_ROWS]
        rows[base + PAY_ROWS - 2 : base + PAY_ROWS, :] = jnp.zeros((2, 128), F32)
    whole = rows[...].astype(BF)
    for c in range(CHAN):
        out_ref[c] = whole


def main_kernel(
    me_ref, pay_ref, window_ref, rim_at_ref, shift_ref, down_ref, rim_ref, order_ref, cell_ref, weights_ref,
    coarse_ref, gp_ref, grads_ref, xs, cs, wf, wd, wins, ups, rims, downs, sems,
):
    copies = []
    for c in range(CHAN):
        for which, held in enumerate((wf, wd)):
            copies.append(
                pltpu.make_async_copy(
                    weights_ref.at[2 * c + which], held.at[:, pl.ds(c * CH, CH), :], sems.at[2 * c + which]
                )
            )
    for copy in copies:
        copy.start()
    chan = me_ref[4]
    pick = jnp.where(
        lax.broadcasted_iota(jnp.int32, (CH, C), 1) == lax.broadcasted_iota(jnp.int32, (CH, C), 0) + chan * CH, 1.0, 0.0
    ).astype(BF)
    for c in range(CHAN):
        for t in range(TILES_HERE):
            base = t * PAY_ROWS
            for h in range(2):
                lanes = slice(h * CH, (h + 1) * CH)
                xs[t, h * X_HALF : (h + 1) * X_HALF, c * CH : (c + 1) * CH] = pay_ref[c, base : base + X_HALF, lanes]
                cs[t, h * C_HALF : (h + 1) * C_HALF, c * CH : (c + 1) * CH] = pay_ref[
                    c, base + X_HALF : base + PAY_ROWS, lanes
                ]
    for t in range(TILES_HERE):
        xs[t, 2 * X_HALF :, :] = jnp.zeros((C - 2 * X_HALF, C), BF)
    for t in range(TILES_HERE):
        for k in range(9):
            wins[t * PRE_ROWS : (t + 1) * PRE_ROWS, k * C : (k + 1) * C] = dot_nn(
                window_ref[t, k * PRE_ROWS : (k + 1) * PRE_ROWS, :], xs[t]
            ).astype(BF)
        shifted = dot_nn(shift_ref[...], cs[t])
        for s in range(4):
            ups[s, t * PART : (t + 1) * PART, :] = shifted[s * PART : (s + 1) * PART]
        near = dot_nn(rim_at_ref[t], cs[t]).astype(BF)
        for s in range(len(RIM_TAPS)):
            rims[s, t * RIM_ROWS : (t + 1) * RIM_ROWS, :] = near[s * RIM_ROWS : (s + 1) * RIM_ROWS]
    for copy in copies:
        copy.wait()
    pre = dot_nn(wins[...], wf[...].reshape(9 * C, C))
    ups_low = [ups[s].astype(BF) for s in range(4)]
    blocks = (
        dot_nt(ups_low[0], wd[4]),
        dot_nt(ups_low[1], wd[3]) + dot_nt(ups_low[0], wd[5]),
        dot_nt(ups_low[2], wd[1]) + dot_nt(ups_low[0], wd[7]),
        dot_nt(ups_low[3], wd[0]) + dot_nt(ups_low[2], wd[2]) + dot_nt(ups_low[1], wd[6]) + dot_nt(ups_low[0], wd[8]),
    )
    rim = dot_nt(rims[0], wd[RIM_TAPS[0]])
    for s in range(1, len(RIM_TAPS)):
        rim = rim + dot_nt(rims[s], wd[RIM_TAPS[s]])
    rim = rim.astype(BF)
    scale = np.float32(np.sqrt(2 / np.pi))
    squared = pre * pre
    bent = jnp.tanh(scale * (pre + np.float32(0.044715) * squared * pre))
    gate = 0.5 * (1.0 + bent)
    hidden = (pre * gate).astype(BF)
    slope = gate + 0.5 * pre * (1.0 - bent * bent) * scale * (1.0 + np.float32(3 * 0.044715) * squared)

    first_sum = None
    down_sum = None
    for t in range(TILES_HERE):
        own_hidden = hidden[t * PRE_ROWS : (t + 1) * PRE_ROWS]
        windows = dot_nn(down_ref[...], own_hidden).astype(BF)
        for k in range(9):
            downs[t * DOWN_ROWS : (t + 1) * DOWN_ROWS, k * C : (k + 1) * C] = windows[k * DOWN_ROWS : (k + 1) * DOWN_ROWS]

        grad_hidden = jnp.concatenate([block[t * PART : (t + 1) * PART] for block in blocks], axis=0)
        grad_hidden = grad_hidden + dot_nn(rim_ref[...], rim[t * RIM_ROWS : (t + 1) * RIM_ROWS])
        grad_pre = (grad_hidden * slope[t * PRE_ROWS : t * PRE_ROWS + INNER]).astype(BF)
        gp_ref[t] = dot_nn(dot_nt(pick, grad_pre).astype(BF), cell_ref[...]).astype(BF)

        x_own = dot_nt(pick, xs[t]).astype(BF)
        h_own = dot_nt(pick, own_hidden).astype(BF)
        up = dot_nn(order_ref[...], cs[t]).astype(BF)
        first_parts, down_parts = [], []
        for k in range(9):
            first_parts.append(
                dot_nt(x_own, window_ref[t, k * PRE_ROWS : k * PRE_ROWS + INNER, :]).astype(BF)
            )
            down_parts.append(
                dot_nt(h_own, down_ref[k * DOWN_ROWS : (k + 1) * DOWN_ROWS, :]).astype(BF)
            )
        part = dot_nn(jnp.concatenate(first_parts, axis=0), grad_pre)
        first_sum = part if first_sum is None else first_sum + part
        part = dot_nn(jnp.concatenate(down_parts, axis=0), up)
        down_sum = part if down_sum is None else down_sum + part
    coarse = dot_nt(dot_nn(downs[...], wd[...].reshape(9 * C, C)).astype(BF), pick).astype(BF)
    for t in range(TILES_HERE):
        coarse_ref[t] = coarse[t * DOWN_ROWS : t * DOWN_ROWS + COARSE]
    for h in range(CORE):
        grads_ref[h, : 9 * CH, :] = first_sum[:, h * 128 : (h + 1) * 128].astype(BF)
        grads_ref[h, 9 * CH :, :] = down_sum[:, h * 128 : (h + 1) * 128].astype(BF)


def vmem(count):
    return [pl.BlockSpec(memory_space=pltpu.VMEM)] * count


def hbm(count):
    return [pl.BlockSpec(memory_space=pltpu.HBM)] * count


def smem(count):
    return [pl.BlockSpec(memory_space=pltpu.SMEM)] * count


LIMIT = pltpu.CompilerParams(vmem_limit_bytes=48 * 1024 * 1024)


def tiles_call(me, payload, window, rim_at, weights):
    constants = (shift_selector(), down_selector(), rim_selector(), order_selector(), cell_selector())
    return pl.pallas_call(
        main_kernel,
        out_shape=(
            jax.ShapeDtypeStruct((TILES_HERE, COARSE, CH), BF),
            jax.ShapeDtypeStruct((TILES_HERE, CH, CELLS), BF),
            jax.ShapeDtypeStruct((CORE, 18 * CH, 128), BF),
        ),
        in_specs=smem(1) + vmem(8) + hbm(1),
        out_specs=tuple(vmem(3)),
        scratch_shapes=[
            pltpu.VMEM((TILES_HERE, C, C), BF),
            pltpu.VMEM((TILES_HERE, 2 * C_HALF, C), BF),
            pltpu.VMEM((9, C, C), BF),
            pltpu.VMEM((9, C, C), BF),
            pltpu.VMEM((TILES_HERE * PRE_ROWS, 9 * C), BF),
            pltpu.VMEM((4, TILES_HERE * PART, C), F32),
            pltpu.VMEM((len(RIM_TAPS), TILES_HERE * RIM_ROWS, C), BF),
            pltpu.VMEM((TILES_HERE * DOWN_ROWS, 9 * C), BF),
            pltpu.SemaphoreType.DMA((2 * CHAN,)),
        ],
        compiler_params=LIMIT,
        name="tiles",
    )(me, payload, window, rim_at, *(jnp.asarray(array, BF) for array in constants), weights)


def shards(fields, seam_table, w_first, w_down, cotangent):
    coords = [lax.axis_index(axis) for axis in ("ylo", "x", "z", "core", "chan")]
    me = jnp.stack(coords).astype(jnp.int32)
    own, units, half = pl.pallas_call(
        pack_kernel,
        out_shape=(
            jax.ShapeDtypeStruct((TILES_HERE, PACK_ROWS, 128), BF),
            jax.ShapeDtypeStruct((YX, TILES_HERE * 4 * UNIT, 128), BF),
            jax.ShapeDtypeStruct(w_first.shape, BF),
        ),
        in_specs=smem(1) + hbm(4),
        out_specs=tuple(vmem(2) + hbm(1)),
        scratch_shapes=[
            pltpu.VMEM((TILES_HERE, CH, CELLS), BF),
            pltpu.VMEM((TILES_HERE, COARSE, CH), BF),
            pltpu.SemaphoreType.DMA((3,)),
        ],
        compiler_params=LIMIT,
        name="pack",
    )(me, fields, jnp.swapaxes(cotangent, 1, 2), w_first, w_down)
    weights = lax.all_gather(half, ("chan", "core"), axis=0, tiled=False)
    units = lax.all_to_all(units, ("ylo", "x"), 0, 0).reshape(-1, 128)
    units = lax.all_gather(units, "core", axis=0, tiled=True)
    words, beyond = edge_words(seam_table)
    sends = pl.pallas_call(
        place_kernel,
        out_shape=jax.ShapeDtypeStruct((NZ, SEND_ROWS, 128), BF),
        in_specs=smem(3) + vmem(1),
        out_specs=vmem(1)[0],
        scratch_shapes=[pltpu.VMEM((NZ, SEND_ROWS, 128), F32)],
        compiler_params=LIMIT,
        name="place",
    )(words, beyond, me, units)
    got = lax.all_to_all(sends, "z", 0, 0)
    joined = pl.pallas_call(
        join_kernel,
        out_shape=jax.ShapeDtypeStruct((CHAN, TILES_HERE * PAY_ROWS, 128), BF),
        in_specs=vmem(2),
        out_specs=vmem(1)[0],
        scratch_shapes=[pltpu.VMEM((TILES_HERE * PAY_ROWS, 128), F32)],
        compiler_params=LIMIT,
        name="join",
    )(got, own)
    payload = lax.all_to_all(joined, "chan", 0, 0)

    tile_at = ((coords[0] * NX + coords[1]) * NZ + coords[2]) * CORE + coords[3]
    own_table = lax.dynamic_slice_in_dim(seam_table, tile_at * TILES_HERE, TILES_HERE, 0)
    code = own_table[:, :, 1] * 2 + own_table[:, :, 2]
    chosen = (code[:, :, None] == jnp.arange(8, dtype=jnp.int32)).astype(BF).reshape(TILES_HERE, 32)
    one_hots = []
    for (fixed, varied), depth in ((window_index(), C), (rim_index(), 2 * C_HALF)):
        at = jnp.dot(chosen, jnp.asarray(varied, BF), preferred_element_type=F32) + jnp.asarray(fixed, F32)
        one_hots.append((at[:, :, None] == jnp.arange(1, depth + 1, dtype=jnp.int32).astype(F32)).astype(BF))

    coarse, grad_pre, grads = tiles_call(me, payload, one_hots[0], one_hots[1], weights)

    part = lax.all_to_all(grads, "core", 0, 0)
    part = (part[0].astype(F32) + part[1].astype(F32)).astype(BF).reshape(NX * NZ, 36, 128)
    part = lax.all_to_all(part, ("x", "z"), 0, 0)
    part = part.astype(F32).sum(0).astype(BF)
    part = lax.all_gather(part, "ylo", axis=0, tiled=False)
    part = (part[0].astype(F32) + part[1].astype(F32)).astype(BF)
    part = lax.all_to_all(jnp.broadcast_to(part[None], (NX * NZ, 36, 128)), ("x", "z"), 0, 0)
    whole = lax.all_gather(part.reshape(18 * CH, 128), "core", axis=0, tiled=False)
    whole = jnp.concatenate([whole[0], whole[1]], axis=1).astype(F32).reshape(2, 9, CH, C)
    tiles = TILES_HERE * PLANE * CORE
    return (
        jnp.swapaxes(coarse, 1, 2),
        whole[0] * float(tiles * CELLS) ** (-0.5),
        whole[1] * float(tiles * COARSE) ** (-0.5),
        grad_pre,
    )


def solution(mesh):
    fine = Mesh(mesh.devices.reshape(YLO, NX, NZ, CORE, CHAN), ("ylo", "x", "z", "core", "chan"))
    return jax.shard_map(
        shards,
        mesh=fine,
        in_specs=(
            P(TILE_AXES, "chan", None),
            P(),
            P(None, "chan", None),
            P(None, "chan", None),
            P(TILE_AXES, "chan", None),
        ),
        out_specs=(
            P(TILE_AXES, "chan", None),
            P(None, "chan", None),
            P(None, "chan", None),
            P(TILE_AXES, "chan", None),
        ),
        check_vma=False,
    )
```

```python
import numpy as np
import jax
import jax.numpy as jnp
from jax import lax
from jax.experimental import pallas as pl
from jax.experimental.pallas import tpu as pltpu
from jax.sharding import Mesh, PartitionSpec as P

S = 12
HALF = 6
CELLS = 144
COARSE = 36
TILES_HERE = 3
CH = 64
C = 256
YLO, NX, NZ, CORE, CHAN = 2, 4, 8, 2, 4
YX = YLO * NX
NEAR = YX * CORE
PLANE = YX * NZ
TILE_AXES = ("ylo", "x", "z", "core")
BF = jnp.bfloat16
F32 = jnp.float32

EDGE_ROWS = (0, 28, 14, 34)
FIELD_ROWS = 40
BLOCK_ROWS = 52
SEND_ROWS = 160
OWN_ROWS = 72
X_HALF = OWN_ROWS + FIELD_ROWS
C_OWN = 18
C_HALF = 32
PAY_ROWS = X_HALF + C_HALF
PACK_ROWS = 96
UNIT = 16
PART = 40
INNER = 4 * PART
PRE_ROWS = INNER + 32
DOWN_ROWS = 48
RIM_ROWS = 48
RIM_TAPS = (0, 1, 2, 3, 6)


def strip_cells(edge, depth):
    if edge == 0:
        return [depth * S + i for i in range(S)]
    if edge == 1:
        return [(S - 1 - depth) * S + i for i in range(S)]
    if edge == 2:
        return [i * S + depth for i in range(S)]
    return [i * S + S - 1 - depth for i in range(S)]


def cell_row(row, col):
    return (row % 2 * 2 + col % 2) * PART + row // 2 * HALF + col // 2


def own_at(cell):
    return cell // 2 + X_HALF * (cell % 2)


def near_at(edge, along, depth):
    row = OWN_ROWS + EDGE_ROWS[edge] + 6 * depth
    if along < 0:
        return OWN_ROWS + EDGE_ROWS[edge] + 12 + X_HALF * depth
    if along >= S:
        return OWN_ROWS + EDGE_ROWS[edge] + 13 + X_HALF * depth
    return row + along // 2 + X_HALF * (along % 2)


def window_index():
    fixed = np.zeros((9, PRE_ROWS), np.float32)
    varied = np.zeros((4, 4, 2, 9, PRE_ROWS), np.float32)
    for k in range(9):
        a, b = k // 3, k % 3
        for cell in range(CELLS):
            row, col = cell // S + a, cell % S + b
            inner_row, inner_col = 1 <= row <= S, 1 <= col <= S
            if inner_row and inner_col:
                fixed[k, cell_row(cell // S, cell % S)] = 1 + own_at((row - 1) * S + col - 1)
            elif inner_row or inner_col:
                edge = (2 if col == 0 else 3) if inner_row else (0 if row == 0 else 1)
                at = row - 1 if inner_row else col - 1
                for flip in range(2):
                    varied[edge, :, flip, k, cell_row(cell // S, cell % S)] = 1 + near_at(
                        edge, 11 - at if flip else at, 0
                    )
        for slot, edge in enumerate((0, 2)):
            own = strip_cells(edge, 0)
            for facing in range(4):
                depth = (a - 1, 1 - a, b - 1, 1 - b)[facing]
                shift = (b - 1, b - 1, a - 1, a - 1)[facing]
                for flip in range(2):
                    for j in range(S):
                        along = (11 - j if flip else j) + shift
                        if depth >= 0:
                            at = near_at(edge, along, depth)
                        elif 0 <= along < S:
                            at = own_at(own[11 - along if flip else along])
                        else:
                            continue
                        varied[edge, facing, flip, k, INNER + 16 * slot + j] = 1 + at
    return fixed.reshape(-1), varied.reshape(32, -1)


def rim_index():
    varied = np.zeros((4, 4, 2, len(RIM_TAPS), RIM_ROWS), np.float32)
    for slot, k in enumerate(RIM_TAPS):
        a, b = k // 3, k % 3
        for edge in range(4):
            for flip in range(2):
                for j in range(S):
                    for facing, live, tap in ((0, a == 0, b), (2, b == 0, a)):
                        at = (11 - j if flip else j) + 1 - tap
                        if live and at % 2 == 0 and 0 <= at < S:
                            at //= 2
                            varied[edge, facing, flip, slot, edge * S + j] = (
                                1 + C_OWN + 3 * edge + at // 2 + C_HALF * (at % 2)
                            )
    return np.zeros(len(RIM_TAPS) * RIM_ROWS, np.float32), varied.reshape(32, -1)


def shift_selector():
    chosen = np.zeros((2, 2, PART, 2 * C_HALF), np.float32)
    for down in range(2):
        for right in range(2):
            for row in range(HALF - down):
                for col in range(HALF - right):
                    at = (row + down) * HALF + col + right
                    chosen[down, right, row * HALF + col, at // 2 + C_HALF * (at % 2)] = 1
    return chosen.reshape(INNER, 2 * C_HALF)


def down_selector():
    chosen = np.zeros((9, DOWN_ROWS, PRE_ROWS), np.float32)
    for k in range(9):
        for cell in range(COARSE):
            row, col = 2 * (cell // HALF) + k // 3, 2 * (cell % HALF) + k % 3
            if row == 0 and col == 0:
                continue
            if row == 0:
                at = INNER + col - 1
            elif col == 0:
                at = INNER + 16 + row - 1
            else:
                at = cell_row(row - 1, col - 1)
            chosen[k, cell, at] = 1
    return chosen.reshape(9 * DOWN_ROWS, PRE_ROWS)


def rim_selector():
    chosen = np.zeros((INNER, RIM_ROWS), np.float32)
    for edge in range(4):
        for j, cell in enumerate(strip_cells(edge, 0)):
            chosen[cell_row(cell // S, cell % S), edge * S + j] = 1
    return chosen


def cell_selector():
    chosen = np.zeros((INNER, CELLS), np.float32)
    for cell in range(CELLS):
        chosen[cell_row(cell // S, cell % S), cell] = 1
    return chosen


def order_selector():
    chosen = np.zeros((DOWN_ROWS, 2 * C_HALF), np.float32)
    for cell in range(COARSE):
        chosen[cell, cell // 2 + C_HALF * (cell % 2)] = 1
    return chosen


def dot_nn(left, right):
    return lax.dot_general(left, right, (((1,), (0,)), ((), ())), preferred_element_type=F32)


def dot_nt(left, right):
    return lax.dot_general(left, right, (((1,), (1,)), ((), ())), preferred_element_type=F32)


def pack_selectors(half):
    rows = PACK_ROWS + 4 * UNIT
    row = lax.broadcasted_iota(jnp.int32, (rows, CELLS), 0)
    at = lax.broadcasted_iota(jnp.int32, (rows, CELLS), 1)
    edge, j = (row - PACK_ROWS) >> 4, (row - PACK_ROWS) & 15
    deep = jnp.where(jnp.logical_and(j >= 9, j < 15), 1, 0)
    along = jnp.where(j < 6, 2 * j + half, jnp.where(j < 15, 2 * (j - 9) + half, 11 - half))
    start = jnp.where(edge == 0, S * deep, jnp.where(edge == 1, S * (S - 1 - deep), jnp.where(edge == 2, deep, S - 1 - deep)))
    cell = start + along * jnp.where(edge < 2, 1, S)
    cell = jnp.where(jnp.logical_or(j < 6, j >= 9), cell, -1)
    cell = jnp.where(row < OWN_ROWS, 2 * row + half, jnp.where(row < PACK_ROWS, -1, cell))
    fields = jnp.where(at == cell, 1.0, 0.0).astype(BF)
    row, at, edge, j = row[:, :COARSE], at[:, :COARSE], edge[:, :COARSE], j[:, :COARSE]
    cell = (2 * (j - 6) + half) * jnp.where(edge == 0, 1, HALF)
    live = jnp.logical_and(jnp.logical_and(j >= 6, j < 9), jnp.logical_or(edge == 0, edge == 2))
    cell = jnp.where(live, cell, -1)
    own = jnp.where(row < OWN_ROWS + C_OWN, 2 * (row - OWN_ROWS) + half, -1)
    cell = jnp.where(row < PACK_ROWS, own, cell)
    return fields, jnp.where(at == cell, 1.0, 0.0).astype(BF)


def pack_kernel(me_ref, fields_hbm, cot_hbm, first_ref, down_ref, own_ref, unit_ref, half_ref, fields_ref, cot_ref, held, sems):
    loads = [
        pltpu.make_async_copy(fields_hbm, fields_ref, sems.at[0]),
        pltpu.make_async_copy(cot_hbm, cot_ref, sems.at[1]),
    ]
    for load in loads:
        load.start()

    @pl.when(me_ref[3] == 0)
    def _():
        pltpu.make_async_copy(first_ref, held, sems.at[2]).start()

    @pl.when(me_ref[3] == 1)
    def _():
        pltpu.make_async_copy(down_ref, held, sems.at[2]).start()

    chosen = [pack_selectors(h) for h in range(2)]
    pltpu.make_async_copy(first_ref, held, sems.at[2]).wait()
    store = pltpu.make_async_copy(held, half_ref, sems.at[3])
    store.start()
    for load in loads:
        load.wait()
    for t in range(TILES_HERE):
        halves = [(dot_nt(f, fields_ref[t]) + dot_nn(c, cot_ref[t])).astype(BF) for f, c in chosen]
        for h in range(2):
            own_ref[t, :, h * CH : (h + 1) * CH] = halves[h][:PACK_ROWS]
            for copy in range(YX):
                unit_ref[copy, t * 4 * UNIT : (t + 1) * 4 * UNIT, h * CH : (h + 1) * CH] = halves[h][PACK_ROWS:]
    store.wait()


def edge_words(seam_table):
    n, f, r = seam_table[:, :, 0], seam_table[:, :, 1], seam_table[:, :, 2]
    device = n // TILES_HERE
    group = (device % CORE) * YX + device // (NZ * CORE)
    unit = (group * TILES_HERE + n % TILES_HERE) * 4 + f
    z = (device // CORE) % NZ
    word = unit + r * 256 + z * 512
    beyond = (n * 4 + jnp.where(f < 2, 2, 0)) * 2 + f % 2
    return word.reshape(-1), beyond.reshape(-1)


def place_kernel(word_ref, beyond_ref, me_ref, unit_ref, out_ref, sent):
    ylo, x, z, core = me_ref[0], me_ref[1], me_ref[2], me_ref[3]

    def unit_at(word):
        keep = jnp.where((word >> 9) == z, 1.0, 0.0).astype(F32)
        at = pl.multiple_of((word & 255) * UNIT, UNIT)
        return unit_ref[pl.ds(at, UNIT), :].astype(F32) * keep

    def body(z_to, carry):
        device = ((ylo * NX + x) * NZ + z_to) * CORE + core
        for t in range(TILES_HERE):
            for edge in range(4):
                at = (device * TILES_HERE + t) * 4 + edge
                unit = unit_at(word_ref[at])
                row = t * BLOCK_ROWS + EDGE_ROWS[edge]
                cot = t * BLOCK_ROWS + FIELD_ROWS + 3 * edge
                sent[z_to, row : row + 6, :] = unit[0:6]
                sent[z_to, cot : cot + 3, :] = unit[6:9]
                if edge % 2 == 0:
                    sent[z_to, row + 6 : row + 12, :] = unit[9:15]
                    beyond = beyond_ref[at]
                    for last in range(2):
                        word = word_ref[(beyond >> 1) + last]
                        end = unit_at(word)
                        low = ((beyond + (word >> 8)) & 1) == 0
                        sent[z_to, row + 12 + last : row + 13 + last, :] = jnp.where(low, end[0:1], end[15:16])
        sent[z_to, TILES_HERE * BLOCK_ROWS :, :] = jnp.zeros((SEND_ROWS - TILES_HERE * BLOCK_ROWS, 128), F32)
        return carry

    lax.fori_loop(0, NZ, body, 0)
    out_ref[...] = sent[...].astype(BF)


def join_kernel(got_ref, own_ref, out_ref, rows):
    total = got_ref[0].astype(F32)
    for q in range(1, NZ):
        total = total + got_ref[q].astype(F32)
    for t in range(TILES_HERE):
        base, block = t * PAY_ROWS, t * BLOCK_ROWS
        own = own_ref[t].astype(F32)
        rows[base : base + OWN_ROWS, :] = own[:OWN_ROWS]
        rows[base + OWN_ROWS : base + X_HALF, :] = total[block : block + FIELD_ROWS]
        rows[base + X_HALF : base + X_HALF + C_OWN, :] = own[OWN_ROWS : OWN_ROWS + C_OWN]
        rows[base + X_HALF + C_OWN : base + PAY_ROWS - 2, :] = total[block + FIELD_ROWS : block + BLOCK_ROWS]
        rows[base + PAY_ROWS - 2 : base + PAY_ROWS, :] = jnp.zeros((2, 128), F32)
    whole = rows[...].astype(BF)
    for c in range(CHAN):
        out_ref[c] = whole


def main_kernel(
    me_ref, pay_ref, rim_at_ref, shift_ref, down_ref, rim_ref, order_ref, cell_ref, window_hbm, weights_ref,
    coarse_ref, gp_ref, grads_ref, window_ref, xs, cs, wf, wd, wins, ups, rims, downs, sems,
):
    window_copies = [
        pltpu.make_async_copy(window_hbm.at[t], window_ref.at[t], sems.at[2 * CHAN + t]) for t in range(TILES_HERE)
    ]
    for copy in window_copies:
        copy.start()
    copies = []
    for c in range(CHAN):
        for which, held in enumerate((wf, wd)):
            copies.append(
                pltpu.make_async_copy(
                    weights_ref.at[2 * c + which], held.at[:, pl.ds(c * CH, CH), :], sems.at[2 * c + which]
                )
            )
    for copy in copies:
        copy.start()
    chan = me_ref[4]
    pick = jnp.where(
        lax.broadcasted_iota(jnp.int32, (CH, C), 1) == lax.broadcasted_iota(jnp.int32, (CH, C), 0) + chan * CH, 1.0, 0.0
    ).astype(BF)
    for c in range(CHAN):
        for t in range(TILES_HERE):
            base = t * PAY_ROWS
            for h in range(2):
                lanes = slice(h * CH, (h + 1) * CH)
                xs[t, h * X_HALF : (h + 1) * X_HALF, c * CH : (c + 1) * CH] = pay_ref[c, base : base + X_HALF, lanes]
                cs[t, h * C_HALF : (h + 1) * C_HALF, c * CH : (c + 1) * CH] = pay_ref[
                    c, base + X_HALF : base + PAY_ROWS, lanes
                ]
    for t in range(TILES_HERE):
        xs[t, 2 * X_HALF :, :] = jnp.zeros((C - 2 * X_HALF, C), BF)
    for t in range(TILES_HERE):
        window_copies[t].wait()
        for k in range(9):
            wins[t * PRE_ROWS : (t + 1) * PRE_ROWS, k * C : (k + 1) * C] = dot_nn(
                window_ref[t, k * PRE_ROWS : (k + 1) * PRE_ROWS, :], xs[t]
            ).astype(BF)
        shifted = dot_nn(shift_ref[...], cs[t])
        for s in range(4):
            ups[s, t * PART : (t + 1) * PART, :] = shifted[s * PART : (s + 1) * PART]
        near = dot_nn(rim_at_ref[t], cs[t]).astype(BF)
        for s in range(len(RIM_TAPS)):
            rims[s, t * RIM_ROWS : (t + 1) * RIM_ROWS, :] = near[s * RIM_ROWS : (s + 1) * RIM_ROWS]
    for copy in copies:
        copy.wait()
    pre = dot_nn(wins[...], wf[...].reshape(9 * C, C))
    ups_low = [ups[s].astype(BF) for s in range(4)]
    blocks = (
        dot_nt(ups_low[0], wd[4]),
        dot_nt(ups_low[1], wd[3]) + dot_nt(ups_low[0], wd[5]),
        dot_nt(ups_low[2], wd[1]) + dot_nt(ups_low[0], wd[7]),
        dot_nt(ups_low[3], wd[0]) + dot_nt(ups_low[2], wd[2]) + dot_nt(ups_low[1], wd[6]) + dot_nt(ups_low[0], wd[8]),
    )
    rim = dot_nt(rims[0], wd[RIM_TAPS[0]])
    for s in range(1, len(RIM_TAPS)):
        rim = rim + dot_nt(rims[s], wd[RIM_TAPS[s]])
    rim = rim.astype(BF)
    scale = np.float32(np.sqrt(2 / np.pi))
    squared = pre * pre
    bent = jnp.tanh(scale * (pre + np.float32(0.044715) * squared * pre))
    gate = 0.5 * (1.0 + bent)
    hidden = (pre * gate).astype(BF)
    slope = gate + 0.5 * pre * (1.0 - bent * bent) * scale * (1.0 + np.float32(3 * 0.044715) * squared)

    first_sum = None
    down_sum = None
    for t in range(TILES_HERE):
        own_hidden = hidden[t * PRE_ROWS : (t + 1) * PRE_ROWS]
        windows = dot_nn(down_ref[...], own_hidden).astype(BF)
        for k in range(9):
            downs[t * DOWN_ROWS : (t + 1) * DOWN_ROWS, k * C : (k + 1) * C] = windows[k * DOWN_ROWS : (k + 1) * DOWN_ROWS]

        grad_hidden = jnp.concatenate([block[t * PART : (t + 1) * PART] for block in blocks], axis=0)
        grad_hidden = grad_hidden + dot_nn(rim_ref[...], rim[t * RIM_ROWS : (t + 1) * RIM_ROWS])
        grad_pre = (grad_hidden * slope[t * PRE_ROWS : t * PRE_ROWS + INNER]).astype(BF)
        gp_ref[t] = dot_nn(dot_nt(pick, grad_pre).astype(BF), cell_ref[...]).astype(BF)

        x_own = dot_nt(pick, xs[t]).astype(BF)
        h_own = dot_nt(pick, own_hidden).astype(BF)
        up = dot_nn(order_ref[...], cs[t]).astype(BF)
        first_parts, down_parts = [], []
        for k in range(9):
            first_parts.append(
                dot_nt(x_own, window_ref[t, k * PRE_ROWS : k * PRE_ROWS + INNER, :]).astype(BF)
            )
            down_parts.append(
                dot_nt(h_own, down_ref[k * DOWN_ROWS : (k + 1) * DOWN_ROWS, :]).astype(BF)
            )
        part = dot_nn(jnp.concatenate(first_parts, axis=0), grad_pre)
        first_sum = part if first_sum is None else first_sum + part
        part = dot_nn(jnp.concatenate(down_parts, axis=0), up)
        down_sum = part if down_sum is None else down_sum + part
    coarse = dot_nt(dot_nn(downs[...], wd[...].reshape(9 * C, C)).astype(BF), pick).astype(BF)
    for t in range(TILES_HERE):
        coarse_ref[t] = coarse[t * DOWN_ROWS : t * DOWN_ROWS + COARSE]
    for h in range(CORE):
        grads_ref[h, : 9 * CH, :] = first_sum[:, h * 128 : (h + 1) * 128].astype(BF)
        grads_ref[h, 9 * CH :, :] = down_sum[:, h * 128 : (h + 1) * 128].astype(BF)


def vmem(count):
    return [pl.BlockSpec(memory_space=pltpu.VMEM)] * count


def hbm(count):
    return [pl.BlockSpec(memory_space=pltpu.HBM)] * count


def smem(count):
    return [pl.BlockSpec(memory_space=pltpu.SMEM)] * count


LIMIT = pltpu.CompilerParams(vmem_limit_bytes=48 * 1024 * 1024)
WHOLE = pltpu.CompilerParams(vmem_limit_bytes=60 * 1024 * 1024)
MOST = pltpu.CompilerParams(vmem_limit_bytes=52 * 1024 * 1024)


def tiles_call(me, payload, window, rim_at, weights):
    constants = (shift_selector(), down_selector(), rim_selector(), order_selector(), cell_selector())
    return pl.pallas_call(
        main_kernel,
        out_shape=(
            jax.ShapeDtypeStruct((TILES_HERE, COARSE, CH), BF),
            jax.ShapeDtypeStruct((TILES_HERE, CH, CELLS), BF),
            jax.ShapeDtypeStruct((CORE, 18 * CH, 128), BF),
        ),
        in_specs=smem(1) + vmem(7) + hbm(2),
        out_specs=tuple(vmem(3)),
        scratch_shapes=[
            pltpu.VMEM((TILES_HERE, 9 * PRE_ROWS, C), BF),
            pltpu.VMEM((TILES_HERE, C, C), BF),
            pltpu.VMEM((TILES_HERE, 2 * C_HALF, C), BF),
            pltpu.VMEM((9, C, C), BF),
            pltpu.VMEM((9, C, C), BF),
            pltpu.VMEM((TILES_HERE * PRE_ROWS, 9 * C), BF),
            pltpu.VMEM((4, TILES_HERE * PART, C), F32),
            pltpu.VMEM((len(RIM_TAPS), TILES_HERE * RIM_ROWS, C), BF),
            pltpu.VMEM((TILES_HERE * DOWN_ROWS, 9 * C), BF),
            pltpu.SemaphoreType.DMA((2 * CHAN + TILES_HERE,)),
        ],
        compiler_params=MOST,
        name="tiles",
    )(me, payload, rim_at, *(jnp.asarray(array, BF) for array in constants), window, weights)


def shards(fields, seam_table, w_first, w_down, cotangent):
    coords = [lax.axis_index(axis) for axis in ("ylo", "x", "z", "core", "chan")]
    me = jnp.stack(coords).astype(jnp.int32)
    own, units, half = pl.pallas_call(
        pack_kernel,
        out_shape=(
            jax.ShapeDtypeStruct((TILES_HERE, PACK_ROWS, 128), BF),
            jax.ShapeDtypeStruct((YX, TILES_HERE * 4 * UNIT, 128), BF),
            jax.ShapeDtypeStruct(w_first.shape, BF),
        ),
        in_specs=smem(1) + hbm(4),
        out_specs=tuple(vmem(2) + hbm(1)),
        scratch_shapes=[
            pltpu.VMEM((TILES_HERE, CH, CELLS), BF),
            pltpu.VMEM((TILES_HERE, COARSE, CH), BF),
            pltpu.VMEM((9, CH, C), BF),
            pltpu.SemaphoreType.DMA((4,)),
        ],
        compiler_params=WHOLE,
        name="pack",
    )(me, fields, jnp.swapaxes(cotangent, 1, 2), w_first, w_down)
    weights = lax.all_gather(half, ("chan", "core"), axis=0, tiled=False)
    units = lax.all_to_all(units, ("ylo", "x"), 0, 0).reshape(-1, 128)
    units = lax.all_gather(units, "core", axis=0, tiled=True)
    words, beyond = edge_words(seam_table)
    sends = pl.pallas_call(
        place_kernel,
        out_shape=jax.ShapeDtypeStruct((NZ, SEND_ROWS, 128), BF),
        in_specs=smem(3) + vmem(1),
        out_specs=vmem(1)[0],
        scratch_shapes=[pltpu.VMEM((NZ, SEND_ROWS, 128), F32)],
        compiler_params=LIMIT,
        name="place",
    )(words, beyond, me, units)
    got = lax.all_to_all(sends, "z", 0, 0)
    joined = pl.pallas_call(
        join_kernel,
        out_shape=jax.ShapeDtypeStruct((CHAN, TILES_HERE * PAY_ROWS, 128), BF),
        in_specs=vmem(2),
        out_specs=vmem(1)[0],
        scratch_shapes=[pltpu.VMEM((TILES_HERE * PAY_ROWS, 128), F32)],
        compiler_params=LIMIT,
        name="join",
    )(got, own)
    payload = lax.all_to_all(joined, "chan", 0, 0)

    tile_at = ((coords[0] * NX + coords[1]) * NZ + coords[2]) * CORE + coords[3]
    own_table = lax.dynamic_slice_in_dim(seam_table, tile_at * TILES_HERE, TILES_HERE, 0)
    code = own_table[:, :, 1] * 2 + own_table[:, :, 2]
    chosen = (code[:, :, None] == jnp.arange(8, dtype=jnp.int32)).astype(BF).reshape(TILES_HERE, 32)
    one_hots = []
    for (fixed, varied), depth in ((window_index(), C), (rim_index(), 2 * C_HALF)):
        at = jnp.dot(chosen, jnp.asarray(varied, BF), preferred_element_type=F32) + jnp.asarray(fixed, F32)
        one_hots.append((at[:, :, None] == jnp.arange(1, depth + 1, dtype=jnp.int32).astype(F32)).astype(BF))

    coarse, grad_pre, grads = tiles_call(me, payload, one_hots[0], one_hots[1], weights)

    part = lax.all_to_all(grads, "core", 0, 0)
    part = (part[0].astype(F32) + part[1].astype(F32)).astype(BF).reshape(NX * NZ, 36, 128)
    part = lax.all_to_all(part, ("x", "z"), 0, 0)
    part = part.astype(F32).sum(0).astype(BF)
    part = lax.all_gather(part, "ylo", axis=0, tiled=False)
    part = (part[0].astype(F32) + part[1].astype(F32)).astype(BF)
    part = lax.all_to_all(jnp.broadcast_to(part[None], (NX * NZ, 36, 128)), ("x", "z"), 0, 0)
    whole = lax.all_gather(part.reshape(18 * CH, 128), "core", axis=0, tiled=False)
    whole = jnp.concatenate([whole[0], whole[1]], axis=1).astype(F32).reshape(2, 9, CH, C)
    tiles = TILES_HERE * PLANE * CORE
    return (
        jnp.swapaxes(coarse, 1, 2),
        whole[0] * float(tiles * CELLS) ** (-0.5),
        whole[1] * float(tiles * COARSE) ** (-0.5),
        grad_pre,
    )


def solution(mesh):
    fine = Mesh(mesh.devices.reshape(YLO, NX, NZ, CORE, CHAN), ("ylo", "x", "z", "core", "chan"))
    return jax.shard_map(
        shards,
        mesh=fine,
        in_specs=(
            P(TILE_AXES, "chan", None),
            P(),
            P(None, "chan", None),
            P(None, "chan", None),
            P(TILE_AXES, "chan", None),
        ),
        out_specs=(
            P(TILE_AXES, "chan", None),
            P(None, "chan", None),
            P(None, "chan", None),
            P(TILE_AXES, "chan", None),
        ),
        check_vma=False,
    )
```

```python
import numpy as np
import jax
import jax.numpy as jnp
from jax import lax
from jax.experimental import pallas as pl
from jax.experimental.pallas import tpu as pltpu
from jax.sharding import Mesh, PartitionSpec as P

S = 12
HALF = 6
CELLS = 144
COARSE = 36
TILES_HERE = 3
CH = 64
C = 256
YLO, NX, NZ, CORE, CHAN = 2, 4, 8, 2, 4
YX = YLO * NX
NEAR = YX * CORE
PLANE = YX * NZ
TILE_AXES = ("ylo", "x", "z", "core")
BF = jnp.bfloat16
F32 = jnp.float32

EDGE_ROWS = (0, 28, 14, 34)
FIELD_ROWS = 40
BLOCK_ROWS = 52
SEND_ROWS = 160
OWN_ROWS = 72
X_HALF = OWN_ROWS + FIELD_ROWS
C_OWN = 18
C_HALF = 32
PAY_ROWS = X_HALF + C_HALF
PACK_ROWS = 96
UNIT = 16
PART = 40
INNER = 4 * PART
PRE_ROWS = INNER + 32
DOWN_ROWS = 48
RIM_ROWS = 48
RIM_TAPS = (0, 1, 2, 3, 6)


def strip_cells(edge, depth):
    if edge == 0:
        return [depth * S + i for i in range(S)]
    if edge == 1:
        return [(S - 1 - depth) * S + i for i in range(S)]
    if edge == 2:
        return [i * S + depth for i in range(S)]
    return [i * S + S - 1 - depth for i in range(S)]


def cell_row(row, col):
    return (row % 2 * 2 + col % 2) * PART + row // 2 * HALF + col // 2


def own_at(cell):
    return cell // 2 + X_HALF * (cell % 2)


def near_at(edge, along, depth):
    row = OWN_ROWS + EDGE_ROWS[edge] + 6 * depth
    if along < 0:
        return OWN_ROWS + EDGE_ROWS[edge] + 12 + X_HALF * depth
    if along >= S:
        return OWN_ROWS + EDGE_ROWS[edge] + 13 + X_HALF * depth
    return row + along // 2 + X_HALF * (along % 2)


def window_index():
    fixed = np.zeros((9, PRE_ROWS), np.float32)
    varied = np.zeros((4, 4, 2, 9, PRE_ROWS), np.float32)
    for k in range(9):
        a, b = k // 3, k % 3
        for cell in range(CELLS):
            row, col = cell // S + a, cell % S + b
            inner_row, inner_col = 1 <= row <= S, 1 <= col <= S
            if inner_row and inner_col:
                fixed[k, cell_row(cell // S, cell % S)] = 1 + own_at((row - 1) * S + col - 1)
            elif inner_row or inner_col:
                edge = (2 if col == 0 else 3) if inner_row else (0 if row == 0 else 1)
                at = row - 1 if inner_row else col - 1
                for flip in range(2):
                    varied[edge, :, flip, k, cell_row(cell // S, cell % S)] = 1 + near_at(
                        edge, 11 - at if flip else at, 0
                    )
        for slot, edge in enumerate((0, 2)):
            own = strip_cells(edge, 0)
            for facing in range(4):
                depth = (a - 1, 1 - a, b - 1, 1 - b)[facing]
                shift = (b - 1, b - 1, a - 1, a - 1)[facing]
                for flip in range(2):
                    for j in range(S):
                        along = (11 - j if flip else j) + shift
                        if depth >= 0:
                            at = near_at(edge, along, depth)
                        elif 0 <= along < S:
                            at = own_at(own[11 - along if flip else along])
                        else:
                            continue
                        varied[edge, facing, flip, k, INNER + 16 * slot + j] = 1 + at
    return fixed.reshape(-1), varied.reshape(32, -1)


def rim_index():
    varied = np.zeros((4, 4, 2, len(RIM_TAPS), RIM_ROWS), np.float32)
    for slot, k in enumerate(RIM_TAPS):
        a, b = k // 3, k % 3
        for edge in range(4):
            for flip in range(2):
                for j in range(S):
                    for facing, live, tap in ((0, a == 0, b), (2, b == 0, a)):
                        at = (11 - j if flip else j) + 1 - tap
                        if live and at % 2 == 0 and 0 <= at < S:
                            at //= 2
                            varied[edge, facing, flip, slot, edge * S + j] = (
                                1 + C_OWN + 3 * edge + at // 2 + C_HALF * (at % 2)
                            )
    return np.zeros(len(RIM_TAPS) * RIM_ROWS, np.float32), varied.reshape(32, -1)


def shift_selector():
    chosen = np.zeros((2, 2, PART, 2 * C_HALF), np.float32)
    for down in range(2):
        for right in range(2):
            for row in range(HALF - down):
                for col in range(HALF - right):
                    at = (row + down) * HALF + col + right
                    chosen[down, right, row * HALF + col, at // 2 + C_HALF * (at % 2)] = 1
    return chosen.reshape(INNER, 2 * C_HALF)


def down_selector():
    chosen = np.zeros((9, DOWN_ROWS, PRE_ROWS), np.float32)
    for k in range(9):
        for cell in range(COARSE):
            row, col = 2 * (cell // HALF) + k // 3, 2 * (cell % HALF) + k % 3
            if row == 0 and col == 0:
                continue
            if row == 0:
                at = INNER + col - 1
            elif col == 0:
                at = INNER + 16 + row - 1
            else:
                at = cell_row(row - 1, col - 1)
            chosen[k, cell, at] = 1
    return chosen.reshape(9 * DOWN_ROWS, PRE_ROWS)


def rim_selector():
    chosen = np.zeros((INNER, RIM_ROWS), np.float32)
    for edge in range(4):
        for j, cell in enumerate(strip_cells(edge, 0)):
            chosen[cell_row(cell // S, cell % S), edge * S + j] = 1
    return chosen


def cell_selector():
    chosen = np.zeros((INNER, CELLS), np.float32)
    for cell in range(CELLS):
        chosen[cell_row(cell // S, cell % S), cell] = 1
    return chosen


def order_selector():
    chosen = np.zeros((DOWN_ROWS, 2 * C_HALF), np.float32)
    for cell in range(COARSE):
        chosen[cell, cell // 2 + C_HALF * (cell % 2)] = 1
    return chosen


def dot_nn(left, right):
    return lax.dot_general(left, right, (((1,), (0,)), ((), ())), preferred_element_type=F32)


def dot_nt(left, right):
    return lax.dot_general(left, right, (((1,), (1,)), ((), ())), preferred_element_type=F32)


def pack_selectors(half):
    rows = PACK_ROWS + 4 * UNIT
    row = lax.broadcasted_iota(jnp.int32, (rows, CELLS), 0)
    at = lax.broadcasted_iota(jnp.int32, (rows, CELLS), 1)
    edge, j = (row - PACK_ROWS) >> 4, (row - PACK_ROWS) & 15
    deep = jnp.where(jnp.logical_and(j >= 9, j < 15), 1, 0)
    along = jnp.where(j < 6, 2 * j + half, jnp.where(j < 15, 2 * (j - 9) + half, 11 - half))
    start = jnp.where(edge == 0, S * deep, jnp.where(edge == 1, S * (S - 1 - deep), jnp.where(edge == 2, deep, S - 1 - deep)))
    cell = start + along * jnp.where(edge < 2, 1, S)
    cell = jnp.where(jnp.logical_or(j < 6, j >= 9), cell, -1)
    cell = jnp.where(row < OWN_ROWS, 2 * row + half, jnp.where(row < PACK_ROWS, -1, cell))
    fields = jnp.where(at == cell, 1.0, 0.0).astype(BF)
    row, at, edge, j = row[:, :COARSE], at[:, :COARSE], edge[:, :COARSE], j[:, :COARSE]
    cell = (2 * (j - 6) + half) * jnp.where(edge == 0, 1, HALF)
    live = jnp.logical_and(jnp.logical_and(j >= 6, j < 9), jnp.logical_or(edge == 0, edge == 2))
    cell = jnp.where(live, cell, -1)
    own = jnp.where(row < OWN_ROWS + C_OWN, 2 * (row - OWN_ROWS) + half, -1)
    cell = jnp.where(row < PACK_ROWS, own, cell)
    return fields, jnp.where(at == cell, 1.0, 0.0).astype(BF)


def pack_kernel(fields_hbm, cot_hbm, first_ref, down_ref, own_ref, unit_hbm, half_ref, fields_ref, cot_ref, held, unit_ref, sems):
    loads = [
        pltpu.make_async_copy(fields_hbm, fields_ref, sems.at[0]),
        pltpu.make_async_copy(cot_hbm, cot_ref, sems.at[1]),
    ]
    for load in loads:
        load.start()
    core = lax.axis_index("core")

    @pl.when(core == 0)
    def _():
        pltpu.make_async_copy(first_ref, held, sems.at[2]).start()

    @pl.when(core == 1)
    def _():
        pltpu.make_async_copy(down_ref, held, sems.at[2]).start()

    chosen = [pack_selectors(h) for h in range(2)]
    for load in loads:
        load.wait()
    for t in range(TILES_HERE):
        halves = [(dot_nt(f, fields_ref[t]) + dot_nn(c, cot_ref[t])).astype(BF) for f, c in chosen]
        for h in range(2):
            own_ref[t, :, h * CH : (h + 1) * CH] = halves[h][:PACK_ROWS]
            unit_ref[t * 4 * UNIT : (t + 1) * 4 * UNIT, h * CH : (h + 1) * CH] = halves[h][PACK_ROWS:]
    pltpu.make_async_copy(first_ref, held, sems.at[2]).wait()
    stores = [pltpu.make_async_copy(held, half_ref, sems.at[3])]
    for copy in range(YX):
        stores.append(pltpu.make_async_copy(unit_ref, unit_hbm.at[copy], sems.at[4 + copy]))
    for store in stores:
        store.start()
    for store in stores:
        store.wait()


def edge_words(seam_table):
    n, f, r = seam_table[:, :, 0], seam_table[:, :, 1], seam_table[:, :, 2]
    device = n // TILES_HERE
    group = (device % CORE) * YX + device // (NZ * CORE)
    unit = (group * TILES_HERE + n % TILES_HERE) * 4 + f
    z = (device // CORE) % NZ
    word = unit + r * 256 + z * 512
    beyond = (n * 4 + jnp.where(f < 2, 2, 0)) * 2 + f % 2
    return word.reshape(-1), beyond.reshape(-1)


def place_kernel(word_ref, beyond_ref, unit_ref, out_ref, sent):
    ylo, x, z, core = (lax.axis_index(axis) for axis in TILE_AXES)

    def unit_at(word):
        keep = jnp.where((word >> 9) == z, 1.0, 0.0).astype(F32)
        at = pl.multiple_of((word & 255) * UNIT, UNIT)
        return unit_ref[pl.ds(at, UNIT), :].astype(F32) * keep

    def body(z_to, carry):
        device = ((ylo * NX + x) * NZ + z_to) * CORE + core
        for t in range(TILES_HERE):
            for edge in range(4):
                at = (device * TILES_HERE + t) * 4 + edge
                unit = unit_at(word_ref[at])
                row = t * BLOCK_ROWS + EDGE_ROWS[edge]
                cot = t * BLOCK_ROWS + FIELD_ROWS + 3 * edge
                sent[z_to, row : row + 6, :] = unit[0:6]
                sent[z_to, cot : cot + 3, :] = unit[6:9]
                if edge % 2 == 0:
                    sent[z_to, row + 6 : row + 12, :] = unit[9:15]
                    beyond = beyond_ref[at]
                    for last in range(2):
                        word = word_ref[(beyond >> 1) + last]
                        end = unit_at(word)
                        low = ((beyond + (word >> 8)) & 1) == 0
                        sent[z_to, row + 12 + last : row + 13 + last, :] = jnp.where(low, end[0:1], end[15:16])
        sent[z_to, TILES_HERE * BLOCK_ROWS :, :] = jnp.zeros((SEND_ROWS - TILES_HERE * BLOCK_ROWS, 128), F32)
        return carry

    lax.fori_loop(0, NZ, body, 0)
    out_ref[...] = sent[...].astype(BF)


def join_kernel(got_ref, own_ref, out_ref, rows):
    total = got_ref[0].astype(F32)
    for q in range(1, NZ):
        total = total + got_ref[q].astype(F32)
    for t in range(TILES_HERE):
        base, block = t * PAY_ROWS, t * BLOCK_ROWS
        own = own_ref[t].astype(F32)
        rows[base : base + OWN_ROWS, :] = own[:OWN_ROWS]
        rows[base + OWN_ROWS : base + X_HALF, :] = total[block : block + FIELD_ROWS]
        rows[base + X_HALF : base + X_HALF + C_OWN, :] = own[OWN_ROWS : OWN_ROWS + C_OWN]
        rows[base + X_HALF + C_OWN : base + PAY_ROWS - 2, :] = total[block + FIELD_ROWS : block + BLOCK_ROWS]
        rows[base + PAY_ROWS - 2 : base + PAY_ROWS, :] = jnp.zeros((2, 128), F32)
    whole = rows[...].astype(BF)
    for c in range(CHAN):
        out_ref[c] = whole


def main_kernel(
    pay_ref, rim_at_ref, shift_ref, down_ref, rim_ref, order_ref, cell_ref, window_hbm, weights_ref,
    coarse_ref, gp_ref, grads_ref, window_ref, xs, cs, wf, wd, wins, ups, rims, downs, sems,
):
    window_copies = [
        pltpu.make_async_copy(window_hbm.at[t], window_ref.at[t], sems.at[2 * CHAN + t]) for t in range(TILES_HERE)
    ]
    for copy in window_copies:
        copy.start()
    copies = []
    for c in range(CHAN):
        for which, held in enumerate((wf, wd)):
            copies.append(
                pltpu.make_async_copy(
                    weights_ref.at[2 * c + which], held.at[:, pl.ds(c * CH, CH), :], sems.at[2 * c + which]
                )
            )
    for copy in copies:
        copy.start()
    chan = lax.axis_index("chan")
    pick = jnp.where(
        lax.broadcasted_iota(jnp.int32, (CH, C), 1) == lax.broadcasted_iota(jnp.int32, (CH, C), 0) + chan * CH, 1.0, 0.0
    ).astype(BF)
    for c in range(CHAN):
        for t in range(TILES_HERE):
            base = t * PAY_ROWS
            for h in range(2):
                lanes = slice(h * CH, (h + 1) * CH)
                xs[t, h * X_HALF : (h + 1) * X_HALF, c * CH : (c + 1) * CH] = pay_ref[c, base : base + X_HALF, lanes]
                cs[t, h * C_HALF : (h + 1) * C_HALF, c * CH : (c + 1) * CH] = pay_ref[
                    c, base + X_HALF : base + PAY_ROWS, lanes
                ]
    for t in range(TILES_HERE):
        xs[t, 2 * X_HALF :, :] = jnp.zeros((C - 2 * X_HALF, C), BF)
    for t in range(TILES_HERE):
        window_copies[t].wait()
        for k in range(9):
            wins[t * PRE_ROWS : (t + 1) * PRE_ROWS, k * C : (k + 1) * C] = dot_nn(
                window_ref[t, k * PRE_ROWS : (k + 1) * PRE_ROWS, :], xs[t]
            ).astype(BF)
        shifted = dot_nn(shift_ref[...], cs[t])
        for s in range(4):
            ups[s, t * PART : (t + 1) * PART, :] = shifted[s * PART : (s + 1) * PART]
        near = dot_nn(rim_at_ref[t], cs[t]).astype(BF)
        for s in range(len(RIM_TAPS)):
            rims[s, t * RIM_ROWS : (t + 1) * RIM_ROWS, :] = near[s * RIM_ROWS : (s + 1) * RIM_ROWS]
    for copy in copies:
        copy.wait()
    pre = dot_nn(wins[...], wf[...].reshape(9 * C, C))
    ups_low = [ups[s].astype(BF) for s in range(4)]
    blocks = (
        dot_nt(ups_low[0], wd[4]),
        dot_nt(ups_low[1], wd[3]) + dot_nt(ups_low[0], wd[5]),
        dot_nt(ups_low[2], wd[1]) + dot_nt(ups_low[0], wd[7]),
        dot_nt(ups_low[3], wd[0]) + dot_nt(ups_low[2], wd[2]) + dot_nt(ups_low[1], wd[6]) + dot_nt(ups_low[0], wd[8]),
    )
    rim = dot_nt(rims[0], wd[RIM_TAPS[0]])
    for s in range(1, len(RIM_TAPS)):
        rim = rim + dot_nt(rims[s], wd[RIM_TAPS[s]])
    rim = rim.astype(BF)
    scale = np.float32(np.sqrt(2 / np.pi))
    squared = pre * pre
    bent = jnp.tanh(scale * (pre + np.float32(0.044715) * squared * pre))
    gate = 0.5 * (1.0 + bent)
    hidden = (pre * gate).astype(BF)
    slope = gate + 0.5 * pre * (1.0 - bent * bent) * scale * (1.0 + np.float32(3 * 0.044715) * squared)

    first_sum = None
    down_sum = None
    for t in range(TILES_HERE):
        own_hidden = hidden[t * PRE_ROWS : (t + 1) * PRE_ROWS]
        windows = dot_nn(down_ref[...], own_hidden).astype(BF)
        for k in range(9):
            downs[t * DOWN_ROWS : (t + 1) * DOWN_ROWS, k * C : (k + 1) * C] = windows[k * DOWN_ROWS : (k + 1) * DOWN_ROWS]

        grad_hidden = jnp.concatenate([block[t * PART : (t + 1) * PART] for block in blocks], axis=0)
        grad_hidden = grad_hidden + dot_nn(rim_ref[...], rim[t * RIM_ROWS : (t + 1) * RIM_ROWS])
        grad_pre = (grad_hidden * slope[t * PRE_ROWS : t * PRE_ROWS + INNER]).astype(BF)
        gp_ref[t] = dot_nn(dot_nt(pick, grad_pre).astype(BF), cell_ref[...]).astype(BF)

        x_own = dot_nt(pick, xs[t]).astype(BF)
        h_own = dot_nt(pick, own_hidden).astype(BF)
        up = dot_nn(order_ref[...], cs[t]).astype(BF)
        first_parts, down_parts = [], []
        for k in range(9):
            first_parts.append(
                dot_nt(x_own, window_ref[t, k * PRE_ROWS : k * PRE_ROWS + INNER, :]).astype(BF)
            )
            down_parts.append(
                dot_nt(h_own, down_ref[k * DOWN_ROWS : (k + 1) * DOWN_ROWS, :]).astype(BF)
            )
        part = dot_nn(jnp.concatenate(first_parts, axis=0), grad_pre)
        first_sum = part if first_sum is None else first_sum + part
        part = dot_nn(jnp.concatenate(down_parts, axis=0), up)
        down_sum = part if down_sum is None else down_sum + part
    coarse = dot_nt(dot_nn(downs[...], wd[...].reshape(9 * C, C)).astype(BF), pick).astype(BF)
    for t in range(TILES_HERE):
        coarse_ref[t] = coarse[t * DOWN_ROWS : t * DOWN_ROWS + COARSE]
    for h in range(CORE):
        grads_ref[h, : 9 * CH, :] = first_sum[:, h * 128 : (h + 1) * 128].astype(BF)
        grads_ref[h, 9 * CH :, :] = down_sum[:, h * 128 : (h + 1) * 128].astype(BF)


def vmem(count):
    return [pl.BlockSpec(memory_space=pltpu.VMEM)] * count


def hbm(count):
    return [pl.BlockSpec(memory_space=pltpu.HBM)] * count


def smem(count):
    return [pl.BlockSpec(memory_space=pltpu.SMEM)] * count


LIMIT = pltpu.CompilerParams(vmem_limit_bytes=48 * 1024 * 1024)
WHOLE = pltpu.CompilerParams(vmem_limit_bytes=60 * 1024 * 1024)
MOST = pltpu.CompilerParams(vmem_limit_bytes=52 * 1024 * 1024)


def tiles_call(payload, window, rim_at, weights):
    constants = (shift_selector(), down_selector(), rim_selector(), order_selector(), cell_selector())
    return pl.pallas_call(
        main_kernel,
        out_shape=(
            jax.ShapeDtypeStruct((TILES_HERE, COARSE, CH), BF),
            jax.ShapeDtypeStruct((TILES_HERE, CH, CELLS), BF),
            jax.ShapeDtypeStruct((CORE, 18 * CH, 128), BF),
        ),
        in_specs=vmem(7) + hbm(2),
        out_specs=tuple(vmem(3)),
        scratch_shapes=[
            pltpu.VMEM((TILES_HERE, 9 * PRE_ROWS, C), BF),
            pltpu.VMEM((TILES_HERE, C, C), BF),
            pltpu.VMEM((TILES_HERE, 2 * C_HALF, C), BF),
            pltpu.VMEM((9, C, C), BF),
            pltpu.VMEM((9, C, C), BF),
            pltpu.VMEM((TILES_HERE * PRE_ROWS, 9 * C), BF),
            pltpu.VMEM((4, TILES_HERE * PART, C), F32),
            pltpu.VMEM((len(RIM_TAPS), TILES_HERE * RIM_ROWS, C), BF),
            pltpu.VMEM((TILES_HERE * DOWN_ROWS, 9 * C), BF),
            pltpu.SemaphoreType.DMA((2 * CHAN + TILES_HERE,)),
        ],
        compiler_params=MOST,
        name="tiles",
    )(payload, rim_at, *(jnp.asarray(array, BF) for array in constants), window, weights)


def shards(fields, seam_table, w_first, w_down, cotangent):
    coords = [lax.axis_index(axis) for axis in ("ylo", "x", "z", "core")]
    own, units, half = pl.pallas_call(
        pack_kernel,
        out_shape=(
            jax.ShapeDtypeStruct((TILES_HERE, PACK_ROWS, 128), BF),
            jax.ShapeDtypeStruct((YX, TILES_HERE * 4 * UNIT, 128), BF),
            jax.ShapeDtypeStruct(w_first.shape, BF),
        ),
        in_specs=hbm(4),
        out_specs=tuple(vmem(1) + hbm(2)),
        scratch_shapes=[
            pltpu.VMEM((TILES_HERE, CH, CELLS), BF),
            pltpu.VMEM((TILES_HERE, COARSE, CH), BF),
            pltpu.VMEM((9, CH, C), BF),
            pltpu.VMEM((TILES_HERE * 4 * UNIT, 128), BF),
            pltpu.SemaphoreType.DMA((4 + YX,)),
        ],
        compiler_params=WHOLE,
        name="pack",
    )(fields, jnp.swapaxes(cotangent, 1, 2), w_first, w_down)
    weights = lax.all_gather(half, ("chan", "core"), axis=0, tiled=False)
    units = lax.all_to_all(units, ("ylo", "x"), 0, 0).reshape(-1, 128)
    units = lax.all_gather(units, "core", axis=0, tiled=True)
    words, beyond = edge_words(seam_table)
    sends = pl.pallas_call(
        place_kernel,
        out_shape=jax.ShapeDtypeStruct((NZ, SEND_ROWS, 128), BF),
        in_specs=smem(2) + vmem(1),
        out_specs=vmem(1)[0],
        scratch_shapes=[pltpu.VMEM((NZ, SEND_ROWS, 128), F32)],
        compiler_params=LIMIT,
        name="place",
    )(words, beyond, units)
    got = lax.all_to_all(sends, "z", 0, 0)
    joined = pl.pallas_call(
        join_kernel,
        out_shape=jax.ShapeDtypeStruct((CHAN, TILES_HERE * PAY_ROWS, 128), BF),
        in_specs=vmem(2),
        out_specs=vmem(1)[0],
        scratch_shapes=[pltpu.VMEM((TILES_HERE * PAY_ROWS, 128), F32)],
        compiler_params=LIMIT,
        name="join",
    )(got, own)
    payload = lax.all_to_all(joined, "chan", 0, 0)

    tile_at = ((coords[0] * NX + coords[1]) * NZ + coords[2]) * CORE + coords[3]
    own_table = lax.dynamic_slice_in_dim(seam_table, tile_at * TILES_HERE, TILES_HERE, 0)
    code = own_table[:, :, 1] * 2 + own_table[:, :, 2]
    chosen = (code[:, :, None] == jnp.arange(8, dtype=jnp.int32)).astype(BF).reshape(TILES_HERE, 32)
    one_hots = []
    for (fixed, varied), depth in ((window_index(), C), (rim_index(), 2 * C_HALF)):
        at = jnp.dot(chosen, jnp.asarray(varied, BF), preferred_element_type=F32) + jnp.asarray(fixed, F32)
        one_hots.append((at[:, :, None] == jnp.arange(1, depth + 1, dtype=jnp.int32).astype(F32)).astype(BF))

    coarse, grad_pre, grads = tiles_call(payload, one_hots[0], one_hots[1], weights)

    part = lax.all_to_all(grads, "core", 0, 0)
    part = (part[0].astype(F32) + part[1].astype(F32)).astype(BF).reshape(YX, 144, 128)
    part = lax.all_to_all(part, ("ylo", "x"), 0, 0)
    part = part.astype(F32).sum(0).astype(BF)
    part = lax.all_to_all(jnp.broadcast_to(part[None], (NZ, 144, 128)), "z", 0, 0)
    part = part.astype(F32).sum(0).astype(BF)
    part = lax.all_to_all(jnp.broadcast_to(part[None], (YX, 144, 128)), ("ylo", "x"), 0, 0)
    whole = lax.all_gather(part.reshape(18 * CH, 128), "core", axis=0, tiled=False)
    whole = jnp.concatenate([whole[0], whole[1]], axis=1).astype(F32).reshape(2, 9, CH, C)
    tiles = TILES_HERE * PLANE * CORE
    return (
        jnp.swapaxes(coarse, 1, 2),
        whole[0] * float(tiles * CELLS) ** (-0.5),
        whole[1] * float(tiles * COARSE) ** (-0.5),
        grad_pre,
    )


def solution(mesh):
    fine = Mesh(mesh.devices.reshape(YLO, NX, NZ, CORE, CHAN), ("ylo", "x", "z", "core", "chan"))
    return jax.shard_map(
        shards,
        mesh=fine,
        in_specs=(
            P(TILE_AXES, "chan", None),
            P(),
            P(None, "chan", None),
            P(None, "chan", None),
            P(TILE_AXES, "chan", None),
        ),
        out_specs=(
            P(TILE_AXES, "chan", None),
            P(None, "chan", None),
            P(None, "chan", None),
            P(TILE_AXES, "chan", None),
        ),
        check_vma=False,
    )
```

```python
import numpy as np
import jax
import jax.numpy as jnp
from jax import lax
from jax.experimental import pallas as pl
from jax.experimental.pallas import tpu as pltpu
from jax.sharding import Mesh, PartitionSpec as P

S = 12
HALF = 6
CELLS = 144
COARSE = 36
TILES_HERE = 3
CH = 64
C = 256
YLO, NX, NZ, CORE, CHAN = 2, 4, 8, 2, 4
YX = YLO * NX
NEAR = YX * CORE
PLANE = YX * NZ
TILE_AXES = ("ylo", "x", "z", "core")
BF = jnp.bfloat16
F32 = jnp.float32

EDGE_ROWS = (0, 28, 14, 34)
FIELD_ROWS = 40
BLOCK_ROWS = 52
SEND_ROWS = 160
OWN_ROWS = 72
X_HALF = OWN_ROWS + FIELD_ROWS
C_OWN = 18
C_HALF = 32
PAY_ROWS = X_HALF + C_HALF
PACK_ROWS = 96
UNIT = 16
PART = 40
INNER = 4 * PART
PRE_ROWS = INNER + 32
DOWN_ROWS = 48
RIM_ROWS = 48
RIM_TAPS = (0, 1, 2, 3, 6)


def strip_cells(edge, depth):
    if edge == 0:
        return [depth * S + i for i in range(S)]
    if edge == 1:
        return [(S - 1 - depth) * S + i for i in range(S)]
    if edge == 2:
        return [i * S + depth for i in range(S)]
    return [i * S + S - 1 - depth for i in range(S)]


def cell_row(row, col):
    return (row % 2 * 2 + col % 2) * PART + row // 2 * HALF + col // 2


def own_at(cell):
    return cell // 2 + X_HALF * (cell % 2)


def near_at(edge, along, depth):
    row = OWN_ROWS + EDGE_ROWS[edge] + 6 * depth
    if along < 0:
        return OWN_ROWS + EDGE_ROWS[edge] + 12 + X_HALF * depth
    if along >= S:
        return OWN_ROWS + EDGE_ROWS[edge] + 13 + X_HALF * depth
    return row + along // 2 + X_HALF * (along % 2)


def window_index():
    fixed = np.zeros((9, PRE_ROWS), np.float32)
    varied = np.zeros((4, 4, 2, 9, PRE_ROWS), np.float32)
    for k in range(9):
        a, b = k // 3, k % 3
        for cell in range(CELLS):
            row, col = cell // S + a, cell % S + b
            inner_row, inner_col = 1 <= row <= S, 1 <= col <= S
            if inner_row and inner_col:
                fixed[k, cell_row(cell // S, cell % S)] = 1 + own_at((row - 1) * S + col - 1)
            elif inner_row or inner_col:
                edge = (2 if col == 0 else 3) if inner_row else (0 if row == 0 else 1)
                at = row - 1 if inner_row else col - 1
                for flip in range(2):
                    varied[edge, :, flip, k, cell_row(cell // S, cell % S)] = 1 + near_at(
                        edge, 11 - at if flip else at, 0
                    )
        for slot, edge in enumerate((0, 2)):
            own = strip_cells(edge, 0)
            for facing in range(4):
                depth = (a - 1, 1 - a, b - 1, 1 - b)[facing]
                shift = (b - 1, b - 1, a - 1, a - 1)[facing]
                for flip in range(2):
                    for j in range(S):
                        along = (11 - j if flip else j) + shift
                        if depth >= 0:
                            at = near_at(edge, along, depth)
                        elif 0 <= along < S:
                            at = own_at(own[11 - along if flip else along])
                        else:
                            continue
                        varied[edge, facing, flip, k, INNER + 16 * slot + j] = 1 + at
    return fixed.reshape(-1), varied.reshape(32, -1)


def rim_index():
    varied = np.zeros((4, 4, 2, len(RIM_TAPS), RIM_ROWS), np.float32)
    for slot, k in enumerate(RIM_TAPS):
        a, b = k // 3, k % 3
        for edge in range(4):
            for flip in range(2):
                for j in range(S):
                    for facing, live, tap in ((0, a == 0, b), (2, b == 0, a)):
                        at = (11 - j if flip else j) + 1 - tap
                        if live and at % 2 == 0 and 0 <= at < S:
                            at //= 2
                            varied[edge, facing, flip, slot, edge * S + j] = (
                                1 + C_OWN + 3 * edge + at // 2 + C_HALF * (at % 2)
                            )
    return np.zeros(len(RIM_TAPS) * RIM_ROWS, np.float32), varied.reshape(32, -1)


def shift_selector():
    chosen = np.zeros((2, 2, PART, 2 * C_HALF), np.float32)
    for down in range(2):
        for right in range(2):
            for row in range(HALF - down):
                for col in range(HALF - right):
                    at = (row + down) * HALF + col + right
                    chosen[down, right, row * HALF + col, at // 2 + C_HALF * (at % 2)] = 1
    return chosen.reshape(INNER, 2 * C_HALF)


def down_selector():
    chosen = np.zeros((9, DOWN_ROWS, PRE_ROWS), np.float32)
    for k in range(9):
        for cell in range(COARSE):
            row, col = 2 * (cell // HALF) + k // 3, 2 * (cell % HALF) + k % 3
            if row == 0 and col == 0:
                continue
            if row == 0:
                at = INNER + col - 1
            elif col == 0:
                at = INNER + 16 + row - 1
            else:
                at = cell_row(row - 1, col - 1)
            chosen[k, cell, at] = 1
    return chosen.reshape(9 * DOWN_ROWS, PRE_ROWS)


def rim_selector():
    chosen = np.zeros((INNER, RIM_ROWS), np.float32)
    for edge in range(4):
        for j, cell in enumerate(strip_cells(edge, 0)):
            chosen[cell_row(cell // S, cell % S), edge * S + j] = 1
    return chosen


def cell_selector():
    chosen = np.zeros((INNER, CELLS), np.float32)
    for cell in range(CELLS):
        chosen[cell_row(cell // S, cell % S), cell] = 1
    return chosen


def order_selector():
    chosen = np.zeros((DOWN_ROWS, 2 * C_HALF), np.float32)
    for cell in range(COARSE):
        chosen[cell, cell // 2 + C_HALF * (cell % 2)] = 1
    return chosen


def dot_nn(left, right):
    return lax.dot_general(left, right, (((1,), (0,)), ((), ())), preferred_element_type=F32)


def dot_tn(left, right):
    return lax.dot_general(left, right, (((0,), (0,)), ((), ())), preferred_element_type=F32)


def dot_nt(left, right):
    return lax.dot_general(left, right, (((1,), (1,)), ((), ())), preferred_element_type=F32)


def pack_selectors(half):
    rows = PACK_ROWS + 4 * UNIT
    row = lax.broadcasted_iota(jnp.int32, (rows, CELLS), 0)
    at = lax.broadcasted_iota(jnp.int32, (rows, CELLS), 1)
    edge, j = (row - PACK_ROWS) >> 4, (row - PACK_ROWS) & 15
    deep = jnp.where(jnp.logical_and(j >= 9, j < 15), 1, 0)
    along = jnp.where(j < 6, 2 * j + half, jnp.where(j < 15, 2 * (j - 9) + half, 11 - half))
    start = jnp.where(edge == 0, S * deep, jnp.where(edge == 1, S * (S - 1 - deep), jnp.where(edge == 2, deep, S - 1 - deep)))
    cell = start + along * jnp.where(edge < 2, 1, S)
    cell = jnp.where(jnp.logical_or(j < 6, j >= 9), cell, -1)
    cell = jnp.where(row < OWN_ROWS, 2 * row + half, jnp.where(row < PACK_ROWS, -1, cell))
    fields = jnp.where(at == cell, 1.0, 0.0).astype(BF)
    row, at, edge, j = row[:, :COARSE], at[:, :COARSE], edge[:, :COARSE], j[:, :COARSE]
    cell = (2 * (j - 6) + half) * jnp.where(edge == 0, 1, HALF)
    live = jnp.logical_and(jnp.logical_and(j >= 6, j < 9), jnp.logical_or(edge == 0, edge == 2))
    cell = jnp.where(live, cell, -1)
    own = jnp.where(row < OWN_ROWS + C_OWN, 2 * (row - OWN_ROWS) + half, -1)
    cell = jnp.where(row < PACK_ROWS, own, cell)
    return fields, jnp.where(at == cell, 1.0, 0.0).astype(BF)


def pack_kernel(fields_hbm, cot_hbm, first_ref, down_ref, own_ref, unit_hbm, half_ref, fields_ref, cot_ref, held, unit_ref, sems):
    loads = [
        pltpu.make_async_copy(fields_hbm, fields_ref, sems.at[0]),
        pltpu.make_async_copy(cot_hbm, cot_ref, sems.at[1]),
    ]
    for load in loads:
        load.start()
    core = lax.axis_index("core")

    @pl.when(core == 0)
    def _():
        pltpu.make_async_copy(first_ref, held, sems.at[2]).start()

    @pl.when(core == 1)
    def _():
        pltpu.make_async_copy(down_ref, held, sems.at[2]).start()

    chosen = [pack_selectors(h) for h in range(2)]
    for load in loads:
        load.wait()
    for t in range(TILES_HERE):
        halves = [(dot_nt(f, fields_ref[t]) + dot_nn(c, cot_ref[t])).astype(BF) for f, c in chosen]
        for h in range(2):
            own_ref[t, :, h * CH : (h + 1) * CH] = halves[h][:PACK_ROWS]
            unit_ref[t * 4 * UNIT : (t + 1) * 4 * UNIT, h * CH : (h + 1) * CH] = halves[h][PACK_ROWS:]
    pltpu.make_async_copy(first_ref, held, sems.at[2]).wait()
    stores = [pltpu.make_async_copy(held, half_ref, sems.at[3])]
    for copy in range(YX):
        stores.append(pltpu.make_async_copy(unit_ref, unit_hbm.at[copy], sems.at[4 + copy]))
    for store in stores:
        store.start()
    for store in stores:
        store.wait()


def edge_words(seam_table):
    n, f, r = seam_table[:, :, 0], seam_table[:, :, 1], seam_table[:, :, 2]
    device = n // TILES_HERE
    group = (device % CORE) * YX + device // (NZ * CORE)
    unit = (group * TILES_HERE + n % TILES_HERE) * 4 + f
    z = (device // CORE) % NZ
    word = unit + r * 256 + z * 512
    beyond = (n * 4 + jnp.where(f < 2, 2, 0)) * 2 + f % 2
    return word.reshape(-1), beyond.reshape(-1)


def place_kernel(word_ref, beyond_ref, unit_ref, out_ref, sent):
    ylo, x, z, core = (lax.axis_index(axis) for axis in TILE_AXES)

    def unit_at(word):
        keep = jnp.where((word >> 9) == z, 1.0, 0.0).astype(F32)
        at = pl.multiple_of((word & 255) * UNIT, UNIT)
        return unit_ref[pl.ds(at, UNIT), :].astype(F32) * keep

    def body(z_to, carry):
        device = ((ylo * NX + x) * NZ + z_to) * CORE + core
        for t in range(TILES_HERE):
            for edge in range(4):
                at = (device * TILES_HERE + t) * 4 + edge
                unit = unit_at(word_ref[at])
                row = t * BLOCK_ROWS + EDGE_ROWS[edge]
                cot = t * BLOCK_ROWS + FIELD_ROWS + 3 * edge
                sent[z_to, row : row + 6, :] = unit[0:6]
                sent[z_to, cot : cot + 3, :] = unit[6:9]
                if edge % 2 == 0:
                    sent[z_to, row + 6 : row + 12, :] = unit[9:15]
                    beyond = beyond_ref[at]
                    for last in range(2):
                        word = word_ref[(beyond >> 1) + last]
                        end = unit_at(word)
                        low = ((beyond + (word >> 8)) & 1) == 0
                        sent[z_to, row + 12 + last : row + 13 + last, :] = jnp.where(low, end[0:1], end[15:16])
        sent[z_to, TILES_HERE * BLOCK_ROWS :, :] = jnp.zeros((SEND_ROWS - TILES_HERE * BLOCK_ROWS, 128), F32)
        return carry

    lax.fori_loop(0, NZ, body, 0)
    out_ref[...] = sent[...].astype(BF)


def join_kernel(got_ref, own_ref, out_ref, rows):
    total = got_ref[0].astype(F32)
    for q in range(1, NZ):
        total = total + got_ref[q].astype(F32)
    for t in range(TILES_HERE):
        base, block = t * PAY_ROWS, t * BLOCK_ROWS
        own = own_ref[t].astype(F32)
        rows[base : base + OWN_ROWS, :] = own[:OWN_ROWS]
        rows[base + OWN_ROWS : base + X_HALF, :] = total[block : block + FIELD_ROWS]
        rows[base + X_HALF : base + X_HALF + C_OWN, :] = own[OWN_ROWS : OWN_ROWS + C_OWN]
        rows[base + X_HALF + C_OWN : base + PAY_ROWS - 2, :] = total[block + FIELD_ROWS : block + BLOCK_ROWS]
        rows[base + PAY_ROWS - 2 : base + PAY_ROWS, :] = jnp.zeros((2, 128), F32)
    whole = rows[...].astype(BF)
    for c in range(CHAN):
        out_ref[c] = whole


def main_kernel(
    pay_ref, rim_at_ref, shift_ref, down_ref, rim_ref, order_ref, cell_ref, window_hbm, weights_ref,
    coarse_ref, gp_ref, grads_ref, window_ref, xs, cs, wf, wd, wins, ups, rims, downs, gps, up, sems,
):
    window_copies = [
        pltpu.make_async_copy(window_hbm.at[t], window_ref.at[t], sems.at[2 * CHAN + t]) for t in range(TILES_HERE)
    ]
    for copy in window_copies:
        copy.start()
    copies = []
    for which, held in enumerate((wf, wd)):
        for c in range(CHAN):
            copies.append(
                pltpu.make_async_copy(
                    weights_ref.at[2 * c + which], held.at[:, pl.ds(c * CH, CH), :], sems.at[2 * c + which]
                )
            )
    for copy in copies:
        copy.start()
    chan = lax.axis_index("chan")
    pick = jnp.where(
        lax.broadcasted_iota(jnp.int32, (CH, C), 1) == lax.broadcasted_iota(jnp.int32, (CH, C), 0) + chan * CH, 1.0, 0.0
    ).astype(BF)
    for c in range(CHAN):
        for t in range(TILES_HERE):
            base = t * PAY_ROWS
            for h in range(2):
                lanes = slice(h * CH, (h + 1) * CH)
                xs[t, h * X_HALF : (h + 1) * X_HALF, c * CH : (c + 1) * CH] = pay_ref[c, base : base + X_HALF, lanes]
                cs[t, h * C_HALF : (h + 1) * C_HALF, c * CH : (c + 1) * CH] = pay_ref[
                    c, base + X_HALF : base + PAY_ROWS, lanes
                ]
    for t in range(TILES_HERE):
        xs[t, 2 * X_HALF :, :] = jnp.zeros((C - 2 * X_HALF, C), BF)
    for t in range(TILES_HERE):
        window_copies[t].wait()
        for k in range(9):
            wins[t * PRE_ROWS : (t + 1) * PRE_ROWS, k * C : (k + 1) * C] = dot_nn(
                window_ref[t, k * PRE_ROWS : (k + 1) * PRE_ROWS, :], xs[t]
            ).astype(BF)
        shifted = dot_nn(shift_ref[...], cs[t])
        for s in range(4):
            ups[s, t * PART : (t + 1) * PART, :] = shifted[s * PART : (s + 1) * PART]
        near = dot_nn(rim_at_ref[t], cs[t]).astype(BF)
        for s in range(len(RIM_TAPS)):
            rims[s, t * RIM_ROWS : (t + 1) * RIM_ROWS, :] = near[s * RIM_ROWS : (s + 1) * RIM_ROWS]
    for copy in copies[:CHAN]:
        copy.wait()
    pre = dot_nn(wins[...], wf[...].reshape(9 * C, C))
    for copy in copies[CHAN:]:
        copy.wait()
    ups_low = [ups[s].astype(BF) for s in range(4)]
    blocks = (
        dot_nt(ups_low[0], wd[4]),
        dot_nt(ups_low[1], wd[3]) + dot_nt(ups_low[0], wd[5]),
        dot_nt(ups_low[2], wd[1]) + dot_nt(ups_low[0], wd[7]),
        dot_nt(ups_low[3], wd[0]) + dot_nt(ups_low[2], wd[2]) + dot_nt(ups_low[1], wd[6]) + dot_nt(ups_low[0], wd[8]),
    )
    rim = dot_nt(rims[0], wd[RIM_TAPS[0]])
    for s in range(1, len(RIM_TAPS)):
        rim = rim + dot_nt(rims[s], wd[RIM_TAPS[s]])
    rim = rim.astype(BF)
    scale = np.float32(np.sqrt(2 / np.pi))
    squared = pre * pre
    bent = jnp.tanh(scale * (pre + np.float32(0.044715) * squared * pre))
    gate = 0.5 * (1.0 + bent)
    hidden = (pre * gate).astype(BF)
    slope = gate + 0.5 * pre * (1.0 - bent * bent) * scale * (1.0 + np.float32(3 * 0.044715) * squared)

    for t in range(TILES_HERE):
        own_hidden = hidden[t * PRE_ROWS : (t + 1) * PRE_ROWS]
        windows = dot_nn(down_ref[...], own_hidden).astype(BF)
        for k in range(9):
            downs[t * DOWN_ROWS : (t + 1) * DOWN_ROWS, k * C : (k + 1) * C] = windows[k * DOWN_ROWS : (k + 1) * DOWN_ROWS]
        up[t * DOWN_ROWS : (t + 1) * DOWN_ROWS, :] = dot_nn(order_ref[...], cs[t]).astype(BF)

        grad_hidden = jnp.concatenate([block[t * PART : (t + 1) * PART] for block in blocks], axis=0)
        grad_hidden = grad_hidden + dot_nn(rim_ref[...], rim[t * RIM_ROWS : (t + 1) * RIM_ROWS])
        grad_pre = (grad_hidden * slope[t * PRE_ROWS : t * PRE_ROWS + INNER]).astype(BF)
        gps[t * PRE_ROWS : t * PRE_ROWS + INNER, :] = grad_pre
        gps[t * PRE_ROWS + INNER : (t + 1) * PRE_ROWS, :] = jnp.zeros((PRE_ROWS - INNER, C), BF)
        gp_ref[t] = dot_nn(dot_nt(pick, grad_pre).astype(BF), cell_ref[...]).astype(BF)

    lanes = pl.multiple_of((chan // 2) * 128, 128)
    for k in range(9):
        for base, left, right in ((0, wins, gps), (9 * CH, downs, up)):
            both = dot_tn(left[:, pl.ds(k * C + lanes, 128)], right[...])
            part = jnp.where(chan % 2 == 0, both[:CH], both[CH:]).astype(BF)
            for h in range(CORE):
                grads_ref[h, base + k * CH : base + (k + 1) * CH, :] = part[:, h * 128 : (h + 1) * 128]
    coarse = dot_nt(dot_nn(downs[...], wd[...].reshape(9 * C, C)).astype(BF), pick).astype(BF)
    for t in range(TILES_HERE):
        coarse_ref[t] = coarse[t * DOWN_ROWS : t * DOWN_ROWS + COARSE]


def vmem(count):
    return [pl.BlockSpec(memory_space=pltpu.VMEM)] * count


def hbm(count):
    return [pl.BlockSpec(memory_space=pltpu.HBM)] * count


def smem(count):
    return [pl.BlockSpec(memory_space=pltpu.SMEM)] * count


LIMIT = pltpu.CompilerParams(vmem_limit_bytes=48 * 1024 * 1024)
WHOLE = pltpu.CompilerParams(vmem_limit_bytes=60 * 1024 * 1024)
MOST = pltpu.CompilerParams(vmem_limit_bytes=52 * 1024 * 1024)


def tiles_call(payload, window, rim_at, weights):
    constants = (shift_selector(), down_selector(), rim_selector(), order_selector(), cell_selector())
    return pl.pallas_call(
        main_kernel,
        out_shape=(
            jax.ShapeDtypeStruct((TILES_HERE, COARSE, CH), BF),
            jax.ShapeDtypeStruct((TILES_HERE, CH, CELLS), BF),
            jax.ShapeDtypeStruct((CORE, 18 * CH, 128), BF),
        ),
        in_specs=vmem(7) + hbm(2),
        out_specs=tuple(vmem(3)),
        scratch_shapes=[
            pltpu.VMEM((TILES_HERE, 9 * PRE_ROWS, C), BF),
            pltpu.VMEM((TILES_HERE, C, C), BF),
            pltpu.VMEM((TILES_HERE, 2 * C_HALF, C), BF),
            pltpu.VMEM((9, C, C), BF),
            pltpu.VMEM((9, C, C), BF),
            pltpu.VMEM((TILES_HERE * PRE_ROWS, 9 * C), BF),
            pltpu.VMEM((4, TILES_HERE * PART, C), F32),
            pltpu.VMEM((len(RIM_TAPS), TILES_HERE * RIM_ROWS, C), BF),
            pltpu.VMEM((TILES_HERE * DOWN_ROWS, 9 * C), BF),
            pltpu.VMEM((TILES_HERE * PRE_ROWS, C), BF),
            pltpu.VMEM((TILES_HERE * DOWN_ROWS, C), BF),
            pltpu.SemaphoreType.DMA((2 * CHAN + TILES_HERE,)),
        ],
        compiler_params=MOST,
        name="tiles",
    )(payload, rim_at, *(jnp.asarray(array, BF) for array in constants), window, weights)


def shards(fields, seam_table, w_first, w_down, cotangent):
    coords = [lax.axis_index(axis) for axis in ("ylo", "x", "z", "core")]
    own, units, half = pl.pallas_call(
        pack_kernel,
        out_shape=(
            jax.ShapeDtypeStruct((TILES_HERE, PACK_ROWS, 128), BF),
            jax.ShapeDtypeStruct((YX, TILES_HERE * 4 * UNIT, 128), BF),
            jax.ShapeDtypeStruct(w_first.shape, BF),
        ),
        in_specs=hbm(4),
        out_specs=tuple(vmem(1) + hbm(2)),
        scratch_shapes=[
            pltpu.VMEM((TILES_HERE, CH, CELLS), BF),
            pltpu.VMEM((TILES_HERE, COARSE, CH), BF),
            pltpu.VMEM((9, CH, C), BF),
            pltpu.VMEM((TILES_HERE * 4 * UNIT, 128), BF),
            pltpu.SemaphoreType.DMA((4 + YX,)),
        ],
        compiler_params=WHOLE,
        name="pack",
    )(fields, jnp.swapaxes(cotangent, 1, 2), w_first, w_down)
    weights = lax.all_gather(half, ("chan", "core"), axis=0, tiled=False)
    units = lax.all_to_all(units, ("ylo", "x"), 0, 0).reshape(-1, 128)
    units = lax.all_gather(units, "core", axis=0, tiled=True)
    words, beyond = edge_words(seam_table)
    sends = pl.pallas_call(
        place_kernel,
        out_shape=jax.ShapeDtypeStruct((NZ, SEND_ROWS, 128), BF),
        in_specs=smem(2) + vmem(1),
        out_specs=vmem(1)[0],
        scratch_shapes=[pltpu.VMEM((NZ, SEND_ROWS, 128), F32)],
        compiler_params=LIMIT,
        name="place",
    )(words, beyond, units)
    got = lax.all_to_all(sends, "z", 0, 0)
    joined = pl.pallas_call(
        join_kernel,
        out_shape=jax.ShapeDtypeStruct((CHAN, TILES_HERE * PAY_ROWS, 128), BF),
        in_specs=vmem(2),
        out_specs=vmem(1)[0],
        scratch_shapes=[pltpu.VMEM((TILES_HERE * PAY_ROWS, 128), F32)],
        compiler_params=LIMIT,
        name="join",
    )(got, own)
    payload = lax.all_to_all(joined, "chan", 0, 0)

    tile_at = ((coords[0] * NX + coords[1]) * NZ + coords[2]) * CORE + coords[3]
    own_table = lax.dynamic_slice_in_dim(seam_table, tile_at * TILES_HERE, TILES_HERE, 0)
    code = own_table[:, :, 1] * 2 + own_table[:, :, 2]
    chosen = (code[:, :, None] == jnp.arange(8, dtype=jnp.int32)).astype(BF).reshape(TILES_HERE, 32)
    one_hots = []
    for (fixed, varied), depth in ((window_index(), C), (rim_index(), 2 * C_HALF)):
        at = jnp.dot(chosen, jnp.asarray(varied, BF), preferred_element_type=F32) + jnp.asarray(fixed, F32)
        one_hots.append((at[:, :, None] == jnp.arange(1, depth + 1, dtype=jnp.int32).astype(F32)).astype(BF))

    coarse, grad_pre, grads = tiles_call(payload, one_hots[0], one_hots[1], weights)

    part = lax.all_to_all(grads, "core", 0, 0)
    part = (part[0].astype(F32) + part[1].astype(F32)).astype(BF).reshape(YX, 144, 128)
    part = lax.all_to_all(part, ("ylo", "x"), 0, 0)
    part = part.astype(F32).sum(0).astype(BF)
    part = lax.all_to_all(jnp.broadcast_to(part[None], (NZ, 144, 128)), "z", 0, 0)
    part = part.astype(F32).sum(0).astype(BF)
    part = lax.all_to_all(jnp.broadcast_to(part[None], (YX, 144, 128)), ("ylo", "x"), 0, 0)
    whole = lax.all_gather(part.reshape(18 * CH, 128), "core", axis=0, tiled=False)
    whole = jnp.concatenate([whole[0], whole[1]], axis=1).astype(F32).reshape(2, 9, CH, C)
    tiles = TILES_HERE * PLANE * CORE
    return (
        jnp.swapaxes(coarse, 1, 2),
        whole[0] * float(tiles * CELLS) ** (-0.5),
        whole[1] * float(tiles * COARSE) ** (-0.5),
        grad_pre,
    )


def solution(mesh):
    fine = Mesh(mesh.devices.reshape(YLO, NX, NZ, CORE, CHAN), ("ylo", "x", "z", "core", "chan"))
    return jax.shard_map(
        shards,
        mesh=fine,
        in_specs=(
            P(TILE_AXES, "chan", None),
            P(),
            P(None, "chan", None),
            P(None, "chan", None),
            P(TILE_AXES, "chan", None),
        ),
        out_specs=(
            P(TILE_AXES, "chan", None),
            P(None, "chan", None),
            P(None, "chan", None),
            P(TILE_AXES, "chan", None),
        ),
        check_vma=False,
    )
```

```python
import numpy as np
import jax
import jax.numpy as jnp
from jax import lax
from jax.experimental import pallas as pl
from jax.experimental.pallas import tpu as pltpu
from jax.sharding import Mesh, PartitionSpec as P

S = 12
HALF = 6
CELLS = 144
COARSE = 36
TILES_HERE = 3
CH = 64
C = 256
YLO, NX, NZ, CORE, CHAN = 2, 4, 8, 2, 4
YX = YLO * NX
NEAR = YX * CORE
PLANE = YX * NZ
TILE_AXES = ("ylo", "x", "z", "core")
BF = jnp.bfloat16
F32 = jnp.float32

EDGE_ROWS = (0, 28, 14, 34)
FIELD_ROWS = 40
BLOCK_ROWS = 52
SEND_ROWS = 160
OWN_ROWS = 72
X_HALF = OWN_ROWS + FIELD_ROWS
C_OWN = 18
C_HALF = 32
PAY_ROWS = X_HALF + C_HALF
PACK_ROWS = 96
UNIT = 16
PART = 40
INNER = 4 * PART
PRE_ROWS = INNER + 32
DOWN_ROWS = 48
RIM_ROWS = 48
RIM_TAPS = (0, 1, 2, 3, 6)


def strip_cells(edge, depth):
    if edge == 0:
        return [depth * S + i for i in range(S)]
    if edge == 1:
        return [(S - 1 - depth) * S + i for i in range(S)]
    if edge == 2:
        return [i * S + depth for i in range(S)]
    return [i * S + S - 1 - depth for i in range(S)]


def cell_row(row, col):
    return (row % 2 * 2 + col % 2) * PART + row // 2 * HALF + col // 2


def own_at(cell):
    return cell // 2 + X_HALF * (cell % 2)


def near_at(edge, along, depth):
    row = OWN_ROWS + EDGE_ROWS[edge] + 6 * depth
    if along < 0:
        return OWN_ROWS + EDGE_ROWS[edge] + 12 + X_HALF * depth
    if along >= S:
        return OWN_ROWS + EDGE_ROWS[edge] + 13 + X_HALF * depth
    return row + along // 2 + X_HALF * (along % 2)


def window_index():
    fixed = np.zeros((9, PRE_ROWS), np.float32)
    varied = np.zeros((4, 4, 2, 9, PRE_ROWS), np.float32)
    for k in range(9):
        a, b = k // 3, k % 3
        for cell in range(CELLS):
            row, col = cell // S + a, cell % S + b
            inner_row, inner_col = 1 <= row <= S, 1 <= col <= S
            if inner_row and inner_col:
                fixed[k, cell_row(cell // S, cell % S)] = 1 + own_at((row - 1) * S + col - 1)
            elif inner_row or inner_col:
                edge = (2 if col == 0 else 3) if inner_row else (0 if row == 0 else 1)
                at = row - 1 if inner_row else col - 1
                for flip in range(2):
                    varied[edge, :, flip, k, cell_row(cell // S, cell % S)] = 1 + near_at(
                        edge, 11 - at if flip else at, 0
                    )
        for slot, edge in enumerate((0, 2)):
            own = strip_cells(edge, 0)
            for facing in range(4):
                depth = (a - 1, 1 - a, b - 1, 1 - b)[facing]
                shift = (b - 1, b - 1, a - 1, a - 1)[facing]
                for flip in range(2):
                    for j in range(S):
                        along = (11 - j if flip else j) + shift
                        if depth >= 0:
                            at = near_at(edge, along, depth)
                        elif 0 <= along < S:
                            at = own_at(own[11 - along if flip else along])
                        else:
                            continue
                        varied[edge, facing, flip, k, INNER + 16 * slot + j] = 1 + at
    return fixed.reshape(-1), varied.reshape(32, -1)


def rim_index():
    varied = np.zeros((4, 4, 2, len(RIM_TAPS), RIM_ROWS), np.float32)
    for slot, k in enumerate(RIM_TAPS):
        a, b = k // 3, k % 3
        for edge in range(4):
            for flip in range(2):
                for j in range(S):
                    for facing, live, tap in ((0, a == 0, b), (2, b == 0, a)):
                        at = (11 - j if flip else j) + 1 - tap
                        if live and at % 2 == 0 and 0 <= at < S:
                            at //= 2
                            varied[edge, facing, flip, slot, edge * S + j] = (
                                1 + C_OWN + 3 * edge + at // 2 + C_HALF * (at % 2)
                            )
    return np.zeros(len(RIM_TAPS) * RIM_ROWS, np.float32), varied.reshape(32, -1)


def shift_selector():
    chosen = np.zeros((2, 2, PART, 2 * C_HALF), np.float32)
    for down in range(2):
        for right in range(2):
            for row in range(HALF - down):
                for col in range(HALF - right):
                    at = (row + down) * HALF + col + right
                    chosen[down, right, row * HALF + col, at // 2 + C_HALF * (at % 2)] = 1
    return chosen.reshape(INNER, 2 * C_HALF)


def down_selector():
    chosen = np.zeros((9, DOWN_ROWS, PRE_ROWS), np.float32)
    for k in range(9):
        for cell in range(COARSE):
            row, col = 2 * (cell // HALF) + k // 3, 2 * (cell % HALF) + k % 3
            if row == 0 and col == 0:
                continue
            if row == 0:
                at = INNER + col - 1
            elif col == 0:
                at = INNER + 16 + row - 1
            else:
                at = cell_row(row - 1, col - 1)
            chosen[k, cell, at] = 1
    return chosen.reshape(9 * DOWN_ROWS, PRE_ROWS)


def rim_selector():
    chosen = np.zeros((INNER, RIM_ROWS), np.float32)
    for edge in range(4):
        for j, cell in enumerate(strip_cells(edge, 0)):
            chosen[cell_row(cell // S, cell % S), edge * S + j] = 1
    return chosen


def cell_selector():
    chosen = np.zeros((INNER, CELLS), np.float32)
    for cell in range(CELLS):
        chosen[cell_row(cell // S, cell % S), cell] = 1
    return chosen


def order_selector():
    chosen = np.zeros((DOWN_ROWS, 2 * C_HALF), np.float32)
    for cell in range(COARSE):
        chosen[cell, cell // 2 + C_HALF * (cell % 2)] = 1
    return chosen


def dot_nn(left, right):
    return lax.dot_general(left, right, (((1,), (0,)), ((), ())), preferred_element_type=F32)


def dot_tn(left, right):
    return lax.dot_general(left, right, (((0,), (0,)), ((), ())), preferred_element_type=F32)


def dot_nt(left, right):
    return lax.dot_general(left, right, (((1,), (1,)), ((), ())), preferred_element_type=F32)


def pack_selectors(half):
    rows = PACK_ROWS + 4 * UNIT
    row = lax.broadcasted_iota(jnp.int32, (rows, CELLS), 0)
    at = lax.broadcasted_iota(jnp.int32, (rows, CELLS), 1)
    edge, j = (row - PACK_ROWS) >> 4, (row - PACK_ROWS) & 15
    deep = jnp.where(jnp.logical_and(j >= 9, j < 15), 1, 0)
    along = jnp.where(j < 6, 2 * j + half, jnp.where(j < 15, 2 * (j - 9) + half, 11 - half))
    start = jnp.where(edge == 0, S * deep, jnp.where(edge == 1, S * (S - 1 - deep), jnp.where(edge == 2, deep, S - 1 - deep)))
    cell = start + along * jnp.where(edge < 2, 1, S)
    cell = jnp.where(jnp.logical_or(j < 6, j >= 9), cell, -1)
    cell = jnp.where(row < OWN_ROWS, 2 * row + half, jnp.where(row < PACK_ROWS, -1, cell))
    fields = jnp.where(at == cell, 1.0, 0.0).astype(BF)
    row, at, edge, j = row[:, :COARSE], at[:, :COARSE], edge[:, :COARSE], j[:, :COARSE]
    cell = (2 * (j - 6) + half) * jnp.where(edge == 0, 1, HALF)
    live = jnp.logical_and(jnp.logical_and(j >= 6, j < 9), jnp.logical_or(edge == 0, edge == 2))
    cell = jnp.where(live, cell, -1)
    own = jnp.where(row < OWN_ROWS + C_OWN, 2 * (row - OWN_ROWS) + half, -1)
    cell = jnp.where(row < PACK_ROWS, own, cell)
    return fields, jnp.where(at == cell, 1.0, 0.0).astype(BF)


def pack_kernel(fields_hbm, cot_hbm, first_ref, down_ref, own_ref, unit_hbm, half_ref, fields_ref, cot_ref, held, unit_ref, sems):
    loads = [
        pltpu.make_async_copy(fields_hbm, fields_ref, sems.at[0]),
        pltpu.make_async_copy(cot_hbm, cot_ref, sems.at[1]),
    ]
    for load in loads:
        load.start()
    core = lax.axis_index("core")

    @pl.when(core == 0)
    def _():
        pltpu.make_async_copy(first_ref, held, sems.at[2]).start()

    @pl.when(core == 1)
    def _():
        pltpu.make_async_copy(down_ref, held, sems.at[2]).start()

    chosen = [pack_selectors(h) for h in range(2)]
    for load in loads:
        load.wait()
    for t in range(TILES_HERE):
        halves = [(dot_nt(f, fields_ref[t]) + dot_nn(c, cot_ref[t])).astype(BF) for f, c in chosen]
        for h in range(2):
            own_ref[t, :, h * CH : (h + 1) * CH] = halves[h][:PACK_ROWS]
            unit_ref[t * 4 * UNIT : (t + 1) * 4 * UNIT, h * CH : (h + 1) * CH] = halves[h][PACK_ROWS:]
    pltpu.make_async_copy(first_ref, held, sems.at[2]).wait()
    stores = [pltpu.make_async_copy(held, half_ref, sems.at[3])]
    for copy in range(YX):
        stores.append(pltpu.make_async_copy(unit_ref, unit_hbm.at[copy], sems.at[4 + copy]))
    for store in stores:
        store.start()
    for store in stores:
        store.wait()


def edge_words(seam_table):
    n, f, r = seam_table[:, :, 0], seam_table[:, :, 1], seam_table[:, :, 2]
    device = n // TILES_HERE
    group = (device % CORE) * YX + device // (NZ * CORE)
    unit = (group * TILES_HERE + n % TILES_HERE) * 4 + f
    z = (device // CORE) % NZ
    word = unit + r * 256 + z * 512
    beyond = (n * 4 + jnp.where(f < 2, 2, 0)) * 2 + f % 2
    return word.reshape(-1), beyond.reshape(-1)


def place_kernel(word_ref, beyond_ref, unit_ref, out_ref, sent):
    ylo, x, z, core = (lax.axis_index(axis) for axis in TILE_AXES)

    def unit_at(word):
        keep = jnp.where((word >> 9) == z, 1.0, 0.0).astype(F32)
        at = pl.multiple_of((word & 255) * UNIT, UNIT)
        return unit_ref[pl.ds(at, UNIT), :].astype(F32) * keep

    def body(z_to, carry):
        device = ((ylo * NX + x) * NZ + z_to) * CORE + core
        for t in range(TILES_HERE):
            for edge in range(4):
                at = (device * TILES_HERE + t) * 4 + edge
                unit = unit_at(word_ref[at])
                row = t * BLOCK_ROWS + EDGE_ROWS[edge]
                cot = t * BLOCK_ROWS + FIELD_ROWS + 3 * edge
                sent[z_to, row : row + 6, :] = unit[0:6]
                sent[z_to, cot : cot + 3, :] = unit[6:9]
                if edge % 2 == 0:
                    sent[z_to, row + 6 : row + 12, :] = unit[9:15]
                    beyond = beyond_ref[at]
                    for last in range(2):
                        word = word_ref[(beyond >> 1) + last]
                        end = unit_at(word)
                        low = ((beyond + (word >> 8)) & 1) == 0
                        sent[z_to, row + 12 + last : row + 13 + last, :] = jnp.where(low, end[0:1], end[15:16])
        sent[z_to, TILES_HERE * BLOCK_ROWS :, :] = jnp.zeros((SEND_ROWS - TILES_HERE * BLOCK_ROWS, 128), F32)
        return carry

    lax.fori_loop(0, NZ, body, 0)
    out_ref[...] = sent[...].astype(BF)


def join_kernel(got_ref, own_ref, out_ref, rows):
    total = got_ref[0].astype(F32)
    for q in range(1, NZ):
        total = total + got_ref[q].astype(F32)
    for t in range(TILES_HERE):
        base, block = t * PAY_ROWS, t * BLOCK_ROWS
        own = own_ref[t].astype(F32)
        rows[base : base + OWN_ROWS, :] = own[:OWN_ROWS]
        rows[base + OWN_ROWS : base + X_HALF, :] = total[block : block + FIELD_ROWS]
        rows[base + X_HALF : base + X_HALF + C_OWN, :] = own[OWN_ROWS : OWN_ROWS + C_OWN]
        rows[base + X_HALF + C_OWN : base + PAY_ROWS - 2, :] = total[block + FIELD_ROWS : block + BLOCK_ROWS]
        rows[base + PAY_ROWS - 2 : base + PAY_ROWS, :] = jnp.zeros((2, 128), F32)
    whole = rows[...].astype(BF)
    for c in range(CHAN):
        out_ref[c] = whole


def main_kernel(
    pay_ref, rim_at_ref, shift_ref, down_ref, rim_ref, order_ref, cell_ref, window_hbm, weights_ref,
    coarse_ref, gp_ref, grads_ref, window_ref, xs, cs, wf, wd, wins, ups, rims, downs, gps, up, sems,
):
    window_copies = [
        pltpu.make_async_copy(window_hbm.at[t], window_ref.at[t], sems.at[2 * CHAN + t]) for t in range(TILES_HERE)
    ]
    for copy in window_copies:
        copy.start()
    copies = []
    for which, held in enumerate((wf, wd)):
        for c in range(CHAN):
            copies.append(
                pltpu.make_async_copy(
                    weights_ref.at[2 * c + which], held.at[:, pl.ds(c * CH, CH), :], sems.at[2 * c + which]
                )
            )
    for copy in copies:
        copy.start()
    chan = lax.axis_index("chan")
    pick = jnp.where(
        lax.broadcasted_iota(jnp.int32, (CH, C), 1) == lax.broadcasted_iota(jnp.int32, (CH, C), 0) + chan * CH, 1.0, 0.0
    ).astype(BF)
    for c in range(CHAN):
        for t in range(TILES_HERE):
            base = t * PAY_ROWS
            for h in range(2):
                lanes = slice(h * CH, (h + 1) * CH)
                xs[t, h * X_HALF : (h + 1) * X_HALF, c * CH : (c + 1) * CH] = pay_ref[c, base : base + X_HALF, lanes]
                cs[t, h * C_HALF : (h + 1) * C_HALF, c * CH : (c + 1) * CH] = pay_ref[
                    c, base + X_HALF : base + PAY_ROWS, lanes
                ]
    for t in range(TILES_HERE):
        xs[t, 2 * X_HALF :, :] = jnp.zeros((C - 2 * X_HALF, C), BF)
    for t in range(TILES_HERE):
        window_copies[t].wait()
        for k in range(9):
            wins[t * PRE_ROWS : (t + 1) * PRE_ROWS, k * C : (k + 1) * C] = dot_nn(
                window_ref[t, k * PRE_ROWS : (k + 1) * PRE_ROWS, :], xs[t]
            ).astype(BF)
        shifted = dot_nn(shift_ref[...], cs[t])
        for s in range(4):
            ups[s, t * PART : (t + 1) * PART, :] = shifted[s * PART : (s + 1) * PART]
        near = dot_nn(rim_at_ref[t], cs[t]).astype(BF)
        for s in range(len(RIM_TAPS)):
            rims[s, t * RIM_ROWS : (t + 1) * RIM_ROWS, :] = near[s * RIM_ROWS : (s + 1) * RIM_ROWS]
    for copy in copies:
        copy.wait()
    pre = dot_nn(wins[...], wf[...].reshape(9 * C, C))
    ups_low = [ups[s].astype(BF) for s in range(4)]
    blocks = (
        dot_nt(ups_low[0], wd[4]),
        dot_nt(ups_low[1], wd[3]) + dot_nt(ups_low[0], wd[5]),
        dot_nt(ups_low[2], wd[1]) + dot_nt(ups_low[0], wd[7]),
        dot_nt(ups_low[3], wd[0]) + dot_nt(ups_low[2], wd[2]) + dot_nt(ups_low[1], wd[6]) + dot_nt(ups_low[0], wd[8]),
    )
    rim = dot_nt(rims[0], wd[RIM_TAPS[0]])
    for s in range(1, len(RIM_TAPS)):
        rim = rim + dot_nt(rims[s], wd[RIM_TAPS[s]])
    rim = rim.astype(BF)
    scale = np.float32(np.sqrt(2 / np.pi))
    squared = pre * pre
    bent = jnp.tanh(scale * (pre + np.float32(0.044715) * squared * pre))
    gate = 0.5 * (1.0 + bent)
    hidden = (pre * gate).astype(BF)
    slope = gate + 0.5 * pre * (1.0 - bent * bent) * scale * (1.0 + np.float32(3 * 0.044715) * squared)

    for t in range(TILES_HERE):
        own_hidden = hidden[t * PRE_ROWS : (t + 1) * PRE_ROWS]
        windows = dot_nn(down_ref[...], own_hidden).astype(BF)
        for k in range(9):
            downs[t * DOWN_ROWS : (t + 1) * DOWN_ROWS, k * C : (k + 1) * C] = windows[k * DOWN_ROWS : (k + 1) * DOWN_ROWS]
        up[t * DOWN_ROWS : (t + 1) * DOWN_ROWS, :] = dot_nn(order_ref[...], cs[t]).astype(BF)

        grad_hidden = jnp.concatenate([block[t * PART : (t + 1) * PART] for block in blocks], axis=0)
        grad_hidden = grad_hidden + dot_nn(rim_ref[...], rim[t * RIM_ROWS : (t + 1) * RIM_ROWS])
        grad_pre = (grad_hidden * slope[t * PRE_ROWS : t * PRE_ROWS + INNER]).astype(BF)
        gps[t * PRE_ROWS : t * PRE_ROWS + INNER, :] = grad_pre
        gps[t * PRE_ROWS + INNER : (t + 1) * PRE_ROWS, :] = jnp.zeros((PRE_ROWS - INNER, C), BF)
        gp_ref[t] = dot_nn(dot_nt(pick, grad_pre).astype(BF), cell_ref[...]).astype(BF)

    lanes = pl.multiple_of((chan // 2) * 128, 128)
    for k in range(9):
        for base, left, right in ((0, wins, gps), (9 * CH, downs, up)):
            both = dot_tn(left[:, pl.ds(k * C + lanes, 128)], right[...])
            part = jnp.where(chan % 2 == 0, both[:CH], both[CH:]).astype(BF)
            for h in range(CORE):
                grads_ref[h, base + k * CH : base + (k + 1) * CH, :] = part[:, h * 128 : (h + 1) * 128]
    coarse = dot_nt(dot_nn(downs[...], wd[...].reshape(9 * C, C)).astype(BF), pick).astype(BF)
    for t in range(TILES_HERE):
        coarse_ref[t] = coarse[t * DOWN_ROWS : t * DOWN_ROWS + COARSE]


def vmem(count):
    return [pl.BlockSpec(memory_space=pltpu.VMEM)] * count


def hbm(count):
    return [pl.BlockSpec(memory_space=pltpu.HBM)] * count


def smem(count):
    return [pl.BlockSpec(memory_space=pltpu.SMEM)] * count


LIMIT = pltpu.CompilerParams(vmem_limit_bytes=48 * 1024 * 1024)
WHOLE = pltpu.CompilerParams(vmem_limit_bytes=60 * 1024 * 1024)
MOST = pltpu.CompilerParams(vmem_limit_bytes=52 * 1024 * 1024)


def tiles_call(payload, window, rim_at, weights):
    constants = (shift_selector(), down_selector(), rim_selector(), order_selector(), cell_selector())
    return pl.pallas_call(
        main_kernel,
        out_shape=(
            jax.ShapeDtypeStruct((TILES_HERE, COARSE, CH), BF),
            jax.ShapeDtypeStruct((TILES_HERE, CH, CELLS), BF),
            jax.ShapeDtypeStruct((CORE, 18 * CH, 128), BF),
        ),
        in_specs=vmem(7) + hbm(2),
        out_specs=tuple(vmem(3)),
        scratch_shapes=[
            pltpu.VMEM((TILES_HERE, 9 * PRE_ROWS, C), BF),
            pltpu.VMEM((TILES_HERE, C, C), BF),
            pltpu.VMEM((TILES_HERE, 2 * C_HALF, C), BF),
            pltpu.VMEM((9, C, C), BF),
            pltpu.VMEM((9, C, C), BF),
            pltpu.VMEM((TILES_HERE * PRE_ROWS, 9 * C), BF),
            pltpu.VMEM((4, TILES_HERE * PART, C), F32),
            pltpu.VMEM((len(RIM_TAPS), TILES_HERE * RIM_ROWS, C), BF),
            pltpu.VMEM((TILES_HERE * DOWN_ROWS, 9 * C), BF),
            pltpu.VMEM((TILES_HERE * PRE_ROWS, C), BF),
            pltpu.VMEM((TILES_HERE * DOWN_ROWS, C), BF),
            pltpu.SemaphoreType.DMA((2 * CHAN + TILES_HERE,)),
        ],
        compiler_params=MOST,
        name="tiles",
    )(payload, rim_at, *(jnp.asarray(array, BF) for array in constants), window, weights)


def shards(fields, seam_table, w_first, w_down, cotangent):
    coords = [lax.axis_index(axis) for axis in ("ylo", "x", "z", "core")]
    own, units, half = pl.pallas_call(
        pack_kernel,
        out_shape=(
            jax.ShapeDtypeStruct((TILES_HERE, PACK_ROWS, 128), BF),
            jax.ShapeDtypeStruct((YX, TILES_HERE * 4 * UNIT, 128), BF),
            jax.ShapeDtypeStruct(w_first.shape, BF),
        ),
        in_specs=hbm(4),
        out_specs=tuple(vmem(1) + hbm(2)),
        scratch_shapes=[
            pltpu.VMEM((TILES_HERE, CH, CELLS), BF),
            pltpu.VMEM((TILES_HERE, COARSE, CH), BF),
            pltpu.VMEM((9, CH, C), BF),
            pltpu.VMEM((TILES_HERE * 4 * UNIT, 128), BF),
            pltpu.SemaphoreType.DMA((4 + YX,)),
        ],
        compiler_params=WHOLE,
        name="pack",
    )(fields, jnp.swapaxes(cotangent, 1, 2), w_first, w_down)
    weights = lax.all_gather(half, ("chan", "core"), axis=0, tiled=False)
    units = lax.all_to_all(units, ("ylo", "x"), 0, 0).reshape(-1, 128)
    units = lax.all_gather(units, "core", axis=0, tiled=True)
    words, beyond = edge_words(seam_table)
    sends = pl.pallas_call(
        place_kernel,
        out_shape=jax.ShapeDtypeStruct((NZ, SEND_ROWS, 128), BF),
        in_specs=smem(2) + vmem(1),
        out_specs=vmem(1)[0],
        scratch_shapes=[pltpu.VMEM((NZ, SEND_ROWS, 128), F32)],
        compiler_params=LIMIT,
        name="place",
    )(words, beyond, units)
    got = lax.all_to_all(sends, "z", 0, 0)
    joined = pl.pallas_call(
        join_kernel,
        out_shape=jax.ShapeDtypeStruct((CHAN, TILES_HERE * PAY_ROWS, 128), BF),
        in_specs=vmem(2),
        out_specs=vmem(1)[0],
        scratch_shapes=[pltpu.VMEM((TILES_HERE * PAY_ROWS, 128), F32)],
        compiler_params=LIMIT,
        name="join",
    )(got, own)
    payload = lax.all_to_all(joined, "chan", 0, 0)

    tile_at = ((coords[0] * NX + coords[1]) * NZ + coords[2]) * CORE + coords[3]
    own_table = lax.dynamic_slice_in_dim(seam_table, tile_at * TILES_HERE, TILES_HERE, 0)
    code = own_table[:, :, 1] * 2 + own_table[:, :, 2]
    chosen = (code[:, :, None] == jnp.arange(8, dtype=jnp.int32)).astype(BF).reshape(TILES_HERE, 32)
    one_hots = []
    for (fixed, varied), depth in ((window_index(), C), (rim_index(), 2 * C_HALF)):
        at = jnp.dot(chosen, jnp.asarray(varied, BF), preferred_element_type=F32) + jnp.asarray(fixed, F32)
        one_hots.append((at[:, :, None] == jnp.arange(1, depth + 1, dtype=jnp.int32).astype(F32)).astype(BF))

    coarse, grad_pre, grads = tiles_call(payload, one_hots[0], one_hots[1], weights)

    part = lax.all_gather(grads, "core", axis=0, tiled=False)
    part = lax.dynamic_index_in_dim(part, coords[3], 1, keepdims=False)
    part = (part[0].astype(F32) + part[1].astype(F32)).astype(BF).reshape(YX, 144, 128)
    part = lax.all_to_all(part, ("ylo", "x"), 0, 0)
    part = part.astype(F32).sum(0).astype(BF)
    part = lax.all_to_all(jnp.broadcast_to(part[None], (NZ, 144, 128)), "z", 0, 0)
    part = part.astype(F32).sum(0).astype(BF)
    part = lax.all_to_all(jnp.broadcast_to(part[None], (YX, 144, 128)), ("ylo", "x"), 0, 0)
    whole = lax.all_gather(part.reshape(18 * CH, 128), "core", axis=0, tiled=False)
    whole = jnp.concatenate([whole[0], whole[1]], axis=1).astype(F32).reshape(2, 9, CH, C)
    tiles = TILES_HERE * PLANE * CORE
    return (
        jnp.swapaxes(coarse, 1, 2),
        whole[0] * float(tiles * CELLS) ** (-0.5),
        whole[1] * float(tiles * COARSE) ** (-0.5),
        grad_pre,
    )


def solution(mesh):
    fine = Mesh(mesh.devices.reshape(YLO, NX, NZ, CORE, CHAN), ("ylo", "x", "z", "core", "chan"))
    return jax.shard_map(
        shards,
        mesh=fine,
        in_specs=(
            P(TILE_AXES, "chan", None),
            P(),
            P(None, "chan", None),
            P(None, "chan", None),
            P(TILE_AXES, "chan", None),
        ),
        out_specs=(
            P(TILE_AXES, "chan", None),
            P(None, "chan", None),
            P(None, "chan", None),
            P(TILE_AXES, "chan", None),
        ),
        check_vma=False,
    )
```

```python
import numpy as np
import jax
import jax.numpy as jnp
from jax import lax
from jax.experimental import pallas as pl
from jax.experimental.pallas import tpu as pltpu
from jax.sharding import Mesh, PartitionSpec as P

S = 12
HALF = 6
CELLS = 144
COARSE = 36
TILES_HERE = 3
CH = 64
C = 256
YLO, NX, NZ, CORE, CHAN = 2, 4, 8, 2, 4
YX = YLO * NX
NEAR = YX * CORE
PLANE = YX * NZ
TILE_AXES = ("ylo", "x", "z", "core")
BF = jnp.bfloat16
F32 = jnp.float32

EDGE_ROWS = (0, 28, 14, 34)
FIELD_ROWS = 40
BLOCK_ROWS = 52
SEND_ROWS = 160
OWN_ROWS = 72
X_HALF = OWN_ROWS + FIELD_ROWS
C_OWN = 18
C_HALF = 32
PAY_ROWS = X_HALF + C_HALF
PACK_ROWS = 96
UNIT = 16
PART = 40
INNER = 4 * PART
PRE_ROWS = INNER + 32
DOWN_ROWS = 48
RIM_ROWS = 48
RIM_TAPS = (0, 1, 2, 3, 6)


def strip_cells(edge, depth):
    if edge == 0:
        return [depth * S + i for i in range(S)]
    if edge == 1:
        return [(S - 1 - depth) * S + i for i in range(S)]
    if edge == 2:
        return [i * S + depth for i in range(S)]
    return [i * S + S - 1 - depth for i in range(S)]


def cell_row(row, col):
    return (row % 2 * 2 + col % 2) * PART + row // 2 * HALF + col // 2


def own_at(cell):
    return cell // 2 + X_HALF * (cell % 2)


def near_at(edge, along, depth):
    row = OWN_ROWS + EDGE_ROWS[edge] + 6 * depth
    if along < 0:
        return OWN_ROWS + EDGE_ROWS[edge] + 12 + X_HALF * depth
    if along >= S:
        return OWN_ROWS + EDGE_ROWS[edge] + 13 + X_HALF * depth
    return row + along // 2 + X_HALF * (along % 2)


def window_index():
    fixed = np.zeros((9, PRE_ROWS), np.float32)
    varied = np.zeros((4, 4, 2, 9, PRE_ROWS), np.float32)
    for k in range(9):
        a, b = k // 3, k % 3
        for cell in range(CELLS):
            row, col = cell // S + a, cell % S + b
            inner_row, inner_col = 1 <= row <= S, 1 <= col <= S
            if inner_row and inner_col:
                fixed[k, cell_row(cell // S, cell % S)] = 1 + own_at((row - 1) * S + col - 1)
            elif inner_row or inner_col:
                edge = (2 if col == 0 else 3) if inner_row else (0 if row == 0 else 1)
                at = row - 1 if inner_row else col - 1
                for flip in range(2):
                    varied[edge, :, flip, k, cell_row(cell // S, cell % S)] = 1 + near_at(
                        edge, 11 - at if flip else at, 0
                    )
        for slot, edge in enumerate((0, 2)):
            own = strip_cells(edge, 0)
            for facing in range(4):
                depth = (a - 1, 1 - a, b - 1, 1 - b)[facing]
                shift = (b - 1, b - 1, a - 1, a - 1)[facing]
                for flip in range(2):
                    for j in range(S):
                        along = (11 - j if flip else j) + shift
                        if depth >= 0:
                            at = near_at(edge, along, depth)
                        elif 0 <= along < S:
                            at = own_at(own[11 - along if flip else along])
                        else:
                            continue
                        varied[edge, facing, flip, k, INNER + 16 * slot + j] = 1 + at
    return fixed.reshape(-1), varied.reshape(32, -1)


def rim_index():
    varied = np.zeros((4, 4, 2, len(RIM_TAPS), RIM_ROWS), np.float32)
    for slot, k in enumerate(RIM_TAPS):
        a, b = k // 3, k % 3
        for edge in range(4):
            for flip in range(2):
                for j in range(S):
                    for facing, live, tap in ((0, a == 0, b), (2, b == 0, a)):
                        at = (11 - j if flip else j) + 1 - tap
                        if live and at % 2 == 0 and 0 <= at < S:
                            at //= 2
                            varied[edge, facing, flip, slot, edge * S + j] = (
                                1 + C_OWN + 3 * edge + at // 2 + C_HALF * (at % 2)
                            )
    return np.zeros(len(RIM_TAPS) * RIM_ROWS, np.float32), varied.reshape(32, -1)


def shift_selector():
    chosen = np.zeros((2, 2, PART, 2 * C_HALF), np.float32)
    for down in range(2):
        for right in range(2):
            for row in range(HALF - down):
                for col in range(HALF - right):
                    at = (row + down) * HALF + col + right
                    chosen[down, right, row * HALF + col, at // 2 + C_HALF * (at % 2)] = 1
    return chosen.reshape(INNER, 2 * C_HALF)


def down_selector():
    chosen = np.zeros((9, DOWN_ROWS, PRE_ROWS), np.float32)
    for k in range(9):
        for cell in range(COARSE):
            row, col = 2 * (cell // HALF) + k // 3, 2 * (cell % HALF) + k % 3
            if row == 0 and col == 0:
                continue
            if row == 0:
                at = INNER + col - 1
            elif col == 0:
                at = INNER + 16 + row - 1
            else:
                at = cell_row(row - 1, col - 1)
            chosen[k, cell, at] = 1
    return chosen.reshape(9 * DOWN_ROWS, PRE_ROWS)


def rim_selector():
    chosen = np.zeros((INNER, RIM_ROWS), np.float32)
    for edge in range(4):
        for j, cell in enumerate(strip_cells(edge, 0)):
            chosen[cell_row(cell // S, cell % S), edge * S + j] = 1
    return chosen


def cell_selector():
    chosen = np.zeros((INNER, CELLS), np.float32)
    for cell in range(CELLS):
        chosen[cell_row(cell // S, cell % S), cell] = 1
    return chosen


def order_selector():
    chosen = np.zeros((DOWN_ROWS, 2 * C_HALF), np.float32)
    for cell in range(COARSE):
        chosen[cell, cell // 2 + C_HALF * (cell % 2)] = 1
    return chosen


def dot_nn(left, right):
    return lax.dot_general(left, right, (((1,), (0,)), ((), ())), preferred_element_type=F32)


def dot_tn(left, right):
    return lax.dot_general(left, right, (((0,), (0,)), ((), ())), preferred_element_type=F32)


def dot_nt(left, right):
    return lax.dot_general(left, right, (((1,), (1,)), ((), ())), preferred_element_type=F32)


def pack_selectors(half):
    rows = PACK_ROWS + 4 * UNIT
    row = lax.broadcasted_iota(jnp.int32, (rows, CELLS), 0)
    at = lax.broadcasted_iota(jnp.int32, (rows, CELLS), 1)
    edge, j = (row - PACK_ROWS) >> 4, (row - PACK_ROWS) & 15
    deep = jnp.where(jnp.logical_and(j >= 9, j < 15), 1, 0)
    along = jnp.where(j < 6, 2 * j + half, jnp.where(j < 15, 2 * (j - 9) + half, 11 - half))
    start = jnp.where(edge == 0, S * deep, jnp.where(edge == 1, S * (S - 1 - deep), jnp.where(edge == 2, deep, S - 1 - deep)))
    cell = start + along * jnp.where(edge < 2, 1, S)
    cell = jnp.where(jnp.logical_or(j < 6, j >= 9), cell, -1)
    cell = jnp.where(row < OWN_ROWS, 2 * row + half, jnp.where(row < PACK_ROWS, -1, cell))
    fields = jnp.where(at == cell, 1.0, 0.0).astype(BF)
    row, at, edge, j = row[:, :COARSE], at[:, :COARSE], edge[:, :COARSE], j[:, :COARSE]
    cell = (2 * (j - 6) + half) * jnp.where(edge == 0, 1, HALF)
    live = jnp.logical_and(jnp.logical_and(j >= 6, j < 9), jnp.logical_or(edge == 0, edge == 2))
    cell = jnp.where(live, cell, -1)
    own = jnp.where(row < OWN_ROWS + C_OWN, 2 * (row - OWN_ROWS) + half, -1)
    cell = jnp.where(row < PACK_ROWS, own, cell)
    return fields, jnp.where(at == cell, 1.0, 0.0).astype(BF)


def pack_kernel(fields_hbm, cot_hbm, first_ref, down_ref, own_ref, unit_hbm, half_ref, fields_ref, cot_ref, held, unit_ref, sems):
    loads = [
        pltpu.make_async_copy(fields_hbm, fields_ref, sems.at[0]),
        pltpu.make_async_copy(cot_hbm, cot_ref, sems.at[1]),
    ]
    for load in loads:
        load.start()
    core = lax.axis_index("core")

    @pl.when(core == 0)
    def _():
        pltpu.make_async_copy(first_ref, held, sems.at[2]).start()

    @pl.when(core == 1)
    def _():
        pltpu.make_async_copy(down_ref, held, sems.at[2]).start()

    chosen = [pack_selectors(h) for h in range(2)]
    for load in loads:
        load.wait()
    for t in range(TILES_HERE):
        halves = [(dot_nt(f, fields_ref[t]) + dot_nn(c, cot_ref[t])).astype(BF) for f, c in chosen]
        for h in range(2):
            own_ref[t, :, h * CH : (h + 1) * CH] = halves[h][:PACK_ROWS]
            unit_ref[t * 4 * UNIT : (t + 1) * 4 * UNIT, h * CH : (h + 1) * CH] = halves[h][PACK_ROWS:]
    pltpu.make_async_copy(first_ref, held, sems.at[2]).wait()
    stores = [pltpu.make_async_copy(held, half_ref, sems.at[3])]
    for copy in range(YX):
        stores.append(pltpu.make_async_copy(unit_ref, unit_hbm.at[copy], sems.at[4 + copy]))
    for store in stores:
        store.start()
    for store in stores:
        store.wait()


def edge_words(seam_table):
    n, f, r = seam_table[:, :, 0], seam_table[:, :, 1], seam_table[:, :, 2]
    device = n // TILES_HERE
    group = (device % CORE) * YX + device // (NZ * CORE)
    unit = (group * TILES_HERE + n % TILES_HERE) * 4 + f
    z = (device // CORE) % NZ
    word = unit + r * 256 + z * 512
    beyond = (n * 4 + jnp.where(f < 2, 2, 0)) * 2 + f % 2
    return word.reshape(-1), beyond.reshape(-1)


def place_kernel(word_ref, beyond_ref, unit_ref, out_ref, sent):
    ylo, x, z, core = (lax.axis_index(axis) for axis in TILE_AXES)

    def unit_at(word):
        keep = jnp.where((word >> 9) == z, 1.0, 0.0).astype(F32)
        at = pl.multiple_of((word & 255) * UNIT, UNIT)
        return unit_ref[pl.ds(at, UNIT), :].astype(F32) * keep

    def body(z_to, carry):
        device = ((ylo * NX + x) * NZ + z_to) * CORE + core
        for t in range(TILES_HERE):
            for edge in range(4):
                at = (device * TILES_HERE + t) * 4 + edge
                unit = unit_at(word_ref[at])
                row = t * BLOCK_ROWS + EDGE_ROWS[edge]
                cot = t * BLOCK_ROWS + FIELD_ROWS + 3 * edge
                sent[z_to, row : row + 6, :] = unit[0:6]
                sent[z_to, cot : cot + 3, :] = unit[6:9]
                if edge % 2 == 0:
                    sent[z_to, row + 6 : row + 12, :] = unit[9:15]
                    beyond = beyond_ref[at]
                    for last in range(2):
                        word = word_ref[(beyond >> 1) + last]
                        end = unit_at(word)
                        low = ((beyond + (word >> 8)) & 1) == 0
                        sent[z_to, row + 12 + last : row + 13 + last, :] = jnp.where(low, end[0:1], end[15:16])
        sent[z_to, TILES_HERE * BLOCK_ROWS :, :] = jnp.zeros((SEND_ROWS - TILES_HERE * BLOCK_ROWS, 128), F32)
        return carry

    lax.fori_loop(0, NZ, body, 0)
    out_ref[...] = sent[...].astype(BF)


def join_kernel(got_ref, own_ref, out_ref, rows):
    total = got_ref[0].astype(F32)
    for q in range(1, NZ):
        total = total + got_ref[q].astype(F32)
    for t in range(TILES_HERE):
        base, block = t * PAY_ROWS, t * BLOCK_ROWS
        own = own_ref[t].astype(F32)
        rows[base : base + OWN_ROWS, :] = own[:OWN_ROWS]
        rows[base + OWN_ROWS : base + X_HALF, :] = total[block : block + FIELD_ROWS]
        rows[base + X_HALF : base + X_HALF + C_OWN, :] = own[OWN_ROWS : OWN_ROWS + C_OWN]
        rows[base + X_HALF + C_OWN : base + PAY_ROWS - 2, :] = total[block + FIELD_ROWS : block + BLOCK_ROWS]
        rows[base + PAY_ROWS - 2 : base + PAY_ROWS, :] = jnp.zeros((2, 128), F32)
    whole = rows[...].astype(BF)
    for c in range(CHAN):
        out_ref[c] = whole


def main_kernel(
    pay_ref, rim_at_ref, shift_ref, down_ref, rim_ref, order_ref, cell_ref, window_hbm, weights_ref,
    coarse_ref, gp_ref, grads_ref, window_ref, xs, cs, wf, wd, wins, ups, rims, downs, gps, up, sems,
):
    window_copies = [
        pltpu.make_async_copy(window_hbm.at[t], window_ref.at[t], sems.at[2 * CHAN + t]) for t in range(TILES_HERE)
    ]
    for copy in window_copies:
        copy.start()
    copies = []
    for which, held in enumerate((wf, wd)):
        for c in range(CHAN):
            copies.append(
                pltpu.make_async_copy(
                    weights_ref.at[2 * c + which], held.at[:, pl.ds(c * CH, CH), :], sems.at[2 * c + which]
                )
            )
    for copy in copies:
        copy.start()
    chan = lax.axis_index("chan")
    pick = jnp.where(
        lax.broadcasted_iota(jnp.int32, (CH, C), 1) == lax.broadcasted_iota(jnp.int32, (CH, C), 0) + chan * CH, 1.0, 0.0
    ).astype(BF)
    for c in range(CHAN):
        for t in range(TILES_HERE):
            base = t * PAY_ROWS
            for h in range(2):
                lanes = slice(h * CH, (h + 1) * CH)
                xs[t, h * X_HALF : (h + 1) * X_HALF, c * CH : (c + 1) * CH] = pay_ref[c, base : base + X_HALF, lanes]
                cs[t, h * C_HALF : (h + 1) * C_HALF, c * CH : (c + 1) * CH] = pay_ref[
                    c, base + X_HALF : base + PAY_ROWS, lanes
                ]
    for t in range(TILES_HERE):
        xs[t, 2 * X_HALF :, :] = jnp.zeros((C - 2 * X_HALF, C), BF)
    for t in range(TILES_HERE):
        window_copies[t].wait()
        for k in range(9):
            wins[t * PRE_ROWS : (t + 1) * PRE_ROWS, k * C : (k + 1) * C] = dot_nn(
                window_ref[t, k * PRE_ROWS : (k + 1) * PRE_ROWS, :], xs[t]
            ).astype(BF)
        shifted = dot_nn(shift_ref[...], cs[t])
        for s in range(4):
            ups[s, t * PART : (t + 1) * PART, :] = shifted[s * PART : (s + 1) * PART]
        near = dot_nn(rim_at_ref[t], cs[t]).astype(BF)
        for s in range(len(RIM_TAPS)):
            rims[s, t * RIM_ROWS : (t + 1) * RIM_ROWS, :] = near[s * RIM_ROWS : (s + 1) * RIM_ROWS]
    for copy in copies:
        copy.wait()
    pre = dot_nn(wins[...], wf[...].reshape(9 * C, C))
    ups_low = [ups[s].astype(BF) for s in range(4)]
    blocks = (
        dot_nt(ups_low[0], wd[4]),
        dot_nt(ups_low[1], wd[3]) + dot_nt(ups_low[0], wd[5]),
        dot_nt(ups_low[2], wd[1]) + dot_nt(ups_low[0], wd[7]),
        dot_nt(ups_low[3], wd[0]) + dot_nt(ups_low[2], wd[2]) + dot_nt(ups_low[1], wd[6]) + dot_nt(ups_low[0], wd[8]),
    )
    rim = dot_nt(rims[0], wd[RIM_TAPS[0]])
    for s in range(1, len(RIM_TAPS)):
        rim = rim + dot_nt(rims[s], wd[RIM_TAPS[s]])
    rim = rim.astype(BF)
    scale = np.float32(np.sqrt(2 / np.pi))
    squared = pre * pre
    bent = jnp.tanh(scale * (pre + np.float32(0.044715) * squared * pre))
    gate = 0.5 * (1.0 + bent)
    hidden = (pre * gate).astype(BF)
    slope = gate + 0.5 * pre * (1.0 - bent * bent) * scale * (1.0 + np.float32(3 * 0.044715) * squared)

    for t in range(TILES_HERE):
        own_hidden = hidden[t * PRE_ROWS : (t + 1) * PRE_ROWS]
        windows = dot_nn(down_ref[...], own_hidden).astype(BF)
        for k in range(9):
            downs[t * DOWN_ROWS : (t + 1) * DOWN_ROWS, k * C : (k + 1) * C] = windows[k * DOWN_ROWS : (k + 1) * DOWN_ROWS]
        up[t * DOWN_ROWS : (t + 1) * DOWN_ROWS, :] = dot_nn(order_ref[...], cs[t]).astype(BF)

        grad_hidden = jnp.concatenate([block[t * PART : (t + 1) * PART] for block in blocks], axis=0)
        grad_hidden = grad_hidden + dot_nn(rim_ref[...], rim[t * RIM_ROWS : (t + 1) * RIM_ROWS])
        grad_pre = (grad_hidden * slope[t * PRE_ROWS : t * PRE_ROWS + INNER]).astype(BF)
        gps[t * PRE_ROWS : t * PRE_ROWS + INNER, :] = grad_pre
        gps[t * PRE_ROWS + INNER : (t + 1) * PRE_ROWS, :] = jnp.zeros((PRE_ROWS - INNER, C), BF)
        gp_ref[t] = dot_nn(dot_nt(pick, grad_pre).astype(BF), cell_ref[...]).astype(BF)

    lanes = pl.multiple_of((chan // 2) * 128, 128)
    for k in range(9):
        for base, left, right in ((0, wins, gps), (9 * CH, downs, up)):
            both = dot_tn(left[:, pl.ds(k * C + lanes, 128)], right[...])
            part = jnp.where(chan % 2 == 0, both[:CH], both[CH:]).astype(BF)
            for h in range(CORE):
                grads_ref[h, base + k * CH : base + (k + 1) * CH, :] = part[:, h * 128 : (h + 1) * 128]
    coarse = dot_nt(dot_nn(downs[...], wd[...].reshape(9 * C, C)).astype(BF), pick).astype(BF)
    for t in range(TILES_HERE):
        coarse_ref[t] = coarse[t * DOWN_ROWS : t * DOWN_ROWS + COARSE]


def vmem(count):
    return [pl.BlockSpec(memory_space=pltpu.VMEM)] * count


def hbm(count):
    return [pl.BlockSpec(memory_space=pltpu.HBM)] * count


def smem(count):
    return [pl.BlockSpec(memory_space=pltpu.SMEM)] * count


LIMIT = pltpu.CompilerParams(vmem_limit_bytes=48 * 1024 * 1024)
WHOLE = pltpu.CompilerParams(vmem_limit_bytes=60 * 1024 * 1024)
MOST = pltpu.CompilerParams(vmem_limit_bytes=52 * 1024 * 1024)


def tiles_call(payload, window, rim_at, weights):
    constants = (shift_selector(), down_selector(), rim_selector(), order_selector(), cell_selector())
    return pl.pallas_call(
        main_kernel,
        out_shape=(
            jax.ShapeDtypeStruct((TILES_HERE, COARSE, CH), BF),
            jax.ShapeDtypeStruct((TILES_HERE, CH, CELLS), BF),
            jax.ShapeDtypeStruct((CORE, 18 * CH, 128), BF),
        ),
        in_specs=vmem(7) + hbm(2),
        out_specs=tuple(vmem(3)),
        scratch_shapes=[
            pltpu.VMEM((TILES_HERE, 9 * PRE_ROWS, C), BF),
            pltpu.VMEM((TILES_HERE, C, C), BF),
            pltpu.VMEM((TILES_HERE, 2 * C_HALF, C), BF),
            pltpu.VMEM((9, C, C), BF),
            pltpu.VMEM((9, C, C), BF),
            pltpu.VMEM((TILES_HERE * PRE_ROWS, 9 * C), BF),
            pltpu.VMEM((4, TILES_HERE * PART, C), F32),
            pltpu.VMEM((len(RIM_TAPS), TILES_HERE * RIM_ROWS, C), BF),
            pltpu.VMEM((TILES_HERE * DOWN_ROWS, 9 * C), BF),
            pltpu.VMEM((TILES_HERE * PRE_ROWS, C), BF),
            pltpu.VMEM((TILES_HERE * DOWN_ROWS, C), BF),
            pltpu.SemaphoreType.DMA((2 * CHAN + TILES_HERE,)),
        ],
        compiler_params=MOST,
        name="tiles",
    )(payload, rim_at, *(jnp.asarray(array, BF) for array in constants), window, weights)


def shards(fields, seam_table, w_first, w_down, cotangent):
    coords = [lax.axis_index(axis) for axis in ("ylo", "x", "z", "core")]
    own, units, half = pl.pallas_call(
        pack_kernel,
        out_shape=(
            jax.ShapeDtypeStruct((TILES_HERE, PACK_ROWS, 128), BF),
            jax.ShapeDtypeStruct((YX, TILES_HERE * 4 * UNIT, 128), BF),
            jax.ShapeDtypeStruct(w_first.shape, BF),
        ),
        in_specs=hbm(4),
        out_specs=tuple(vmem(1) + hbm(2)),
        scratch_shapes=[
            pltpu.VMEM((TILES_HERE, CH, CELLS), BF),
            pltpu.VMEM((TILES_HERE, COARSE, CH), BF),
            pltpu.VMEM((9, CH, C), BF),
            pltpu.VMEM((TILES_HERE * 4 * UNIT, 128), BF),
            pltpu.SemaphoreType.DMA((4 + YX,)),
        ],
        compiler_params=WHOLE,
        name="pack",
    )(fields, jnp.swapaxes(cotangent, 1, 2), w_first, w_down)
    weights = lax.all_gather(half, ("chan", "core"), axis=0, tiled=False)
    units = lax.all_to_all(units, ("ylo", "x"), 0, 0).reshape(-1, 128)
    units = lax.all_gather(units, "core", axis=0, tiled=True)
    words, beyond = edge_words(seam_table)
    sends = pl.pallas_call(
        place_kernel,
        out_shape=jax.ShapeDtypeStruct((NZ, SEND_ROWS, 128), BF),
        in_specs=smem(2) + vmem(1),
        out_specs=vmem(1)[0],
        scratch_shapes=[pltpu.VMEM((NZ, SEND_ROWS, 128), F32)],
        compiler_params=LIMIT,
        name="place",
    )(words, beyond, units)
    got = lax.all_to_all(sends, "z", 0, 0)
    joined = pl.pallas_call(
        join_kernel,
        out_shape=jax.ShapeDtypeStruct((CHAN, TILES_HERE * PAY_ROWS, 128), BF),
        in_specs=vmem(2),
        out_specs=vmem(1)[0],
        scratch_shapes=[pltpu.VMEM((TILES_HERE * PAY_ROWS, 128), F32)],
        compiler_params=LIMIT,
        name="join",
    )(got, own)
    payload = lax.all_to_all(joined, "chan", 0, 0)

    tile_at = ((coords[0] * NX + coords[1]) * NZ + coords[2]) * CORE + coords[3]
    own_table = lax.dynamic_slice_in_dim(seam_table, tile_at * TILES_HERE, TILES_HERE, 0)
    code = own_table[:, :, 1] * 2 + own_table[:, :, 2]
    chosen = (code[:, :, None] == jnp.arange(8, dtype=jnp.int32)).astype(BF).reshape(TILES_HERE, 32)
    one_hots = []
    for (fixed, varied), depth in ((window_index(), C), (rim_index(), 2 * C_HALF)):
        at = jnp.dot(chosen, jnp.asarray(varied, BF), preferred_element_type=F32) + jnp.asarray(fixed, F32)
        one_hots.append((at[:, :, None] == jnp.arange(1, depth + 1, dtype=jnp.int32).astype(F32)).astype(BF))

    coarse, grad_pre, grads = tiles_call(payload, one_hots[0], one_hots[1], weights)

    part = lax.all_to_all(grads, "core", 0, 0)
    part = (part[0].astype(F32) + part[1].astype(F32)).astype(BF).reshape(YX, 144, 128)
    part = lax.all_to_all(part, ("ylo", "x"), 0, 0)
    part = part.astype(F32).sum(0).astype(BF)
    part = lax.all_to_all(jnp.broadcast_to(part[None], (NZ, 144, 128)), "z", 0, 0)
    part = part.astype(F32).sum(0).astype(BF)
    part = lax.all_to_all(jnp.broadcast_to(part[None], (YX, 144, 128)), ("ylo", "x"), 0, 0)
    whole = lax.all_gather(part.reshape(18 * CH, 128), "core", axis=0, tiled=False)
    whole = jnp.concatenate([whole[0], whole[1]], axis=1).astype(F32).reshape(2, 9, CH, C)
    tiles = TILES_HERE * PLANE * CORE
    return (
        jnp.swapaxes(coarse, 1, 2),
        whole[0] * float(tiles * CELLS) ** (-0.5),
        whole[1] * float(tiles * COARSE) ** (-0.5),
        grad_pre,
    )


def solution(mesh):
    fine = Mesh(mesh.devices.reshape(YLO, NX, NZ, CORE, CHAN), ("ylo", "x", "z", "core", "chan"))
    return jax.shard_map(
        shards,
        mesh=fine,
        in_specs=(
            P(TILE_AXES, "chan", None),
            P(),
            P(None, "chan", None),
            P(None, "chan", None),
            P(TILE_AXES, "chan", None),
        ),
        out_specs=(
            P(TILE_AXES, "chan", None),
            P(None, "chan", None),
            P(None, "chan", None),
            P(TILE_AXES, "chan", None),
        ),
        check_vma=False,
    )
```

```python
import numpy as np
import jax
import jax.numpy as jnp
from jax import lax
from jax.experimental import pallas as pl
from jax.experimental.pallas import tpu as pltpu
from jax.sharding import Mesh, PartitionSpec as P

S = 12
HALF = 6
CELLS = 144
COARSE = 36
TILES_HERE = 3
CH = 64
C = 256
YLO, NX, NZ, CORE, CHAN = 2, 4, 8, 2, 4
YX = YLO * NX
NEAR = YX * CORE
PLANE = YX * NZ
TILE_AXES = ("ylo", "x", "z", "core")
BF = jnp.bfloat16
F32 = jnp.float32

EDGE_ROWS = (0, 28, 14, 34)
FIELD_ROWS = 40
BLOCK_ROWS = 52
SEND_ROWS = 160
OWN_ROWS = 72
X_HALF = OWN_ROWS + FIELD_ROWS
C_OWN = 18
C_HALF = 32
PAY_ROWS = X_HALF + C_HALF
PACK_ROWS = 96
UNIT = 16
PART = 40
INNER = 4 * PART
PRE_ROWS = INNER + 32
DOWN_ROWS = 48
RIM_ROWS = 48
RIM_TAPS = (0, 1, 2, 3, 6)


def strip_cells(edge, depth):
    if edge == 0:
        return [depth * S + i for i in range(S)]
    if edge == 1:
        return [(S - 1 - depth) * S + i for i in range(S)]
    if edge == 2:
        return [i * S + depth for i in range(S)]
    return [i * S + S - 1 - depth for i in range(S)]


def cell_row(row, col):
    return (row % 2 * 2 + col % 2) * PART + row // 2 * HALF + col // 2


def own_at(cell):
    return cell // 2 + X_HALF * (cell % 2)


def near_at(edge, along, depth):
    row = OWN_ROWS + EDGE_ROWS[edge] + 6 * depth
    if along < 0:
        return OWN_ROWS + EDGE_ROWS[edge] + 12 + X_HALF * depth
    if along >= S:
        return OWN_ROWS + EDGE_ROWS[edge] + 13 + X_HALF * depth
    return row + along // 2 + X_HALF * (along % 2)


def window_index():
    fixed = np.zeros((9, PRE_ROWS), np.float32)
    varied = np.zeros((4, 4, 2, 9, PRE_ROWS), np.float32)
    for k in range(9):
        a, b = k // 3, k % 3
        for cell in range(CELLS):
            row, col = cell // S + a, cell % S + b
            inner_row, inner_col = 1 <= row <= S, 1 <= col <= S
            if inner_row and inner_col:
                fixed[k, cell_row(cell // S, cell % S)] = 1 + own_at((row - 1) * S + col - 1)
            elif inner_row or inner_col:
                edge = (2 if col == 0 else 3) if inner_row else (0 if row == 0 else 1)
                at = row - 1 if inner_row else col - 1
                for flip in range(2):
                    varied[edge, :, flip, k, cell_row(cell // S, cell % S)] = 1 + near_at(
                        edge, 11 - at if flip else at, 0
                    )
        for slot, edge in enumerate((0, 2)):
            own = strip_cells(edge, 0)
            for facing in range(4):
                depth = (a - 1, 1 - a, b - 1, 1 - b)[facing]
                shift = (b - 1, b - 1, a - 1, a - 1)[facing]
                for flip in range(2):
                    for j in range(S):
                        along = (11 - j if flip else j) + shift
                        if depth >= 0:
                            at = near_at(edge, along, depth)
                        elif 0 <= along < S:
                            at = own_at(own[11 - along if flip else along])
                        else:
                            continue
                        varied[edge, facing, flip, k, INNER + 16 * slot + j] = 1 + at
    return fixed.reshape(-1), varied.reshape(32, -1)


def rim_index():
    varied = np.zeros((4, 4, 2, len(RIM_TAPS), RIM_ROWS), np.float32)
    for slot, k in enumerate(RIM_TAPS):
        a, b = k // 3, k % 3
        for edge in range(4):
            for flip in range(2):
                for j in range(S):
                    for facing, live, tap in ((0, a == 0, b), (2, b == 0, a)):
                        at = (11 - j if flip else j) + 1 - tap
                        if live and at % 2 == 0 and 0 <= at < S:
                            at //= 2
                            varied[edge, facing, flip, slot, edge * S + j] = (
                                1 + C_OWN + 3 * edge + at // 2 + C_HALF * (at % 2)
                            )
    return np.zeros(len(RIM_TAPS) * RIM_ROWS, np.float32), varied.reshape(32, -1)


def shift_selector():
    chosen = np.zeros((2, 2, PART, 2 * C_HALF), np.float32)
    for down in range(2):
        for right in range(2):
            for row in range(HALF - down):
                for col in range(HALF - right):
                    at = (row + down) * HALF + col + right
                    chosen[down, right, row * HALF + col, at // 2 + C_HALF * (at % 2)] = 1
    return chosen.reshape(INNER, 2 * C_HALF)


def down_selector():
    chosen = np.zeros((9, DOWN_ROWS, PRE_ROWS), np.float32)
    for k in range(9):
        for cell in range(COARSE):
            row, col = 2 * (cell // HALF) + k // 3, 2 * (cell % HALF) + k % 3
            if row == 0 and col == 0:
                continue
            if row == 0:
                at = INNER + col - 1
            elif col == 0:
                at = INNER + 16 + row - 1
            else:
                at = cell_row(row - 1, col - 1)
            chosen[k, cell, at] = 1
    return chosen.reshape(9 * DOWN_ROWS, PRE_ROWS)


def rim_selector():
    chosen = np.zeros((INNER, RIM_ROWS), np.float32)
    for edge in range(4):
        for j, cell in enumerate(strip_cells(edge, 0)):
            chosen[cell_row(cell // S, cell % S), edge * S + j] = 1
    return chosen


def cell_selector():
    chosen = np.zeros((INNER, CELLS), np.float32)
    for cell in range(CELLS):
        chosen[cell_row(cell // S, cell % S), cell] = 1
    return chosen


def order_selector():
    chosen = np.zeros((DOWN_ROWS, 2 * C_HALF), np.float32)
    for cell in range(COARSE):
        chosen[cell, cell // 2 + C_HALF * (cell % 2)] = 1
    return chosen


def dot_nn(left, right):
    return lax.dot_general(left, right, (((1,), (0,)), ((), ())), preferred_element_type=F32)


def dot_tn(left, right):
    return lax.dot_general(left, right, (((0,), (0,)), ((), ())), preferred_element_type=F32)


def dot_nt(left, right):
    return lax.dot_general(left, right, (((1,), (1,)), ((), ())), preferred_element_type=F32)


def pack_selectors(half):
    rows = PACK_ROWS + 4 * UNIT
    row = lax.broadcasted_iota(jnp.int32, (rows, CELLS), 0)
    at = lax.broadcasted_iota(jnp.int32, (rows, CELLS), 1)
    edge, j = (row - PACK_ROWS) >> 4, (row - PACK_ROWS) & 15
    deep = jnp.where(jnp.logical_and(j >= 9, j < 15), 1, 0)
    along = jnp.where(j < 6, 2 * j + half, jnp.where(j < 15, 2 * (j - 9) + half, 11 - half))
    start = jnp.where(edge == 0, S * deep, jnp.where(edge == 1, S * (S - 1 - deep), jnp.where(edge == 2, deep, S - 1 - deep)))
    cell = start + along * jnp.where(edge < 2, 1, S)
    cell = jnp.where(jnp.logical_or(j < 6, j >= 9), cell, -1)
    cell = jnp.where(row < OWN_ROWS, 2 * row + half, jnp.where(row < PACK_ROWS, -1, cell))
    fields = jnp.where(at == cell, 1.0, 0.0).astype(BF)
    row, at, edge, j = row[:, :COARSE], at[:, :COARSE], edge[:, :COARSE], j[:, :COARSE]
    cell = (2 * (j - 6) + half) * jnp.where(edge == 0, 1, HALF)
    live = jnp.logical_and(jnp.logical_and(j >= 6, j < 9), jnp.logical_or(edge == 0, edge == 2))
    cell = jnp.where(live, cell, -1)
    own = jnp.where(row < OWN_ROWS + C_OWN, 2 * (row - OWN_ROWS) + half, -1)
    cell = jnp.where(row < PACK_ROWS, own, cell)
    return fields, jnp.where(at == cell, 1.0, 0.0).astype(BF)


def pack_kernel(fields_hbm, cot_hbm, first_ref, down_ref, own_hbm, unit_hbm, half_ref, fields_ref, cot_ref, held, unit_ref, own_ref, sems):
    loads = [
        pltpu.make_async_copy(fields_hbm, fields_ref, sems.at[0]),
        pltpu.make_async_copy(cot_hbm, cot_ref, sems.at[1]),
    ]
    for load in loads:
        load.start()
    core = lax.axis_index("core")

    @pl.when(core == 0)
    def _():
        pltpu.make_async_copy(first_ref, held, sems.at[2]).start()

    @pl.when(core == 1)
    def _():
        pltpu.make_async_copy(down_ref, held, sems.at[2]).start()

    chosen = [pack_selectors(h) for h in range(2)]
    for load in loads:
        load.wait()
    for t in range(TILES_HERE):
        halves = [(dot_nt(f, fields_ref[t]) + dot_nn(c, cot_ref[t])).astype(BF) for f, c in chosen]
        for h in range(2):
            own_ref[t, :, h * CH : (h + 1) * CH] = halves[h][:PACK_ROWS]
            unit_ref[t * 4 * UNIT : (t + 1) * 4 * UNIT, h * CH : (h + 1) * CH] = halves[h][PACK_ROWS:]
    pltpu.make_async_copy(first_ref, held, sems.at[2]).wait()
    stores = [pltpu.make_async_copy(held, half_ref, sems.at[3])]
    for copy in range(YX):
        stores.append(pltpu.make_async_copy(unit_ref, unit_hbm.at[copy], sems.at[4 + copy]))
    stores.append(pltpu.make_async_copy(own_ref, own_hbm, sems.at[4 + YX]))
    for store in stores:
        store.start()
    for store in stores:
        store.wait()


def edge_words(seam_table):
    n, f, r = seam_table[:, :, 0], seam_table[:, :, 1], seam_table[:, :, 2]
    device = n // TILES_HERE
    group = (device % CORE) * YX + device // (NZ * CORE)
    unit = (group * TILES_HERE + n % TILES_HERE) * 4 + f
    z = (device // CORE) % NZ
    word = unit + r * 256 + z * 512
    beyond = (n * 4 + jnp.where(f < 2, 2, 0)) * 2 + f % 2
    return word.reshape(-1), beyond.reshape(-1)


def place_kernel(word_ref, beyond_ref, unit_ref, out_ref, sent):
    ylo, x, z, core = (lax.axis_index(axis) for axis in TILE_AXES)

    def unit_at(word):
        keep = jnp.where((word >> 9) == z, 1.0, 0.0).astype(F32)
        at = pl.multiple_of((word & 255) * UNIT, UNIT)
        return unit_ref[pl.ds(at, UNIT), :].astype(F32) * keep

    def body(z_to, carry):
        device = ((ylo * NX + x) * NZ + z_to) * CORE + core
        for t in range(TILES_HERE):
            for edge in range(4):
                at = (device * TILES_HERE + t) * 4 + edge
                unit = unit_at(word_ref[at])
                row = t * BLOCK_ROWS + EDGE_ROWS[edge]
                cot = t * BLOCK_ROWS + FIELD_ROWS + 3 * edge
                sent[z_to, row : row + 6, :] = unit[0:6]
                sent[z_to, cot : cot + 3, :] = unit[6:9]
                if edge % 2 == 0:
                    sent[z_to, row + 6 : row + 12, :] = unit[9:15]
                    beyond = beyond_ref[at]
                    for last in range(2):
                        word = word_ref[(beyond >> 1) + last]
                        end = unit_at(word)
                        low = ((beyond + (word >> 8)) & 1) == 0
                        sent[z_to, row + 12 + last : row + 13 + last, :] = jnp.where(low, end[0:1], end[15:16])
        sent[z_to, TILES_HERE * BLOCK_ROWS :, :] = jnp.zeros((SEND_ROWS - TILES_HERE * BLOCK_ROWS, 128), F32)
        return carry

    lax.fori_loop(0, NZ, body, 0)
    out_ref[...] = sent[...].astype(BF)


def join_kernel(got_ref, own_ref, out_ref, rows):
    total = got_ref[0].astype(F32)
    for q in range(1, NZ):
        total = total + got_ref[q].astype(F32)
    for t in range(TILES_HERE):
        base, block = t * PAY_ROWS, t * BLOCK_ROWS
        own = own_ref[t].astype(F32)
        rows[base : base + OWN_ROWS, :] = own[:OWN_ROWS]
        rows[base + OWN_ROWS : base + X_HALF, :] = total[block : block + FIELD_ROWS]
        rows[base + X_HALF : base + X_HALF + C_OWN, :] = own[OWN_ROWS : OWN_ROWS + C_OWN]
        rows[base + X_HALF + C_OWN : base + PAY_ROWS - 2, :] = total[block + FIELD_ROWS : block + BLOCK_ROWS]
        rows[base + PAY_ROWS - 2 : base + PAY_ROWS, :] = jnp.zeros((2, 128), F32)
    whole = rows[...].astype(BF)
    for c in range(CHAN):
        out_ref[c] = whole


def main_kernel(
    pay_ref, rim_at_ref, shift_ref, down_ref, rim_ref, order_ref, cell_ref, window_hbm, weights_ref,
    coarse_ref, gp_ref, kept_ref, given_ref, window_ref, xs, cs, wf, wd, wins, ups, rims, downs, gps, up, sems,
):
    window_copies = [
        pltpu.make_async_copy(window_hbm.at[t], window_ref.at[t], sems.at[2 * CHAN + t]) for t in range(TILES_HERE)
    ]
    for copy in window_copies:
        copy.start()
    copies = []
    for which, held in enumerate((wf, wd)):
        for c in range(CHAN):
            copies.append(
                pltpu.make_async_copy(
                    weights_ref.at[2 * c + which], held.at[:, pl.ds(c * CH, CH), :], sems.at[2 * c + which]
                )
            )
    for copy in copies:
        copy.start()
    chan, core = lax.axis_index("chan"), lax.axis_index("core")
    pick = jnp.where(
        lax.broadcasted_iota(jnp.int32, (CH, C), 1) == lax.broadcasted_iota(jnp.int32, (CH, C), 0) + chan * CH, 1.0, 0.0
    ).astype(BF)
    for c in range(CHAN):
        for t in range(TILES_HERE):
            base = t * PAY_ROWS
            for h in range(2):
                lanes = slice(h * CH, (h + 1) * CH)
                xs[t, h * X_HALF : (h + 1) * X_HALF, c * CH : (c + 1) * CH] = pay_ref[c, base : base + X_HALF, lanes]
                cs[t, h * C_HALF : (h + 1) * C_HALF, c * CH : (c + 1) * CH] = pay_ref[
                    c, base + X_HALF : base + PAY_ROWS, lanes
                ]
    for t in range(TILES_HERE):
        xs[t, 2 * X_HALF :, :] = jnp.zeros((C - 2 * X_HALF, C), BF)
    for t in range(TILES_HERE):
        window_copies[t].wait()
        for k in range(9):
            wins[t * PRE_ROWS : (t + 1) * PRE_ROWS, k * C : (k + 1) * C] = dot_nn(
                window_ref[t, k * PRE_ROWS : (k + 1) * PRE_ROWS, :], xs[t]
            ).astype(BF)
        shifted = dot_nn(shift_ref[...], cs[t])
        for s in range(4):
            ups[s, t * PART : (t + 1) * PART, :] = shifted[s * PART : (s + 1) * PART]
        near = dot_nn(rim_at_ref[t], cs[t]).astype(BF)
        for s in range(len(RIM_TAPS)):
            rims[s, t * RIM_ROWS : (t + 1) * RIM_ROWS, :] = near[s * RIM_ROWS : (s + 1) * RIM_ROWS]
    for copy in copies:
        copy.wait()
    pre = dot_nn(wins[...], wf[...].reshape(9 * C, C))
    ups_low = [ups[s].astype(BF) for s in range(4)]
    blocks = (
        dot_nt(ups_low[0], wd[4]),
        dot_nt(ups_low[1], wd[3]) + dot_nt(ups_low[0], wd[5]),
        dot_nt(ups_low[2], wd[1]) + dot_nt(ups_low[0], wd[7]),
        dot_nt(ups_low[3], wd[0]) + dot_nt(ups_low[2], wd[2]) + dot_nt(ups_low[1], wd[6]) + dot_nt(ups_low[0], wd[8]),
    )
    rim = dot_nt(rims[0], wd[RIM_TAPS[0]])
    for s in range(1, len(RIM_TAPS)):
        rim = rim + dot_nt(rims[s], wd[RIM_TAPS[s]])
    rim = rim.astype(BF)
    scale = np.float32(np.sqrt(2 / np.pi))
    squared = pre * pre
    bent = jnp.tanh(scale * (pre + np.float32(0.044715) * squared * pre))
    gate = 0.5 * (1.0 + bent)
    hidden = (pre * gate).astype(BF)
    slope = gate + 0.5 * pre * (1.0 - bent * bent) * scale * (1.0 + np.float32(3 * 0.044715) * squared)

    for t in range(TILES_HERE):
        own_hidden = hidden[t * PRE_ROWS : (t + 1) * PRE_ROWS]
        windows = dot_nn(down_ref[...], own_hidden).astype(BF)
        for k in range(9):
            downs[t * DOWN_ROWS : (t + 1) * DOWN_ROWS, k * C : (k + 1) * C] = windows[k * DOWN_ROWS : (k + 1) * DOWN_ROWS]
        up[t * DOWN_ROWS : (t + 1) * DOWN_ROWS, :] = dot_nn(order_ref[...], cs[t]).astype(BF)

        grad_hidden = jnp.concatenate([block[t * PART : (t + 1) * PART] for block in blocks], axis=0)
        grad_hidden = grad_hidden + dot_nn(rim_ref[...], rim[t * RIM_ROWS : (t + 1) * RIM_ROWS])
        grad_pre = (grad_hidden * slope[t * PRE_ROWS : t * PRE_ROWS + INNER]).astype(BF)
        gps[t * PRE_ROWS : t * PRE_ROWS + INNER, :] = grad_pre
        gps[t * PRE_ROWS + INNER : (t + 1) * PRE_ROWS, :] = jnp.zeros((PRE_ROWS - INNER, C), BF)
        gp_ref[t] = dot_nn(dot_nt(pick, grad_pre).astype(BF), cell_ref[...]).astype(BF)

    lanes = pl.multiple_of((chan // 2) * 128, 128)
    for k in range(9):
        for base, left, right in ((0, wins, gps), (9 * CH, downs, up)):
            both = dot_tn(left[:, pl.ds(k * C + lanes, 128)], right[...])
            part = jnp.where(chan % 2 == 0, both[:CH], both[CH:]).astype(BF)
            left_half, right_half = part[:, :128], part[:, 128:]
            rows = slice(base + k * CH, base + (k + 1) * CH)
            kept_ref[rows, :] = jnp.where(core == 0, left_half, right_half)
            given_ref[rows, :] = jnp.where(core == 0, right_half, left_half)
    coarse = dot_nt(dot_nn(downs[...], wd[...].reshape(9 * C, C)).astype(BF), pick).astype(BF)
    for t in range(TILES_HERE):
        coarse_ref[t] = coarse[t * DOWN_ROWS : t * DOWN_ROWS + COARSE]


def vmem(count):
    return [pl.BlockSpec(memory_space=pltpu.VMEM)] * count


def hbm(count):
    return [pl.BlockSpec(memory_space=pltpu.HBM)] * count


def smem(count):
    return [pl.BlockSpec(memory_space=pltpu.SMEM)] * count


LIMIT = pltpu.CompilerParams(vmem_limit_bytes=48 * 1024 * 1024)
WHOLE = pltpu.CompilerParams(vmem_limit_bytes=60 * 1024 * 1024)
MOST = pltpu.CompilerParams(vmem_limit_bytes=52 * 1024 * 1024)


def tiles_call(payload, window, rim_at, weights):
    constants = (shift_selector(), down_selector(), rim_selector(), order_selector(), cell_selector())
    return pl.pallas_call(
        main_kernel,
        out_shape=(
            jax.ShapeDtypeStruct((TILES_HERE, COARSE, CH), BF),
            jax.ShapeDtypeStruct((TILES_HERE, CH, CELLS), BF),
            jax.ShapeDtypeStruct((18 * CH, 128), BF),
            jax.ShapeDtypeStruct((18 * CH, 128), BF),
        ),
        in_specs=vmem(7) + hbm(2),
        out_specs=tuple(vmem(4)),
        scratch_shapes=[
            pltpu.VMEM((TILES_HERE, 9 * PRE_ROWS, C), BF),
            pltpu.VMEM((TILES_HERE, C, C), BF),
            pltpu.VMEM((TILES_HERE, 2 * C_HALF, C), BF),
            pltpu.VMEM((9, C, C), BF),
            pltpu.VMEM((9, C, C), BF),
            pltpu.VMEM((TILES_HERE * PRE_ROWS, 9 * C), BF),
            pltpu.VMEM((4, TILES_HERE * PART, C), F32),
            pltpu.VMEM((len(RIM_TAPS), TILES_HERE * RIM_ROWS, C), BF),
            pltpu.VMEM((TILES_HERE * DOWN_ROWS, 9 * C), BF),
            pltpu.VMEM((TILES_HERE * PRE_ROWS, C), BF),
            pltpu.VMEM((TILES_HERE * DOWN_ROWS, C), BF),
            pltpu.SemaphoreType.DMA((2 * CHAN + TILES_HERE,)),
        ],
        compiler_params=MOST,
        name="tiles",
    )(payload, rim_at, *(jnp.asarray(array, BF) for array in constants), window, weights)


def shards(fields, seam_table, w_first, w_down, cotangent):
    coords = [lax.axis_index(axis) for axis in ("ylo", "x", "z", "core")]
    own, units, half = pl.pallas_call(
        pack_kernel,
        out_shape=(
            jax.ShapeDtypeStruct((TILES_HERE, PACK_ROWS, 128), BF),
            jax.ShapeDtypeStruct((YX, TILES_HERE * 4 * UNIT, 128), BF),
            jax.ShapeDtypeStruct(w_first.shape, BF),
        ),
        in_specs=hbm(4),
        out_specs=tuple(hbm(3)),
        scratch_shapes=[
            pltpu.VMEM((TILES_HERE, CH, CELLS), BF),
            pltpu.VMEM((TILES_HERE, COARSE, CH), BF),
            pltpu.VMEM((9, CH, C), BF),
            pltpu.VMEM((TILES_HERE * 4 * UNIT, 128), BF),
            pltpu.VMEM((TILES_HERE, PACK_ROWS, 128), BF),
            pltpu.SemaphoreType.DMA((5 + YX,)),
        ],
        compiler_params=WHOLE,
        name="pack",
    )(fields, jnp.swapaxes(cotangent, 1, 2), w_first, w_down)
    weights = lax.all_gather(half, ("chan", "core"), axis=0, tiled=False)
    units = lax.all_to_all(units, ("ylo", "x"), 0, 0).reshape(-1, 128)
    units = lax.all_gather(units, "core", axis=0, tiled=True)
    words, beyond = edge_words(seam_table)
    sends = pl.pallas_call(
        place_kernel,
        out_shape=jax.ShapeDtypeStruct((NZ, SEND_ROWS, 128), BF),
        in_specs=smem(2) + vmem(1),
        out_specs=vmem(1)[0],
        scratch_shapes=[pltpu.VMEM((NZ, SEND_ROWS, 128), F32)],
        compiler_params=LIMIT,
        name="place",
    )(words, beyond, units)
    got = lax.all_to_all(sends, "z", 0, 0)
    joined = pl.pallas_call(
        join_kernel,
        out_shape=jax.ShapeDtypeStruct((CHAN, TILES_HERE * PAY_ROWS, 128), BF),
        in_specs=vmem(2),
        out_specs=vmem(1)[0],
        scratch_shapes=[pltpu.VMEM((TILES_HERE * PAY_ROWS, 128), F32)],
        compiler_params=LIMIT,
        name="join",
    )(got, own)
    payload = lax.all_to_all(joined, "chan", 0, 0)

    tile_at = ((coords[0] * NX + coords[1]) * NZ + coords[2]) * CORE + coords[3]
    own_table = lax.dynamic_slice_in_dim(seam_table, tile_at * TILES_HERE, TILES_HERE, 0)
    code = own_table[:, :, 1] * 2 + own_table[:, :, 2]
    chosen = (code[:, :, None] == jnp.arange(8, dtype=jnp.int32)).astype(BF).reshape(TILES_HERE, 32)
    one_hots = []
    for (fixed, varied), depth in ((window_index(), C), (rim_index(), 2 * C_HALF)):
        at = jnp.dot(chosen, jnp.asarray(varied, BF), preferred_element_type=F32) + jnp.asarray(fixed, F32)
        one_hots.append((at[:, :, None] == jnp.arange(1, depth + 1, dtype=jnp.int32).astype(F32)).astype(BF))

    coarse, grad_pre, kept, given = tiles_call(payload, one_hots[0], one_hots[1], weights)

    part = lax.ppermute(given, "core", [(0, 1), (1, 0)])
    part = (kept.astype(F32) + part.astype(F32)).astype(BF).reshape(YX, 144, 128)
    part = lax.all_to_all(part, ("ylo", "x"), 0, 0)
    part = part.astype(F32).sum(0).astype(BF)
    part = lax.all_to_all(jnp.broadcast_to(part[None], (NZ, 144, 128)), "z", 0, 0)
    part = part.astype(F32).sum(0).astype(BF)
    part = lax.all_to_all(jnp.broadcast_to(part[None], (YX, 144, 128)), ("ylo", "x"), 0, 0)
    whole = lax.all_gather(part.reshape(18 * CH, 128), "core", axis=0, tiled=False)
    whole = jnp.concatenate([whole[0], whole[1]], axis=1).astype(F32).reshape(2, 9, CH, C)
    tiles = TILES_HERE * PLANE * CORE
    return (
        jnp.swapaxes(coarse, 1, 2),
        whole[0] * float(tiles * CELLS) ** (-0.5),
        whole[1] * float(tiles * COARSE) ** (-0.5),
        grad_pre,
    )


def solution(mesh):
    fine = Mesh(mesh.devices.reshape(YLO, NX, NZ, CORE, CHAN), ("ylo", "x", "z", "core", "chan"))
    return jax.shard_map(
        shards,
        mesh=fine,
        in_specs=(
            P(TILE_AXES, "chan", None),
            P(),
            P(None, "chan", None),
            P(None, "chan", None),
            P(TILE_AXES, "chan", None),
        ),
        out_specs=(
            P(TILE_AXES, "chan", None),
            P(None, "chan", None),
            P(None, "chan", None),
            P(TILE_AXES, "chan", None),
        ),
        check_vma=False,
    )
```

```python
import numpy as np
import jax
import jax.numpy as jnp
from jax import lax
from jax.experimental import pallas as pl
from jax.experimental.pallas import tpu as pltpu
from jax.sharding import Mesh, PartitionSpec as P

S = 12
HALF = 6
CELLS = 144
COARSE = 36
TILES_HERE = 3
CH = 64
C = 256
YLO, NX, NZ, CORE, CHAN = 2, 4, 8, 2, 4
YX = YLO * NX
NEAR = YX * CORE
PLANE = YX * NZ
TILE_AXES = ("ylo", "x", "z", "core")
BF = jnp.bfloat16
F32 = jnp.float32

EDGE_ROWS = (0, 28, 14, 34)
FIELD_ROWS = 40
BLOCK_ROWS = 52
SEND_ROWS = 160
OWN_ROWS = 72
X_HALF = OWN_ROWS + FIELD_ROWS
C_OWN = 18
C_HALF = 32
PAY_ROWS = X_HALF + C_HALF
PACK_ROWS = 96
UNIT = 16
PART = 40
INNER = 4 * PART
PRE_ROWS = INNER + 32
DOWN_ROWS = 48
RIM_ROWS = 48
RIM_TAPS = (0, 1, 2, 3, 6)


def strip_cells(edge, depth):
    if edge == 0:
        return [depth * S + i for i in range(S)]
    if edge == 1:
        return [(S - 1 - depth) * S + i for i in range(S)]
    if edge == 2:
        return [i * S + depth for i in range(S)]
    return [i * S + S - 1 - depth for i in range(S)]


def cell_row(row, col):
    return (row % 2 * 2 + col % 2) * PART + row // 2 * HALF + col // 2


def own_at(cell):
    return cell // 2 + X_HALF * (cell % 2)


def near_at(edge, along, depth):
    row = OWN_ROWS + EDGE_ROWS[edge] + 6 * depth
    if along < 0:
        return OWN_ROWS + EDGE_ROWS[edge] + 12 + X_HALF * depth
    if along >= S:
        return OWN_ROWS + EDGE_ROWS[edge] + 13 + X_HALF * depth
    return row + along // 2 + X_HALF * (along % 2)


def window_index():
    fixed = np.zeros((9, PRE_ROWS), np.float32)
    varied = np.zeros((4, 4, 2, 9, PRE_ROWS), np.float32)
    for k in range(9):
        a, b = k // 3, k % 3
        for cell in range(CELLS):
            row, col = cell // S + a, cell % S + b
            inner_row, inner_col = 1 <= row <= S, 1 <= col <= S
            if inner_row and inner_col:
                fixed[k, cell_row(cell // S, cell % S)] = 1 + own_at((row - 1) * S + col - 1)
            elif inner_row or inner_col:
                edge = (2 if col == 0 else 3) if inner_row else (0 if row == 0 else 1)
                at = row - 1 if inner_row else col - 1
                for flip in range(2):
                    varied[edge, :, flip, k, cell_row(cell // S, cell % S)] = 1 + near_at(
                        edge, 11 - at if flip else at, 0
                    )
        for slot, edge in enumerate((0, 2)):
            own = strip_cells(edge, 0)
            for facing in range(4):
                depth = (a - 1, 1 - a, b - 1, 1 - b)[facing]
                shift = (b - 1, b - 1, a - 1, a - 1)[facing]
                for flip in range(2):
                    for j in range(S):
                        along = (11 - j if flip else j) + shift
                        if depth >= 0:
                            at = near_at(edge, along, depth)
                        elif 0 <= along < S:
                            at = own_at(own[11 - along if flip else along])
                        else:
                            continue
                        varied[edge, facing, flip, k, INNER + 16 * slot + j] = 1 + at
    return fixed.reshape(-1), varied.reshape(32, -1)


def rim_index():
    varied = np.zeros((4, 4, 2, len(RIM_TAPS), RIM_ROWS), np.float32)
    for slot, k in enumerate(RIM_TAPS):
        a, b = k // 3, k % 3
        for edge in range(4):
            for flip in range(2):
                for j in range(S):
                    for facing, live, tap in ((0, a == 0, b), (2, b == 0, a)):
                        at = (11 - j if flip else j) + 1 - tap
                        if live and at % 2 == 0 and 0 <= at < S:
                            at //= 2
                            varied[edge, facing, flip, slot, edge * S + j] = (
                                1 + C_OWN + 3 * edge + at // 2 + C_HALF * (at % 2)
                            )
    return np.zeros(len(RIM_TAPS) * RIM_ROWS, np.float32), varied.reshape(32, -1)


def shift_selector():
    chosen = np.zeros((2, 2, PART, 2 * C_HALF), np.float32)
    for down in range(2):
        for right in range(2):
            for row in range(HALF - down):
                for col in range(HALF - right):
                    at = (row + down) * HALF + col + right
                    chosen[down, right, row * HALF + col, at // 2 + C_HALF * (at % 2)] = 1
    return chosen.reshape(INNER, 2 * C_HALF)


def down_selector():
    chosen = np.zeros((9, DOWN_ROWS, PRE_ROWS), np.float32)
    for k in range(9):
        for cell in range(COARSE):
            row, col = 2 * (cell // HALF) + k // 3, 2 * (cell % HALF) + k % 3
            if row == 0 and col == 0:
                continue
            if row == 0:
                at = INNER + col - 1
            elif col == 0:
                at = INNER + 16 + row - 1
            else:
                at = cell_row(row - 1, col - 1)
            chosen[k, cell, at] = 1
    return chosen.reshape(9 * DOWN_ROWS, PRE_ROWS)


def rim_selector():
    chosen = np.zeros((INNER, RIM_ROWS), np.float32)
    for edge in range(4):
        for j, cell in enumerate(strip_cells(edge, 0)):
            chosen[cell_row(cell // S, cell % S), edge * S + j] = 1
    return chosen


def cell_selector():
    chosen = np.zeros((INNER, CELLS), np.float32)
    for cell in range(CELLS):
        chosen[cell_row(cell // S, cell % S), cell] = 1
    return chosen


def order_selector():
    chosen = np.zeros((DOWN_ROWS, 2 * C_HALF), np.float32)
    for cell in range(COARSE):
        chosen[cell, cell // 2 + C_HALF * (cell % 2)] = 1
    return chosen


def dot_nn(left, right):
    return lax.dot_general(left, right, (((1,), (0,)), ((), ())), preferred_element_type=F32)


def dot_tn(left, right):
    return lax.dot_general(left, right, (((0,), (0,)), ((), ())), preferred_element_type=F32)


def dot_nt(left, right):
    return lax.dot_general(left, right, (((1,), (1,)), ((), ())), preferred_element_type=F32)


def pack_selectors(half):
    rows = PACK_ROWS + 4 * UNIT
    row = lax.broadcasted_iota(jnp.int32, (rows, CELLS), 0)
    at = lax.broadcasted_iota(jnp.int32, (rows, CELLS), 1)
    edge, j = (row - PACK_ROWS) >> 4, (row - PACK_ROWS) & 15
    deep = jnp.where(jnp.logical_and(j >= 9, j < 15), 1, 0)
    along = jnp.where(j < 6, 2 * j + half, jnp.where(j < 15, 2 * (j - 9) + half, 11 - half))
    start = jnp.where(edge == 0, S * deep, jnp.where(edge == 1, S * (S - 1 - deep), jnp.where(edge == 2, deep, S - 1 - deep)))
    cell = start + along * jnp.where(edge < 2, 1, S)
    cell = jnp.where(jnp.logical_or(j < 6, j >= 9), cell, -1)
    cell = jnp.where(row < OWN_ROWS, 2 * row + half, jnp.where(row < PACK_ROWS, -1, cell))
    fields = jnp.where(at == cell, 1.0, 0.0).astype(BF)
    row, at, edge, j = row[:, :COARSE], at[:, :COARSE], edge[:, :COARSE], j[:, :COARSE]
    cell = (2 * (j - 6) + half) * jnp.where(edge == 0, 1, HALF)
    live = jnp.logical_and(jnp.logical_and(j >= 6, j < 9), jnp.logical_or(edge == 0, edge == 2))
    cell = jnp.where(live, cell, -1)
    own = jnp.where(row < OWN_ROWS + C_OWN, 2 * (row - OWN_ROWS) + half, -1)
    cell = jnp.where(row < PACK_ROWS, own, cell)
    return fields, jnp.where(at == cell, 1.0, 0.0).astype(BF)


def pack_kernel(fields_hbm, cot_hbm, first_ref, down_ref, own_hbm, unit_hbm, half_ref, fields_ref, cot_ref, held, unit_ref, own_ref, sems):
    loads = [
        pltpu.make_async_copy(fields_hbm, fields_ref, sems.at[0]),
        pltpu.make_async_copy(cot_hbm, cot_ref, sems.at[1]),
    ]
    for load in loads:
        load.start()
    core = lax.axis_index("core")

    @pl.when(core == 0)
    def _():
        pltpu.make_async_copy(first_ref, held, sems.at[2]).start()

    @pl.when(core == 1)
    def _():
        pltpu.make_async_copy(down_ref, held, sems.at[2]).start()

    chosen = [pack_selectors(h) for h in range(2)]
    for load in loads:
        load.wait()
    for t in range(TILES_HERE):
        halves = [(dot_nt(f, fields_ref[t]) + dot_nn(c, cot_ref[t])).astype(BF) for f, c in chosen]
        for h in range(2):
            own_ref[t, :, h * CH : (h + 1) * CH] = halves[h][:PACK_ROWS]
            unit_ref[t * 4 * UNIT : (t + 1) * 4 * UNIT, h * CH : (h + 1) * CH] = halves[h][PACK_ROWS:]
    pltpu.make_async_copy(first_ref, held, sems.at[2]).wait()
    stores = [pltpu.make_async_copy(held, half_ref, sems.at[3])]
    for copy in range(YX):
        stores.append(pltpu.make_async_copy(unit_ref, unit_hbm.at[copy], sems.at[4 + copy]))
    stores.append(pltpu.make_async_copy(own_ref, own_hbm, sems.at[4 + YX]))
    for store in stores:
        store.start()
    for store in stores:
        store.wait()


def edge_words(seam_table):
    n, f, r = seam_table[:, :, 0], seam_table[:, :, 1], seam_table[:, :, 2]
    device = n // TILES_HERE
    group = (device % CORE) * YX + device // (NZ * CORE)
    unit = (group * TILES_HERE + n % TILES_HERE) * 4 + f
    z = (device // CORE) % NZ
    word = unit + r * 256 + z * 512
    beyond = (n * 4 + jnp.where(f < 2, 2, 0)) * 2 + f % 2
    return word.reshape(-1), beyond.reshape(-1)


def place_kernel(word_ref, beyond_ref, unit_ref, out_ref, sent):
    ylo, x, z, core = (lax.axis_index(axis) for axis in TILE_AXES)

    def unit_at(word):
        keep = jnp.where((word >> 9) == z, 1.0, 0.0).astype(F32)
        at = pl.multiple_of((word & 255) * UNIT, UNIT)
        return unit_ref[pl.ds(at, UNIT), :].astype(F32) * keep

    def body(z_to, carry):
        device = ((ylo * NX + x) * NZ + z_to) * CORE + core
        for t in range(TILES_HERE):
            for edge in range(4):
                at = (device * TILES_HERE + t) * 4 + edge
                unit = unit_at(word_ref[at])
                row = t * BLOCK_ROWS + EDGE_ROWS[edge]
                cot = t * BLOCK_ROWS + FIELD_ROWS + 3 * edge
                sent[z_to, row : row + 6, :] = unit[0:6]
                sent[z_to, cot : cot + 3, :] = unit[6:9]
                if edge % 2 == 0:
                    sent[z_to, row + 6 : row + 12, :] = unit[9:15]
                    beyond = beyond_ref[at]
                    for last in range(2):
                        word = word_ref[(beyond >> 1) + last]
                        end = unit_at(word)
                        low = ((beyond + (word >> 8)) & 1) == 0
                        sent[z_to, row + 12 + last : row + 13 + last, :] = jnp.where(low, end[0:1], end[15:16])
        sent[z_to, TILES_HERE * BLOCK_ROWS :, :] = jnp.zeros((SEND_ROWS - TILES_HERE * BLOCK_ROWS, 128), F32)
        return carry

    lax.fori_loop(0, NZ, body, 0)
    out_ref[...] = sent[...].astype(BF)


def join_kernel(got_ref, own_ref, out_ref, rows):
    total = got_ref[0].astype(F32)
    for q in range(1, NZ):
        total = total + got_ref[q].astype(F32)
    for t in range(TILES_HERE):
        base, block = t * PAY_ROWS, t * BLOCK_ROWS
        own = own_ref[t].astype(F32)
        rows[base : base + OWN_ROWS, :] = own[:OWN_ROWS]
        rows[base + OWN_ROWS : base + X_HALF, :] = total[block : block + FIELD_ROWS]
        rows[base + X_HALF : base + X_HALF + C_OWN, :] = own[OWN_ROWS : OWN_ROWS + C_OWN]
        rows[base + X_HALF + C_OWN : base + PAY_ROWS - 2, :] = total[block + FIELD_ROWS : block + BLOCK_ROWS]
        rows[base + PAY_ROWS - 2 : base + PAY_ROWS, :] = jnp.zeros((2, 128), F32)
    whole = rows[...].astype(BF)
    for c in range(CHAN):
        out_ref[c] = whole


def hold_kernel(weights_ref, wf, wd, sems):
    copies = []
    for which, held in enumerate((wf, wd)):
        for c in range(CHAN):
            copies.append(
                pltpu.make_async_copy(
                    weights_ref.at[2 * c + which], held.at[:, pl.ds(c * CH, CH), :], sems.at[2 * c + which]
                )
            )
    for copy in copies:
        copy.start()
    for copy in copies:
        copy.wait()


def main_kernel(
    pay_ref, rim_at_ref, shift_ref, down_ref, rim_ref, order_ref, cell_ref, wf, wd, window_hbm,
    coarse_ref, gp_ref, kept_ref, given_ref, window_ref, xs, cs, wins, ups, rims, downs, gps, up, sems,
):
    window_copies = [
        pltpu.make_async_copy(window_hbm.at[t], window_ref.at[t], sems.at[t]) for t in range(TILES_HERE)
    ]
    for copy in window_copies:
        copy.start()
    chan, core = lax.axis_index("chan"), lax.axis_index("core")
    pick = jnp.where(
        lax.broadcasted_iota(jnp.int32, (CH, C), 1) == lax.broadcasted_iota(jnp.int32, (CH, C), 0) + chan * CH, 1.0, 0.0
    ).astype(BF)
    for c in range(CHAN):
        for t in range(TILES_HERE):
            base = t * PAY_ROWS
            for h in range(2):
                lanes = slice(h * CH, (h + 1) * CH)
                xs[t, h * X_HALF : (h + 1) * X_HALF, c * CH : (c + 1) * CH] = pay_ref[c, base : base + X_HALF, lanes]
                cs[t, h * C_HALF : (h + 1) * C_HALF, c * CH : (c + 1) * CH] = pay_ref[
                    c, base + X_HALF : base + PAY_ROWS, lanes
                ]
    for t in range(TILES_HERE):
        xs[t, 2 * X_HALF :, :] = jnp.zeros((C - 2 * X_HALF, C), BF)
    for t in range(TILES_HERE):
        window_copies[t].wait()
        for k in range(9):
            wins[t * PRE_ROWS : (t + 1) * PRE_ROWS, k * C : (k + 1) * C] = dot_nn(
                window_ref[t, k * PRE_ROWS : (k + 1) * PRE_ROWS, :], xs[t]
            ).astype(BF)
        shifted = dot_nn(shift_ref[...], cs[t])
        for s in range(4):
            ups[s, t * PART : (t + 1) * PART, :] = shifted[s * PART : (s + 1) * PART]
        near = dot_nn(rim_at_ref[t], cs[t]).astype(BF)
        for s in range(len(RIM_TAPS)):
            rims[s, t * RIM_ROWS : (t + 1) * RIM_ROWS, :] = near[s * RIM_ROWS : (s + 1) * RIM_ROWS]
    pre = dot_nn(wins[...], wf[...].reshape(9 * C, C))
    ups_low = [ups[s].astype(BF) for s in range(4)]
    blocks = (
        dot_nt(ups_low[0], wd[4]),
        dot_nt(ups_low[1], wd[3]) + dot_nt(ups_low[0], wd[5]),
        dot_nt(ups_low[2], wd[1]) + dot_nt(ups_low[0], wd[7]),
        dot_nt(ups_low[3], wd[0]) + dot_nt(ups_low[2], wd[2]) + dot_nt(ups_low[1], wd[6]) + dot_nt(ups_low[0], wd[8]),
    )
    rim = dot_nt(rims[0], wd[RIM_TAPS[0]])
    for s in range(1, len(RIM_TAPS)):
        rim = rim + dot_nt(rims[s], wd[RIM_TAPS[s]])
    rim = rim.astype(BF)
    scale = np.float32(np.sqrt(2 / np.pi))
    squared = pre * pre
    bent = jnp.tanh(scale * (pre + np.float32(0.044715) * squared * pre))
    gate = 0.5 * (1.0 + bent)
    hidden = (pre * gate).astype(BF)
    slope = gate + 0.5 * pre * (1.0 - bent * bent) * scale * (1.0 + np.float32(3 * 0.044715) * squared)

    for t in range(TILES_HERE):
        own_hidden = hidden[t * PRE_ROWS : (t + 1) * PRE_ROWS]
        windows = dot_nn(down_ref[...], own_hidden).astype(BF)
        for k in range(9):
            downs[t * DOWN_ROWS : (t + 1) * DOWN_ROWS, k * C : (k + 1) * C] = windows[k * DOWN_ROWS : (k + 1) * DOWN_ROWS]
        up[t * DOWN_ROWS : (t + 1) * DOWN_ROWS, :] = dot_nn(order_ref[...], cs[t]).astype(BF)

        grad_hidden = jnp.concatenate([block[t * PART : (t + 1) * PART] for block in blocks], axis=0)
        grad_hidden = grad_hidden + dot_nn(rim_ref[...], rim[t * RIM_ROWS : (t + 1) * RIM_ROWS])
        grad_pre = (grad_hidden * slope[t * PRE_ROWS : t * PRE_ROWS + INNER]).astype(BF)
        gps[t * PRE_ROWS : t * PRE_ROWS + INNER, :] = grad_pre
        gps[t * PRE_ROWS + INNER : (t + 1) * PRE_ROWS, :] = jnp.zeros((PRE_ROWS - INNER, C), BF)
        gp_ref[t] = dot_nn(dot_nt(pick, grad_pre).astype(BF), cell_ref[...]).astype(BF)

    lanes = pl.multiple_of((chan // 2) * 128, 128)
    for k in range(9):
        for base, left, right in ((0, wins, gps), (9 * CH, downs, up)):
            both = dot_tn(left[:, pl.ds(k * C + lanes, 128)], right[...])
            part = jnp.where(chan % 2 == 0, both[:CH], both[CH:]).astype(BF)
            left_half, right_half = part[:, :128], part[:, 128:]
            rows = slice(base + k * CH, base + (k + 1) * CH)
            kept_ref[rows, :] = jnp.where(core == 0, left_half, right_half)
            given_ref[rows, :] = jnp.where(core == 0, right_half, left_half)
    coarse = dot_nt(dot_nn(downs[...], wd[...].reshape(9 * C, C)).astype(BF), pick).astype(BF)
    for t in range(TILES_HERE):
        coarse_ref[t] = coarse[t * DOWN_ROWS : t * DOWN_ROWS + COARSE]


def vmem(count):
    return [pl.BlockSpec(memory_space=pltpu.VMEM)] * count


def hbm(count):
    return [pl.BlockSpec(memory_space=pltpu.HBM)] * count


def smem(count):
    return [pl.BlockSpec(memory_space=pltpu.SMEM)] * count


LIMIT = pltpu.CompilerParams(vmem_limit_bytes=48 * 1024 * 1024)
WHOLE = pltpu.CompilerParams(vmem_limit_bytes=60 * 1024 * 1024)
MOST = pltpu.CompilerParams(vmem_limit_bytes=50 * 1024 * 1024)


def tiles_call(payload, window, rim_at, weights):
    held = pl.pallas_call(
        hold_kernel,
        out_shape=(jax.ShapeDtypeStruct((9, C, C), BF), jax.ShapeDtypeStruct((9, C, C), BF)),
        in_specs=hbm(1),
        out_specs=tuple(vmem(2)),
        scratch_shapes=[pltpu.SemaphoreType.DMA((2 * CHAN,))],
        compiler_params=MOST,
        cost_estimate=pl.CostEstimate(flops=0, bytes_accessed=2 * 18 * C * C * 2, transcendentals=0),
        name="hold",
    )(weights)
    constants = (shift_selector(), down_selector(), rim_selector(), order_selector(), cell_selector())
    return pl.pallas_call(
        main_kernel,
        out_shape=(
            jax.ShapeDtypeStruct((TILES_HERE, COARSE, CH), BF),
            jax.ShapeDtypeStruct((TILES_HERE, CH, CELLS), BF),
            jax.ShapeDtypeStruct((18 * CH, 128), BF),
            jax.ShapeDtypeStruct((18 * CH, 128), BF),
        ),
        in_specs=vmem(9) + hbm(1),
        out_specs=tuple(vmem(4)),
        scratch_shapes=[
            pltpu.VMEM((TILES_HERE, 9 * PRE_ROWS, C), BF),
            pltpu.VMEM((TILES_HERE, C, C), BF),
            pltpu.VMEM((TILES_HERE, 2 * C_HALF, C), BF),
            pltpu.VMEM((TILES_HERE * PRE_ROWS, 9 * C), BF),
            pltpu.VMEM((4, TILES_HERE * PART, C), F32),
            pltpu.VMEM((len(RIM_TAPS), TILES_HERE * RIM_ROWS, C), BF),
            pltpu.VMEM((TILES_HERE * DOWN_ROWS, 9 * C), BF),
            pltpu.VMEM((TILES_HERE * PRE_ROWS, C), BF),
            pltpu.VMEM((TILES_HERE * DOWN_ROWS, C), BF),
            pltpu.SemaphoreType.DMA((TILES_HERE,)),
        ],
        compiler_params=MOST,
        name="tiles",
    )(payload, rim_at, *(jnp.asarray(array, BF) for array in constants), *held, window)


def shards(fields, seam_table, w_first, w_down, cotangent):
    coords = [lax.axis_index(axis) for axis in ("ylo", "x", "z", "core")]
    own, units, half = pl.pallas_call(
        pack_kernel,
        out_shape=(
            jax.ShapeDtypeStruct((TILES_HERE, PACK_ROWS, 128), BF),
            jax.ShapeDtypeStruct((YX, TILES_HERE * 4 * UNIT, 128), BF),
            jax.ShapeDtypeStruct(w_first.shape, BF),
        ),
        in_specs=hbm(4),
        out_specs=tuple(hbm(3)),
        scratch_shapes=[
            pltpu.VMEM((TILES_HERE, CH, CELLS), BF),
            pltpu.VMEM((TILES_HERE, COARSE, CH), BF),
            pltpu.VMEM((9, CH, C), BF),
            pltpu.VMEM((TILES_HERE * 4 * UNIT, 128), BF),
            pltpu.VMEM((TILES_HERE, PACK_ROWS, 128), BF),
            pltpu.SemaphoreType.DMA((5 + YX,)),
        ],
        compiler_params=WHOLE,
        name="pack",
    )(fields, jnp.swapaxes(cotangent, 1, 2), w_first, w_down)
    weights = lax.all_gather(half, ("chan", "core"), axis=0, tiled=False)
    units = lax.all_to_all(units, ("ylo", "x"), 0, 0).reshape(-1, 128)
    units = lax.all_gather(units, "core", axis=0, tiled=True)
    words, beyond = edge_words(seam_table)
    sends = pl.pallas_call(
        place_kernel,
        out_shape=jax.ShapeDtypeStruct((NZ, SEND_ROWS, 128), BF),
        in_specs=smem(2) + vmem(1),
        out_specs=vmem(1)[0],
        scratch_shapes=[pltpu.VMEM((NZ, SEND_ROWS, 128), F32)],
        compiler_params=LIMIT,
        name="place",
    )(words, beyond, units)
    got = lax.all_to_all(sends, "z", 0, 0)
    joined = pl.pallas_call(
        join_kernel,
        out_shape=jax.ShapeDtypeStruct((CHAN, TILES_HERE * PAY_ROWS, 128), BF),
        in_specs=vmem(2),
        out_specs=vmem(1)[0],
        scratch_shapes=[pltpu.VMEM((TILES_HERE * PAY_ROWS, 128), F32)],
        compiler_params=LIMIT,
        name="join",
    )(got, own)
    payload = lax.all_to_all(joined, "chan", 0, 0)

    tile_at = ((coords[0] * NX + coords[1]) * NZ + coords[2]) * CORE + coords[3]
    own_table = lax.dynamic_slice_in_dim(seam_table, tile_at * TILES_HERE, TILES_HERE, 0)
    code = own_table[:, :, 1] * 2 + own_table[:, :, 2]
    chosen = (code[:, :, None] == jnp.arange(8, dtype=jnp.int32)).astype(BF).reshape(TILES_HERE, 32)
    one_hots = []
    for (fixed, varied), depth in ((window_index(), C), (rim_index(), 2 * C_HALF)):
        at = jnp.dot(chosen, jnp.asarray(varied, BF), preferred_element_type=F32) + jnp.asarray(fixed, F32)
        one_hots.append((at[:, :, None] == jnp.arange(1, depth + 1, dtype=jnp.int32).astype(F32)).astype(BF))

    coarse, grad_pre, kept, given = tiles_call(payload, one_hots[0], one_hots[1], weights)

    part = lax.ppermute(given, "core", [(0, 1), (1, 0)])
    part = (kept.astype(F32) + part.astype(F32)).astype(BF).reshape(YX, 144, 128)
    part = lax.all_to_all(part, ("ylo", "x"), 0, 0)
    part = part.astype(F32).sum(0).astype(BF)
    part = lax.all_to_all(jnp.broadcast_to(part[None], (NZ, 144, 128)), "z", 0, 0)
    part = part.astype(F32).sum(0).astype(BF)
    part = lax.all_to_all(jnp.broadcast_to(part[None], (YX, 144, 128)), ("ylo", "x"), 0, 0)
    whole = lax.all_gather(part.reshape(18 * CH, 128), "core", axis=0, tiled=False)
    whole = jnp.concatenate([whole[0], whole[1]], axis=1).astype(F32).reshape(2, 9, CH, C)
    tiles = TILES_HERE * PLANE * CORE
    return (
        jnp.swapaxes(coarse, 1, 2),
        whole[0] * float(tiles * CELLS) ** (-0.5),
        whole[1] * float(tiles * COARSE) ** (-0.5),
        grad_pre,
    )


def solution(mesh):
    fine = Mesh(mesh.devices.reshape(YLO, NX, NZ, CORE, CHAN), ("ylo", "x", "z", "core", "chan"))
    return jax.shard_map(
        shards,
        mesh=fine,
        in_specs=(
            P(TILE_AXES, "chan", None),
            P(),
            P(None, "chan", None),
            P(None, "chan", None),
            P(TILE_AXES, "chan", None),
        ),
        out_specs=(
            P(TILE_AXES, "chan", None),
            P(None, "chan", None),
            P(None, "chan", None),
            P(TILE_AXES, "chan", None),
        ),
        check_vma=False,
    )
```

```python
import numpy as np
import jax
import jax.numpy as jnp
from jax import lax
from jax.experimental import pallas as pl
from jax.experimental.pallas import tpu as pltpu
from jax.sharding import Mesh, PartitionSpec as P

S = 12
HALF = 6
CELLS = 144
COARSE = 36
TILES_HERE = 3
CH = 64
C = 256
YLO, NX, NZ, CORE, CHAN = 2, 4, 8, 2, 4
YX = YLO * NX
NEAR = YX * CORE
PLANE = YX * NZ
TILE_AXES = ("ylo", "x", "z", "core")
BF = jnp.bfloat16
F32 = jnp.float32

EDGE_ROWS = (0, 28, 14, 34)
FIELD_ROWS = 40
BLOCK_ROWS = 52
SEND_ROWS = 160
OWN_ROWS = 72
X_HALF = OWN_ROWS + FIELD_ROWS
C_OWN = 18
C_HALF = 32
PAY_ROWS = X_HALF + C_HALF
PACK_ROWS = 96
UNIT = 16
PART = 40
INNER = 4 * PART
PRE_ROWS = INNER + 32
DOWN_ROWS = 48
RIM_ROWS = 48
RIM_TAPS = (0, 1, 2, 3, 6)


def strip_cells(edge, depth):
    if edge == 0:
        return [depth * S + i for i in range(S)]
    if edge == 1:
        return [(S - 1 - depth) * S + i for i in range(S)]
    if edge == 2:
        return [i * S + depth for i in range(S)]
    return [i * S + S - 1 - depth for i in range(S)]


def cell_row(row, col):
    return (row % 2 * 2 + col % 2) * PART + row // 2 * HALF + col // 2


def own_at(cell):
    return cell // 2 + X_HALF * (cell % 2)


def near_at(edge, along, depth):
    row = OWN_ROWS + EDGE_ROWS[edge] + 6 * depth
    if along < 0:
        return OWN_ROWS + EDGE_ROWS[edge] + 12 + X_HALF * depth
    if along >= S:
        return OWN_ROWS + EDGE_ROWS[edge] + 13 + X_HALF * depth
    return row + along // 2 + X_HALF * (along % 2)


def window_index():
    fixed = np.zeros((9, PRE_ROWS), np.float32)
    varied = np.zeros((4, 4, 2, 9, PRE_ROWS), np.float32)
    for k in range(9):
        a, b = k // 3, k % 3
        for cell in range(CELLS):
            row, col = cell // S + a, cell % S + b
            inner_row, inner_col = 1 <= row <= S, 1 <= col <= S
            if inner_row and inner_col:
                fixed[k, cell_row(cell // S, cell % S)] = 1 + own_at((row - 1) * S + col - 1)
            elif inner_row or inner_col:
                edge = (2 if col == 0 else 3) if inner_row else (0 if row == 0 else 1)
                at = row - 1 if inner_row else col - 1
                for flip in range(2):
                    varied[edge, :, flip, k, cell_row(cell // S, cell % S)] = 1 + near_at(
                        edge, 11 - at if flip else at, 0
                    )
        for slot, edge in enumerate((0, 2)):
            own = strip_cells(edge, 0)
            for facing in range(4):
                depth = (a - 1, 1 - a, b - 1, 1 - b)[facing]
                shift = (b - 1, b - 1, a - 1, a - 1)[facing]
                for flip in range(2):
                    for j in range(S):
                        along = (11 - j if flip else j) + shift
                        if depth >= 0:
                            at = near_at(edge, along, depth)
                        elif 0 <= along < S:
                            at = own_at(own[11 - along if flip else along])
                        else:
                            continue
                        varied[edge, facing, flip, k, INNER + 16 * slot + j] = 1 + at
    return fixed.reshape(-1), varied.reshape(32, -1)


def rim_index():
    varied = np.zeros((4, 4, 2, len(RIM_TAPS), RIM_ROWS), np.float32)
    for slot, k in enumerate(RIM_TAPS):
        a, b = k // 3, k % 3
        for edge in range(4):
            for flip in range(2):
                for j in range(S):
                    for facing, live, tap in ((0, a == 0, b), (2, b == 0, a)):
                        at = (11 - j if flip else j) + 1 - tap
                        if live and at % 2 == 0 and 0 <= at < S:
                            at //= 2
                            varied[edge, facing, flip, slot, edge * S + j] = (
                                1 + C_OWN + 3 * edge + at // 2 + C_HALF * (at % 2)
                            )
    return np.zeros(len(RIM_TAPS) * RIM_ROWS, np.float32), varied.reshape(32, -1)


def shift_selector():
    chosen = np.zeros((2, 2, PART, 2 * C_HALF), np.float32)
    for down in range(2):
        for right in range(2):
            for row in range(HALF - down):
                for col in range(HALF - right):
                    at = (row + down) * HALF + col + right
                    chosen[down, right, row * HALF + col, at // 2 + C_HALF * (at % 2)] = 1
    return chosen.reshape(INNER, 2 * C_HALF)


def down_selector():
    chosen = np.zeros((9, DOWN_ROWS, PRE_ROWS), np.float32)
    for k in range(9):
        for cell in range(COARSE):
            row, col = 2 * (cell // HALF) + k // 3, 2 * (cell % HALF) + k % 3
            if row == 0 and col == 0:
                continue
            if row == 0:
                at = INNER + col - 1
            elif col == 0:
                at = INNER + 16 + row - 1
            else:
                at = cell_row(row - 1, col - 1)
            chosen[k, cell, at] = 1
    return chosen.reshape(9 * DOWN_ROWS, PRE_ROWS)


def rim_selector():
    chosen = np.zeros((INNER, RIM_ROWS), np.float32)
    for edge in range(4):
        for j, cell in enumerate(strip_cells(edge, 0)):
            chosen[cell_row(cell // S, cell % S), edge * S + j] = 1
    return chosen


def cell_selector():
    chosen = np.zeros((INNER, CELLS), np.float32)
    for cell in range(CELLS):
        chosen[cell_row(cell // S, cell % S), cell] = 1
    return chosen


def order_selector():
    chosen = np.zeros((DOWN_ROWS, 2 * C_HALF), np.float32)
    for cell in range(COARSE):
        chosen[cell, cell // 2 + C_HALF * (cell % 2)] = 1
    return chosen


def dot_nn(left, right):
    return lax.dot_general(left, right, (((1,), (0,)), ((), ())), preferred_element_type=F32)


def dot_tn(left, right):
    return lax.dot_general(left, right, (((0,), (0,)), ((), ())), preferred_element_type=F32)


def dot_nt(left, right):
    return lax.dot_general(left, right, (((1,), (1,)), ((), ())), preferred_element_type=F32)


def pack_selectors(half):
    rows = PACK_ROWS + 4 * UNIT
    row = lax.broadcasted_iota(jnp.int32, (rows, CELLS), 0)
    at = lax.broadcasted_iota(jnp.int32, (rows, CELLS), 1)
    edge, j = (row - PACK_ROWS) >> 4, (row - PACK_ROWS) & 15
    deep = jnp.where(jnp.logical_and(j >= 9, j < 15), 1, 0)
    along = jnp.where(j < 6, 2 * j + half, jnp.where(j < 15, 2 * (j - 9) + half, 11 - half))
    start = jnp.where(edge == 0, S * deep, jnp.where(edge == 1, S * (S - 1 - deep), jnp.where(edge == 2, deep, S - 1 - deep)))
    cell = start + along * jnp.where(edge < 2, 1, S)
    cell = jnp.where(jnp.logical_or(j < 6, j >= 9), cell, -1)
    cell = jnp.where(row < OWN_ROWS, 2 * row + half, jnp.where(row < PACK_ROWS, -1, cell))
    fields = jnp.where(at == cell, 1.0, 0.0).astype(BF)
    row, at, edge, j = row[:, :COARSE], at[:, :COARSE], edge[:, :COARSE], j[:, :COARSE]
    cell = (2 * (j - 6) + half) * jnp.where(edge == 0, 1, HALF)
    live = jnp.logical_and(jnp.logical_and(j >= 6, j < 9), jnp.logical_or(edge == 0, edge == 2))
    cell = jnp.where(live, cell, -1)
    own = jnp.where(row < OWN_ROWS + C_OWN, 2 * (row - OWN_ROWS) + half, -1)
    cell = jnp.where(row < PACK_ROWS, own, cell)
    return fields, jnp.where(at == cell, 1.0, 0.0).astype(BF)


def pack_kernel(fields_hbm, cot_hbm, first_ref, down_ref, own_hbm, unit_hbm, half_ref, fields_ref, cot_ref, held, unit_ref, own_ref, sems):
    loads = [
        pltpu.make_async_copy(fields_hbm, fields_ref, sems.at[0]),
        pltpu.make_async_copy(cot_hbm, cot_ref, sems.at[1]),
    ]
    for load in loads:
        load.start()
    core = lax.axis_index("core")

    @pl.when(core == 0)
    def _():
        pltpu.make_async_copy(first_ref, held, sems.at[2]).start()

    @pl.when(core == 1)
    def _():
        pltpu.make_async_copy(down_ref, held, sems.at[2]).start()

    chosen = [pack_selectors(h) for h in range(2)]
    for load in loads:
        load.wait()
    for t in range(TILES_HERE):
        halves = [(dot_nt(f, fields_ref[t]) + dot_nn(c, cot_ref[t])).astype(BF) for f, c in chosen]
        for h in range(2):
            own_ref[t, :, h * CH : (h + 1) * CH] = halves[h][:PACK_ROWS]
            unit_ref[t * 4 * UNIT : (t + 1) * 4 * UNIT, h * CH : (h + 1) * CH] = halves[h][PACK_ROWS:]
    pltpu.make_async_copy(first_ref, held, sems.at[2]).wait()
    stores = [pltpu.make_async_copy(held, half_ref, sems.at[3])]
    for copy in range(YX):
        stores.append(pltpu.make_async_copy(unit_ref, unit_hbm.at[copy], sems.at[4 + copy]))
    stores.append(pltpu.make_async_copy(own_ref, own_hbm, sems.at[4 + YX]))
    for store in stores:
        store.start()
    for store in stores:
        store.wait()


def edge_words(seam_table):
    n, f, r = seam_table[:, :, 0], seam_table[:, :, 1], seam_table[:, :, 2]
    device = n // TILES_HERE
    group = (device % CORE) * YX + device // (NZ * CORE)
    unit = (group * TILES_HERE + n % TILES_HERE) * 4 + f
    z = (device // CORE) % NZ
    word = unit + r * 256 + z * 512
    beyond = (n * 4 + jnp.where(f < 2, 2, 0)) * 2 + f % 2
    return word.reshape(-1), beyond.reshape(-1)


def place_kernel(word_ref, beyond_ref, unit_ref, out_ref, sent):
    ylo, x, z, core = (lax.axis_index(axis) for axis in TILE_AXES)

    def unit_at(word):
        keep = jnp.where((word >> 9) == z, 1.0, 0.0).astype(F32)
        at = pl.multiple_of((word & 255) * UNIT, UNIT)
        return unit_ref[pl.ds(at, UNIT), :].astype(F32) * keep

    def body(z_to, carry):
        device = ((ylo * NX + x) * NZ + z_to) * CORE + core
        for t in range(TILES_HERE):
            for edge in range(4):
                at = (device * TILES_HERE + t) * 4 + edge
                unit = unit_at(word_ref[at])
                row = t * BLOCK_ROWS + EDGE_ROWS[edge]
                cot = t * BLOCK_ROWS + FIELD_ROWS + 3 * edge
                sent[z_to, row : row + 6, :] = unit[0:6]
                sent[z_to, cot : cot + 3, :] = unit[6:9]
                if edge % 2 == 0:
                    sent[z_to, row + 6 : row + 12, :] = unit[9:15]
                    beyond = beyond_ref[at]
                    for last in range(2):
                        word = word_ref[(beyond >> 1) + last]
                        end = unit_at(word)
                        low = ((beyond + (word >> 8)) & 1) == 0
                        sent[z_to, row + 12 + last : row + 13 + last, :] = jnp.where(low, end[0:1], end[15:16])
        sent[z_to, TILES_HERE * BLOCK_ROWS :, :] = jnp.zeros((SEND_ROWS - TILES_HERE * BLOCK_ROWS, 128), F32)
        return carry

    lax.fori_loop(0, NZ, body, 0)
    out_ref[...] = sent[...].astype(BF)


def join_kernel(got_ref, own_ref, out_ref, rows):
    total = got_ref[0].astype(F32)
    for q in range(1, NZ):
        total = total + got_ref[q].astype(F32)
    for t in range(TILES_HERE):
        base, block = t * PAY_ROWS, t * BLOCK_ROWS
        own = own_ref[t].astype(F32)
        rows[base : base + OWN_ROWS, :] = own[:OWN_ROWS]
        rows[base + OWN_ROWS : base + X_HALF, :] = total[block : block + FIELD_ROWS]
        rows[base + X_HALF : base + X_HALF + C_OWN, :] = own[OWN_ROWS : OWN_ROWS + C_OWN]
        rows[base + X_HALF + C_OWN : base + PAY_ROWS - 2, :] = total[block + FIELD_ROWS : block + BLOCK_ROWS]
        rows[base + PAY_ROWS - 2 : base + PAY_ROWS, :] = jnp.zeros((2, 128), F32)
    whole = rows[...].astype(BF)
    for c in range(CHAN):
        out_ref[c] = whole


def hold_kernel(weights_ref, wf, wd, sems):
    copies = []
    for which, held in enumerate((wf, wd)):
        for c in range(CHAN):
            copies.append(
                pltpu.make_async_copy(
                    weights_ref.at[2 * c + which], held.at[:, pl.ds(c * CH, CH), :], sems.at[2 * c + which]
                )
            )
    for copy in copies:
        copy.start()
    for copy in copies:
        copy.wait()


def main_kernel(
    pay_ref, rim_at_ref, shift_ref, down_ref, rim_ref, order_ref, cell_ref, wf, wd, window_ref,
    coarse_ref, gp_ref, kept_ref, given_ref, xs, cs, wins, ups, rims, downs, gps, up,
):
    chan, core = lax.axis_index("chan"), lax.axis_index("core")
    pick = jnp.where(
        lax.broadcasted_iota(jnp.int32, (CH, C), 1) == lax.broadcasted_iota(jnp.int32, (CH, C), 0) + chan * CH, 1.0, 0.0
    ).astype(BF)
    for c in range(CHAN):
        for t in range(TILES_HERE):
            base = t * PAY_ROWS
            for h in range(2):
                lanes = slice(h * CH, (h + 1) * CH)
                xs[t, h * X_HALF : (h + 1) * X_HALF, c * CH : (c + 1) * CH] = pay_ref[c, base : base + X_HALF, lanes]
                cs[t, h * C_HALF : (h + 1) * C_HALF, c * CH : (c + 1) * CH] = pay_ref[
                    c, base + X_HALF : base + PAY_ROWS, lanes
                ]
    for t in range(TILES_HERE):
        xs[t, 2 * X_HALF :, :] = jnp.zeros((C - 2 * X_HALF, C), BF)
    for t in range(TILES_HERE):
        for k in range(9):
            wins[t * PRE_ROWS : (t + 1) * PRE_ROWS, k * C : (k + 1) * C] = dot_nn(
                window_ref[t, k * PRE_ROWS : (k + 1) * PRE_ROWS, :], xs[t]
            ).astype(BF)
        shifted = dot_nn(shift_ref[...], cs[t])
        for s in range(4):
            ups[s, t * PART : (t + 1) * PART, :] = shifted[s * PART : (s + 1) * PART]
        near = dot_nn(rim_at_ref[t], cs[t]).astype(BF)
        for s in range(len(RIM_TAPS)):
            rims[s, t * RIM_ROWS : (t + 1) * RIM_ROWS, :] = near[s * RIM_ROWS : (s + 1) * RIM_ROWS]
    pre = dot_nn(wins[...], wf[...].reshape(9 * C, C))
    ups_low = [ups[s].astype(BF) for s in range(4)]
    blocks = (
        dot_nt(ups_low[0], wd[4]),
        dot_nt(ups_low[1], wd[3]) + dot_nt(ups_low[0], wd[5]),
        dot_nt(ups_low[2], wd[1]) + dot_nt(ups_low[0], wd[7]),
        dot_nt(ups_low[3], wd[0]) + dot_nt(ups_low[2], wd[2]) + dot_nt(ups_low[1], wd[6]) + dot_nt(ups_low[0], wd[8]),
    )
    rim = dot_nt(rims[0], wd[RIM_TAPS[0]])
    for s in range(1, len(RIM_TAPS)):
        rim = rim + dot_nt(rims[s], wd[RIM_TAPS[s]])
    rim = rim.astype(BF)
    scale = np.float32(np.sqrt(2 / np.pi))
    squared = pre * pre
    bent = jnp.tanh(scale * (pre + np.float32(0.044715) * squared * pre))
    gate = 0.5 * (1.0 + bent)
    hidden = (pre * gate).astype(BF)
    slope = gate + 0.5 * pre * (1.0 - bent * bent) * scale * (1.0 + np.float32(3 * 0.044715) * squared)

    for t in range(TILES_HERE):
        own_hidden = hidden[t * PRE_ROWS : (t + 1) * PRE_ROWS]
        windows = dot_nn(down_ref[...], own_hidden).astype(BF)
        for k in range(9):
            downs[t * DOWN_ROWS : (t + 1) * DOWN_ROWS, k * C : (k + 1) * C] = windows[k * DOWN_ROWS : (k + 1) * DOWN_ROWS]
        up[t * DOWN_ROWS : (t + 1) * DOWN_ROWS, :] = dot_nn(order_ref[...], cs[t]).astype(BF)

        grad_hidden = jnp.concatenate([block[t * PART : (t + 1) * PART] for block in blocks], axis=0)
        grad_hidden = grad_hidden + dot_nn(rim_ref[...], rim[t * RIM_ROWS : (t + 1) * RIM_ROWS])
        grad_pre = (grad_hidden * slope[t * PRE_ROWS : t * PRE_ROWS + INNER]).astype(BF)
        gps[t * PRE_ROWS : t * PRE_ROWS + INNER, :] = grad_pre
        gps[t * PRE_ROWS + INNER : (t + 1) * PRE_ROWS, :] = jnp.zeros((PRE_ROWS - INNER, C), BF)
        gp_ref[t] = dot_nn(dot_nt(pick, grad_pre).astype(BF), cell_ref[...]).astype(BF)

    lanes = pl.multiple_of((chan // 2) * 128, 128)
    for k in range(9):
        for base, left, right in ((0, wins, gps), (9 * CH, downs, up)):
            both = dot_tn(left[:, pl.ds(k * C + lanes, 128)], right[...])
            part = jnp.where(chan % 2 == 0, both[:CH], both[CH:]).astype(BF)
            left_half, right_half = part[:, :128], part[:, 128:]
            rows = slice(base + k * CH, base + (k + 1) * CH)
            kept_ref[rows, :] = jnp.where(core == 0, left_half, right_half)
            given_ref[rows, :] = jnp.where(core == 0, right_half, left_half)
    coarse = dot_nt(dot_nn(downs[...], wd[...].reshape(9 * C, C)).astype(BF), pick).astype(BF)
    for t in range(TILES_HERE):
        coarse_ref[t] = coarse[t * DOWN_ROWS : t * DOWN_ROWS + COARSE]


def vmem(count):
    return [pl.BlockSpec(memory_space=pltpu.VMEM)] * count


def hbm(count):
    return [pl.BlockSpec(memory_space=pltpu.HBM)] * count


def smem(count):
    return [pl.BlockSpec(memory_space=pltpu.SMEM)] * count


LIMIT = pltpu.CompilerParams(vmem_limit_bytes=48 * 1024 * 1024)
WHOLE = pltpu.CompilerParams(vmem_limit_bytes=60 * 1024 * 1024)
MOST = pltpu.CompilerParams(vmem_limit_bytes=40 * 1024 * 1024)


def tiles_call(payload, window, rim_at, weights):
    held = pl.pallas_call(
        hold_kernel,
        out_shape=(jax.ShapeDtypeStruct((9, C, C), BF), jax.ShapeDtypeStruct((9, C, C), BF)),
        in_specs=hbm(1),
        out_specs=tuple(vmem(2)),
        scratch_shapes=[pltpu.SemaphoreType.DMA((2 * CHAN,))],
        compiler_params=MOST,
        cost_estimate=pl.CostEstimate(flops=0, bytes_accessed=2 * 18 * C * C * 2, transcendentals=0),
        name="hold",
    )(weights)
    constants = (shift_selector(), down_selector(), rim_selector(), order_selector(), cell_selector())
    return pl.pallas_call(
        main_kernel,
        out_shape=(
            jax.ShapeDtypeStruct((TILES_HERE, COARSE, CH), BF),
            jax.ShapeDtypeStruct((TILES_HERE, CH, CELLS), BF),
            jax.ShapeDtypeStruct((18 * CH, 128), BF),
            jax.ShapeDtypeStruct((18 * CH, 128), BF),
        ),
        in_specs=vmem(10),
        out_specs=tuple(vmem(4)),
        scratch_shapes=[
            pltpu.VMEM((TILES_HERE, C, C), BF),
            pltpu.VMEM((TILES_HERE, 2 * C_HALF, C), BF),
            pltpu.VMEM((TILES_HERE * PRE_ROWS, 9 * C), BF),
            pltpu.VMEM((4, TILES_HERE * PART, C), F32),
            pltpu.VMEM((len(RIM_TAPS), TILES_HERE * RIM_ROWS, C), BF),
            pltpu.VMEM((TILES_HERE * DOWN_ROWS, 9 * C), BF),
            pltpu.VMEM((TILES_HERE * PRE_ROWS, C), BF),
            pltpu.VMEM((TILES_HERE * DOWN_ROWS, C), BF),
        ],
        compiler_params=MOST,
        name="tiles",
    )(payload, rim_at, *(jnp.asarray(array, BF) for array in constants), *held, window)


def shards(fields, seam_table, w_first, w_down, cotangent):
    coords = [lax.axis_index(axis) for axis in ("ylo", "x", "z", "core")]
    own, units, half = pl.pallas_call(
        pack_kernel,
        out_shape=(
            jax.ShapeDtypeStruct((TILES_HERE, PACK_ROWS, 128), BF),
            jax.ShapeDtypeStruct((YX, TILES_HERE * 4 * UNIT, 128), BF),
            jax.ShapeDtypeStruct(w_first.shape, BF),
        ),
        in_specs=hbm(4),
        out_specs=tuple(hbm(3)),
        scratch_shapes=[
            pltpu.VMEM((TILES_HERE, CH, CELLS), BF),
            pltpu.VMEM((TILES_HERE, COARSE, CH), BF),
            pltpu.VMEM((9, CH, C), BF),
            pltpu.VMEM((TILES_HERE * 4 * UNIT, 128), BF),
            pltpu.VMEM((TILES_HERE, PACK_ROWS, 128), BF),
            pltpu.SemaphoreType.DMA((5 + YX,)),
        ],
        compiler_params=WHOLE,
        name="pack",
    )(fields, jnp.swapaxes(cotangent, 1, 2), w_first, w_down)
    weights = lax.all_gather(half, ("chan", "core"), axis=0, tiled=False)
    units = lax.all_to_all(units, ("ylo", "x"), 0, 0).reshape(-1, 128)
    units = lax.all_gather(units, "core", axis=0, tiled=True)
    words, beyond = edge_words(seam_table)
    sends = pl.pallas_call(
        place_kernel,
        out_shape=jax.ShapeDtypeStruct((NZ, SEND_ROWS, 128), BF),
        in_specs=smem(2) + vmem(1),
        out_specs=vmem(1)[0],
        scratch_shapes=[pltpu.VMEM((NZ, SEND_ROWS, 128), F32)],
        compiler_params=LIMIT,
        name="place",
    )(words, beyond, units)
    got = lax.all_to_all(sends, "z", 0, 0)
    joined = pl.pallas_call(
        join_kernel,
        out_shape=jax.ShapeDtypeStruct((CHAN, TILES_HERE * PAY_ROWS, 128), BF),
        in_specs=vmem(2),
        out_specs=vmem(1)[0],
        scratch_shapes=[pltpu.VMEM((TILES_HERE * PAY_ROWS, 128), F32)],
        compiler_params=LIMIT,
        name="join",
    )(got, own)
    payload = lax.all_to_all(joined, "chan", 0, 0)

    tile_at = ((coords[0] * NX + coords[1]) * NZ + coords[2]) * CORE + coords[3]
    own_table = lax.dynamic_slice_in_dim(seam_table, tile_at * TILES_HERE, TILES_HERE, 0)
    code = own_table[:, :, 1] * 2 + own_table[:, :, 2]
    chosen = (code[:, :, None] == jnp.arange(8, dtype=jnp.int32)).astype(BF).reshape(TILES_HERE, 32)
    one_hots = []
    for (fixed, varied), depth in ((window_index(), C), (rim_index(), 2 * C_HALF)):
        at = jnp.dot(chosen, jnp.asarray(varied, BF), preferred_element_type=F32) + jnp.asarray(fixed, F32)
        one_hots.append((at[:, :, None] == jnp.arange(1, depth + 1, dtype=jnp.int32).astype(F32)).astype(BF))

    coarse, grad_pre, kept, given = tiles_call(payload, one_hots[0], one_hots[1], weights)

    part = lax.ppermute(given, "core", [(0, 1), (1, 0)])
    part = (kept.astype(F32) + part.astype(F32)).astype(BF).reshape(YX, 144, 128)
    part = lax.all_to_all(part, ("ylo", "x"), 0, 0)
    part = part.astype(F32).sum(0).astype(BF)
    part = lax.all_to_all(jnp.broadcast_to(part[None], (NZ, 144, 128)), "z", 0, 0)
    part = part.astype(F32).sum(0).astype(BF)
    part = lax.all_to_all(jnp.broadcast_to(part[None], (YX, 144, 128)), ("ylo", "x"), 0, 0)
    whole = lax.all_gather(part.reshape(18 * CH, 128), "core", axis=0, tiled=False)
    whole = jnp.concatenate([whole[0], whole[1]], axis=1).astype(F32).reshape(2, 9, CH, C)
    tiles = TILES_HERE * PLANE * CORE
    return (
        jnp.swapaxes(coarse, 1, 2),
        whole[0] * float(tiles * CELLS) ** (-0.5),
        whole[1] * float(tiles * COARSE) ** (-0.5),
        grad_pre,
    )


def solution(mesh):
    fine = Mesh(mesh.devices.reshape(YLO, NX, NZ, CORE, CHAN), ("ylo", "x", "z", "core", "chan"))
    return jax.shard_map(
        shards,
        mesh=fine,
        in_specs=(
            P(TILE_AXES, "chan", None),
            P(),
            P(None, "chan", None),
            P(None, "chan", None),
            P(TILE_AXES, "chan", None),
        ),
        out_specs=(
            P(TILE_AXES, "chan", None),
            P(None, "chan", None),
            P(None, "chan", None),
            P(TILE_AXES, "chan", None),
        ),
        check_vma=False,
    )
```
